32 devices in a mesh: space: 8 (over z, x), filt: 4 (over y, core).
Axes of the slice: x: 2, y: 2, z: 4, core: 2. Of those that a mesh axis runs over, the one named last changes fastest.
Arguments:
- inputs: bfloat16 [8, 32, 32, 256], P('space'), may hold values from -6 to 6
- out_grad: bfloat16 [8, 256, 1024], P('space', 'filt'), may hold values from -6 to 6
- pre_act: bfloat16 [8, 256, 1024], P('space', 'filt'), may hold values from -8 to 8
- weight: bfloat16 [27, 256, 256], P(None, 'filt'), may hold values from -0.078125 to 0.078125
Outputs:
- grad_input: bfloat16 [8, 32, 32, 256], P('space', 'filt')
- grad_weight: float32 [256, 27, 256], P('space', None, 'filt')
The draws below stay inside these ranges and needn't reach their ends.
All inputs are finite; a program needn't handle non-finite values.
Results may differ from the reference program's by a relative error of at most 0.0049.
Values may be sent and summed in bfloat16 or wider, within the bound.
No kernel may reach another device: no remote copies, remote signals or barrier semaphores. Data moves between devices by JAX's collectives and lax.ppermute only.
A program may use at most 64 MiB of HBM per device.

```python
import jax
import jax.numpy as jnp
from jax import lax

C = 256
F = 256
TAPS = 27
GRID_H = 32
GRID_W = 32
DEPTH = 8


def raised(array, stream_key, source, target, blocks, factor):
    def block_of(dim):
        return (jnp.arange(array.shape[dim]) // (array.shape[dim] // blocks)).reshape((-1,) + (1,) * (array.ndim - 1 - dim))

    near = jax.random.permutation(stream_key, blocks)[block_of(target)]
    second = (block_of(target) + blocks // 2) % blocks
    return jnp.where((block_of(source) == near) | (block_of(source) == second), factor * array, array)


def levels(rng, extent, cuts, smallest, largest):
    factor_of = 1.0
    for position, blocks in cuts:
        draws = jax.random.uniform(jax.random.fold_in(jax.random.fold_in(rng, 6), position), (blocks,), jnp.float32, smallest / len(cuts), largest / len(cuts))
        factor_of = factor_of * jnp.repeat(jnp.exp(draws), extent[position] // blocks).reshape((-1,) + (1,) * (len(extent) - 1 - position))
    return factor_of


def centred(rng, dims, spread, reach, cuts=(), dtype=jnp.bfloat16):
    loudness = levels(rng, dims, cuts, -0.22, 0.18) if cuts else 1.0
    entries = jax.random.normal(rng, dims, jnp.float32) * spread * loudness
    return jnp.minimum(jnp.maximum(entries, -reach), reach).astype(dtype)


def noise_with(rng, shape, width, bound, split, heavy, kind=jnp.bfloat16):
    entries = width * jax.random.normal(rng, shape, jnp.float32)
    if split:
        entries = entries * levels(rng, shape, split, -0.22, 0.18)
    return jnp.clip(raised(entries, jax.random.fold_in(rng, 3), *heavy), -bound, bound).astype(kind)


def setup_inputs(seed: int = 0) -> dict:
    splits = jax.random.split(jax.random.key(seed), 5)
    inputs = noise_with(splits[0], (DEPTH, GRID_H, GRID_W, C), 1.0, 6.0, ((0, 8),), (0, 3, 8, 2.0))
    out_grad = centred(splits[1], (DEPTH, F, GRID_H * GRID_W), 1.0, 6.0, ((0, 8), (1, 4)))
    pre_act = centred(splits[2], (DEPTH, F, GRID_H * GRID_W), 2.0, 8.0, ((0, 8), (1, 4)))
    weight = centred(splits[3], (TAPS, F, C), (TAPS * C) ** -0.5, 0.078125, ((1, 4),))
    return dict(inputs=inputs, out_grad=out_grad, pre_act=pre_act, weight=weight)


def silu_grad(values):
    sig = jax.nn.sigmoid(values)
    return sig * (1.0 + values * (1.0 - sig))

def reference(inputs, out_grad, pre_act, weight):
    n_depth, n_height, n_width, in_chans = inputs.shape
    n_filt = weight.shape[1]
    d_pre = (out_grad.astype(jnp.float32) * silu_grad(pre_act.astype(jnp.float32))).astype(jnp.bfloat16)
    d_grid = d_pre.reshape(n_depth, n_filt, n_height, n_width)
    padded = jnp.pad(d_grid, ((1, 1), (0, 0), (1, 1), (1, 1)))
    cell_count = n_depth * n_height * n_width
    in_flat = inputs.reshape(cell_count, in_chans)
    grad_flat = jnp.zeros((cell_count, in_chans), jnp.float32)
    tap_list = []
    for offset_d in range(3):
        for offset_h in range(3):
            for offset_w in range(3):
                tap_index = 9 * offset_d + 3 * offset_h + offset_w
                window = padded[2 - offset_d:2 - offset_d + n_depth, :, 2 - offset_h:2 - offset_h + n_height, 2 - offset_w:2 - offset_w + n_width]
                shifted = jnp.moveaxis(window, 1, 0).reshape(n_filt, cell_count)
                grad_flat = grad_flat + lax.dot_general(shifted, weight[tap_index], (((0,), (0,)), ((), ())), preferred_element_type=jnp.float32)
                tap_list.append(lax.dot_general(in_flat, shifted, (((0,), (1,)), ((), ())), preferred_element_type=jnp.float32))
    grad_scale = float(cell_count) ** (-0.5)
    grad_weight = jnp.stack(tap_list, axis=1) * grad_scale
    grad_input = grad_flat.reshape(n_depth, n_height, n_width, in_chans).astype(jnp.bfloat16)
    return (grad_input, grad_weight)
```

```python
import functools

import jax
import jax.numpy as jnp
from jax import lax
from jax.experimental import pallas as pl
from jax.experimental.pallas import tpu as pltpu
from jax.sharding import PartitionSpec as P

MIB = 1 << 20
PAIRED = ((0, 0), (2, 0), (0, 1), (2, 1), (0, 2), (2, 2), (1, 0), (1, 2))
VMEM = pl.BlockSpec(memory_space=pltpu.VMEM)
SMEM = pl.BlockSpec(memory_space=pltpu.SMEM)


def silu_grad(values):
    sig = jax.nn.sigmoid(values)
    return sig * (1.0 + values * (1.0 - sig))


def bits_of(count):
    return count.bit_length() - 1


def reversed_bits(value, width):
    return sum(((value >> bit) & 1) << (width - 1 - bit) for bit in range(width))


def call(kernel, outs, scratch=(), flops=0, bytes_accessed=0, limit=24):
    return functools.partial(
        pl.pallas_call,
        kernel,
        out_shape=outs,
        scratch_shapes=scratch,
        compiler_params=pltpu.CompilerParams(vmem_limit_bytes=limit * MIB),
        cost_estimate=pl.CostEstimate(flops=flops, bytes_accessed=bytes_accessed, transcendentals=0),
    )


def windows_kernel(width, blocks, place, own, near, far, inputs, paired, single, keep, send, tall, tall_own, flipped):
    filt, cells = own.shape
    chans = inputs.shape[1]
    rows = chans // blocks
    index = place[0]
    even = lax.rem(index, 2) == 0

    above = jnp.where(even, near[...], far[...])
    below = jnp.where(even, far[...], near[...])
    both = jnp.concatenate([above, below], axis=0).astype(jnp.float32)
    tall[pl.ds(8, cells), :] = both.T
    mine = own[...].astype(jnp.float32)
    tall_own[pl.ds(0, width), :] = jnp.zeros((width, 2 * filt), jnp.float32)
    tall_own[pl.ds(width + cells, width), :] = jnp.zeros((width, 2 * filt), jnp.float32)
    tall_own[pl.ds(width, cells), :] = jnp.concatenate([mine, mine], axis=0).T

    row = lax.broadcasted_iota(jnp.int32, (cells, 2 * filt), 0)
    column = row & (width - 1) if width & (width - 1) == 0 else lax.rem(row, width)
    lane = lax.broadcasted_iota(jnp.int32, (cells, 2 * filt), 1)
    left = lane < filt
    not_last = column != width - 1
    not_first = column != 0

    zero_rows = jnp.zeros((width, paired.shape[1]), jnp.bfloat16)
    paired[pl.ds(0, width), :] = zero_rows
    paired[pl.ds(width + cells, width), :] = zero_rows
    body = pl.ds(width, cells)
    lanes = 2 * filt
    paired[body, 0:lanes] = jnp.where(not_last, tall[pl.ds(9, cells), :], 0.0).astype(jnp.bfloat16)
    paired[body, lanes : 2 * lanes] = tall[pl.ds(8, cells), :].astype(jnp.bfloat16)
    paired[body, 2 * lanes : 3 * lanes] = jnp.where(not_first, tall[pl.ds(7, cells), :], 0.0).astype(jnp.bfloat16)
    after = jnp.where(not_last, tall_own[pl.ds(width + 1, cells), :], 0.0)
    before = jnp.where(not_first, tall_own[pl.ds(width - 1, cells), :], 0.0)
    paired[body, 3 * lanes : 4 * lanes] = jnp.where(left, after, before).astype(jnp.bfloat16)

    up, level, down = (tall_own[pl.ds((2 - b) * width, cells), :] for b in range(3))
    single[:, 0:lanes] = jnp.where(left, up, level).astype(jnp.bfloat16)
    single[:, lanes : lanes + filt] = down[:, 0:filt].astype(jnp.bfloat16)

    order = lax.broadcasted_iota(jnp.int32, (chans, chans), 0)
    count = bits_of(blocks)
    block = index ^ reversed_bits(order >> bits_of(rows), count)
    source = (block << bits_of(rows)) | (order & (rows - 1))
    picked = (lax.broadcasted_iota(jnp.int32, (chans, chans), 1) == source).astype(jnp.bfloat16)
    turned = lax.dot_general(picked, inputs[...], (((1,), (1,)), ((), ())), preferred_element_type=jnp.float32)
    flipped[...] = turned.astype(jnp.bfloat16)

    half = chans // 2
    wide = paired.shape[1]
    for b in range(4):
        window = paired[pl.ds((2 - b) * width, cells), :] if b < 3 else single[...]
        lo = b * wide
        hi = lo + window.shape[1]
        sent = jnp.dot(flipped[pl.ds(half, half), :], window, preferred_element_type=jnp.float32)
        send[:, lo:hi] = sent.astype(jnp.bfloat16)
        kept = jnp.dot(flipped[pl.ds(0, half), :], window, preferred_element_type=jnp.float32)
        keep[:, lo:hi] = kept


def spread_kernel(width, groups, place, paired, single, weight, keep, send, ordered, ordered_single):
    cells = single.shape[0]
    filt = weight.shape[1]
    part = cells // groups
    index = place[1]
    for b in range(3):
        for slot, (a, c) in enumerate(PAIRED):
            ordered[b, pl.ds(slot * filt, filt), :] = weight[9 * a + 3 * b + c]
        ordered_single[pl.ds(b * filt, filt), :] = weight[9 + 3 * b + 1]
    count = bits_of(groups)
    for target in reversed(range(groups)):
        block = 0
        for bit in range(count):
            differs = (target >> (count - 1 - bit)) & 1
            block = block + (((index >> bit) & 1) ^ differs) * (1 << bit)
        start = pl.multiple_of(block * part, part)
        total = jnp.dot(single[pl.ds(start, part), :], ordered_single[...], preferred_element_type=jnp.float32)
        for b in range(3):
            window = paired[pl.ds(pl.multiple_of(start + (2 - b) * width, width), part), :]
            total = total + jnp.dot(window, ordered[b], preferred_element_type=jnp.float32)
        if target < groups // 2:
            keep[pl.ds(target * part, part), :] = total
        else:
            send[pl.ds((target - groups // 2) * part, part), :] = total.astype(jnp.bfloat16)


def halve_kernel(kept, came, keep, send):
    half = keep.shape[0]
    keep[...] = kept[0:half, :] + came[0:half, :].astype(jnp.float32)
    send[...] = (kept[half:, :] + came[half:, :].astype(jnp.float32)).astype(jnp.bfloat16)


def last_input_kernel(kept, came, out):
    out[...] = (kept[...] + came[...].astype(jnp.float32)).astype(out.dtype)


def last_weight_kernel(scale, filt, kept, came, out):
    total = (kept[...] + came[...].astype(jnp.float32)) * scale
    wide = len(PAIRED) * filt
    for b in range(3):
        for slot, (a, c) in enumerate(PAIRED):
            lo = b * wide + slot * filt
            out[:, 9 * a + 3 * b + c, :] = total[:, lo : lo + filt]
        lo = 3 * wide + b * filt
        out[:, 9 + 3 * b + 1, :] = total[:, lo : lo + filt]


def swapped(value, axis, distance):
    count = lax.axis_size(axis)
    return lax.ppermute(value, axis, [(i, i ^ distance) for i in range(count)])


def halved(kept, sent, axis):
    count = lax.axis_size(axis)
    distance = 1
    while True:
        came = swapped(sent, axis, distance)
        distance *= 2
        if distance == count:
            return kept, came
        rows, lanes = kept.shape
        if rows // 2 % 16:
            total = kept + came.astype(jnp.float32)
            kept, sent = total[: rows // 2], total[rows // 2 :].astype(jnp.bfloat16)
            continue
        outs = (
            jax.ShapeDtypeStruct((rows // 2, lanes), jnp.float32),
            jax.ShapeDtypeStruct((rows // 2, lanes), jnp.bfloat16),
        )
        kept, sent = call(halve_kernel, outs, flops=rows * lanes, bytes_accessed=9 * rows * lanes)(
            in_specs=[VMEM] * 2, out_specs=[VMEM] * 2
        )(kept, came)


def on_device(inputs, out_grad, pre_act, weight):
    _, height, width, chans = inputs.shape
    taps, filt, _ = weight.shape
    cells = height * width
    blocks, groups = lax.axis_size("space"), lax.axis_size("filt")
    place = jnp.stack([lax.axis_index("space"), lax.axis_index("filt")]).astype(jnp.int32)

    own = (out_grad.astype(jnp.float32) * silu_grad(pre_act.astype(jnp.float32))).astype(jnp.bfloat16)[0]
    near = swapped(own, "space", 1)
    far_pairs = [(i, i + 1) for i in range(1, blocks - 1, 2)]
    far = lax.ppermute(own, "space", far_pairs + [(target, source) for source, target in far_pairs])

    flat = inputs.reshape(cells, chans)
    wide = len(PAIRED) * filt
    flops = 2 * cells * taps * filt * chans
    paired, single, kept, sent = call(
        functools.partial(windows_kernel, width, blocks),
        (
            jax.ShapeDtypeStruct((cells + 2 * width, wide), jnp.bfloat16),
            jax.ShapeDtypeStruct((cells, 3 * filt), jnp.bfloat16),
            jax.ShapeDtypeStruct((chans // 2, taps * filt), jnp.float32),
            jax.ShapeDtypeStruct((chans // 2, taps * filt), jnp.bfloat16),
        ),
        (
            pltpu.VMEM((cells + 16, 2 * filt), jnp.float32),
            pltpu.VMEM((cells + 2 * width, 2 * filt), jnp.float32),
            pltpu.VMEM((chans, cells), jnp.bfloat16),
        ),
        flops=flops,
        bytes_accessed=4 * MIB,
    )(in_specs=[SMEM] + [VMEM] * 4, out_specs=[VMEM] * 4)(place, own, near, far, flat)

    kept_in, sent_in = call(
        functools.partial(spread_kernel, width, groups),
        (
            jax.ShapeDtypeStruct((cells // 2, chans), jnp.float32),
            jax.ShapeDtypeStruct((cells // 2, chans), jnp.bfloat16),
        ),
        (
            pltpu.VMEM((3, wide, chans), jnp.bfloat16),
            pltpu.VMEM((3 * filt, chans), jnp.bfloat16),
        ),
        flops=flops,
        bytes_accessed=4 * MIB,
    )(in_specs=[SMEM] + [VMEM] * 3, out_specs=[VMEM] * 2)(place, paired, single, weight)

    kept, came = halved(kept, sent, "space")
    kept_in, came_in = halved(kept_in, sent_in, "filt")
    grad_scale = float(cells * blocks) ** (-0.5)
    grad_weight = call(
        functools.partial(last_weight_kernel, grad_scale, filt),
        jax.ShapeDtypeStruct((chans // blocks, taps, filt), jnp.float32),
    )(in_specs=[VMEM] * 2, out_specs=VMEM)(kept, came)
    grad_input = call(
        last_input_kernel, jax.ShapeDtypeStruct((cells // groups, chans), jnp.bfloat16)
    )(in_specs=[VMEM] * 2, out_specs=VMEM)(kept_in, came_in)
    return grad_input.reshape(1, height // groups, width, chans), grad_weight


def solution(mesh):
    placed = (
        P("space", None, None, None),
        P("space", "filt", None),
        P("space", "filt", None),
        P(None, "filt", None),
    )
    return jax.shard_map(
        on_device,
        mesh=mesh,
        in_specs=placed,
        out_specs=(P("space", "filt", None, None), P("space", None, "filt")),
        check_vma=False,
    )
```

```python
import functools

import jax
import jax.numpy as jnp
from jax import lax
from jax.experimental import pallas as pl
from jax.experimental.pallas import tpu as pltpu
from jax.sharding import PartitionSpec as P

MIB = 1 << 20
VMEM = pl.BlockSpec(memory_space=pltpu.VMEM)
SMEM = pl.BlockSpec(memory_space=pltpu.SMEM)


def silu_grad(values):
    sig = jax.nn.sigmoid(values)
    return sig * (1.0 + values * (1.0 - sig))


def bits_of(count):
    return count.bit_length() - 1


def reversed_bits(value, width):
    return sum(((value >> bit) & 1) << (width - 1 - bit) for bit in range(width))


def call(kernel, outs, scratch=(), flops=0, bytes_accessed=0, limit=24):
    return functools.partial(
        pl.pallas_call,
        kernel,
        out_shape=outs,
        scratch_shapes=scratch,
        compiler_params=pltpu.CompilerParams(vmem_limit_bytes=limit * MIB),
        cost_estimate=pl.CostEstimate(flops=flops, bytes_accessed=bytes_accessed, transcendentals=0),
    )


def lay_windows(width, first, second, windows, tall):
    filt, cells = first.shape
    lanes = 2 * filt
    tall[pl.ds(8, cells), :] = jnp.concatenate([first, second], axis=0).astype(jnp.float32).T
    row = lax.broadcasted_iota(jnp.int32, (cells, lanes), 0)
    column = row & (width - 1) if width & (width - 1) == 0 else lax.rem(row, width)
    zero_rows = jnp.zeros((width, windows.shape[1]), jnp.bfloat16)
    windows[pl.ds(0, width), :] = zero_rows
    windows[pl.ds(width + cells, width), :] = zero_rows
    body = pl.ds(width, cells)
    windows[body, 0:lanes] = jnp.where(column != width - 1, tall[pl.ds(9, cells), :], 0.0).astype(jnp.bfloat16)
    windows[body, lanes : 2 * lanes] = tall[pl.ds(8, cells), :].astype(jnp.bfloat16)
    windows[body, 2 * lanes : 3 * lanes] = jnp.where(column != 0, tall[pl.ds(7, cells), :], 0.0).astype(jnp.bfloat16)


def turn_kernel(blocks, place, inputs, mine, sent):
    chans = inputs.shape[1]
    rows = chans // blocks
    half, part = mine.shape[0], sent.shape[0]
    count = bits_of(blocks)
    order = lax.broadcasted_iota(jnp.int32, (half + part, chans), 0)
    order = order + jnp.where(order >= half, (place[1] & 1) * part, 0)
    block = place[0] ^ reversed_bits(order >> bits_of(rows), count)
    source = (block << bits_of(rows)) | (order & (rows - 1))
    picked = (lax.broadcasted_iota(jnp.int32, (half + part, chans), 1) == source).astype(jnp.bfloat16)
    turned = lax.dot_general(picked, inputs[...], (((1,), (1,)), ((), ())), preferred_element_type=jnp.float32)
    turned = turned.astype(jnp.bfloat16)
    mine[...] = turned[0:half, :]
    sent[...] = turned[half:, :]


def near_kernel(width, place, own, near, mine, came, other, windows, turned, outer, middle, tall):
    filt, cells = own.shape
    half = mine.shape[0]
    lanes = 2 * filt
    even = place[0] & 1 == 0
    first_core = place[1] & 1 == 0
    lay_windows(
        width, jnp.where(even, own[...], near[...]), jnp.where(even, near[...], own[...]), windows, tall
    )
    theirs = jnp.concatenate(
        [jnp.where(first_core, came[...], other[...]), jnp.where(first_core, other[...], came[...])], axis=0
    )
    turned[0:half, :] = jnp.where(even, mine[...], theirs)
    turned[half:, :] = jnp.where(even, theirs, mine[...])
    left = lax.broadcasted_iota(jnp.int32, (half, lanes), 1) < filt
    for b in range(3):
        terms = jnp.dot(turned[...], windows[pl.ds((2 - b) * width, cells), :], preferred_element_type=jnp.float32)
        for c in range(3):
            tap = 3 * b + c
            lower = terms[0:half, c * lanes : (c + 1) * lanes]
            upper = terms[half:, c * lanes : (c + 1) * lanes]
            outer[:, tap * lanes : (tap + 1) * lanes] = jnp.where(left, upper, lower)
            lo = tap // 2 * lanes
            if tap % 2 == 0:
                before = lower + pltpu.roll(upper, filt, 1)
                if tap == 8:
                    middle[:, lo : lo + filt] = before[:, 0:filt]
            else:
                middle[:, lo : lo + lanes] = jnp.where(left, before, pltpu.roll(lower, filt, 1) + upper)


def far_kernel(width, place, two_off, one_off, turned, outer, middle, windows, keep, send, tall):
    filt, cells = two_off.shape
    half = turned.shape[0] // 2
    lanes = 2 * filt
    even = place[0] & 1 == 0
    lay_windows(
        width,
        jnp.where(even, one_off[...], two_off[...]),
        jnp.where(even, two_off[...], one_off[...]),
        windows,
        tall,
    )
    left = lax.broadcasted_iota(jnp.int32, (half, lanes), 1) < filt
    kept = half // 2
    for b in range(3):
        terms = jnp.dot(turned[...], windows[pl.ds((2 - b) * width, cells), :], preferred_element_type=jnp.float32)
        for c in range(3):
            lo = (3 * b + c) * lanes
            lower = terms[0:half, c * lanes : (c + 1) * lanes]
            upper = terms[half:, c * lanes : (c + 1) * lanes]
            total = outer[:, lo : lo + lanes] + jnp.where(left, lower, upper)
            keep[:, lo : lo + lanes] = total[0:kept, :]
            send[:, lo : lo + lanes] = total[kept:, :].astype(jnp.bfloat16)
    keep[:, 9 * lanes :] = middle[0:kept, :]
    send[:, 9 * lanes :] = middle[kept:, :].astype(jnp.bfloat16)


def spread_kernel(width, groups, place, pair, ends, weight, keep, send, ordered):
    cells = pair.shape[0] - 2 * width
    filt = weight.shape[1]
    part = cells // groups
    index = place[1]
    odd = place[0] & 1
    even = odd == 0
    for b in range(3):
        for c in range(3):
            tap = 3 * b + c
            zero = jnp.zeros_like(weight[0])
            rows = (
                weight[9 * (1 + odd) + tap],
                weight[9 * odd + tap],
                jnp.where(even, weight[18 + tap], zero),
                jnp.where(even, zero, weight[tap]),
            )
            for slot, value in zip((2 * c, 2 * c + 1, 2 * c + 6, 2 * c + 7), rows):
                ordered[b, pl.ds(slot * filt, filt), :] = value
    count = bits_of(groups)
    for target in reversed(range(groups)):
        block = 0
        for bit in range(count):
            differs = (target >> (count - 1 - bit)) & 1
            block = block + (((index >> bit) & 1) ^ differs) * (1 << bit)
        total = 0.0
        for b in range(3):
            rows = pl.ds(pl.multiple_of(block * part + (2 - b) * width, width), part)
            window = jnp.concatenate([pair[rows, :], ends[rows, :]], axis=1)
            total = total + jnp.dot(window, ordered[b], preferred_element_type=jnp.float32)
        if target < groups // 2:
            keep[pl.ds(target * part, part), :] = total
        else:
            send[pl.ds((target - groups // 2) * part, part), :] = total.astype(jnp.bfloat16)


def halve_kernel(kept, came, keep, send):
    half = keep.shape[0]
    keep[...] = kept[0:half, :] + came[0:half, :].astype(jnp.float32)
    send[...] = (kept[half:, :] + came[half:, :].astype(jnp.float32)).astype(jnp.bfloat16)


def last_input_kernel(kept, came, out):
    out[...] = (kept[...] + came[...].astype(jnp.float32)).astype(out.dtype)


def last_weight_kernel(scale, filt, kept, came, out):
    total = (kept[...] + came[...].astype(jnp.float32)) * scale
    for tap in range(9):
        for slot, place in ((2 * tap, 18 + tap), (2 * tap + 1, tap), (18 + tap, 9 + tap)):
            out[place] = total[:, slot * filt : (slot + 1) * filt]


def swapped(value, axis, distance):
    count = lax.axis_size(axis)
    return lax.ppermute(value, axis, [(i, i ^ distance) for i in range(count)])


def halved(kept, came):
    rows, lanes = kept.shape
    if rows // 2 % 16:
        total = kept + came.astype(jnp.float32)
        return total[: rows // 2], total[rows // 2 :].astype(jnp.bfloat16)
    outs = (
        jax.ShapeDtypeStruct((rows // 2, lanes), jnp.float32),
        jax.ShapeDtypeStruct((rows // 2, lanes), jnp.bfloat16),
    )
    return call(halve_kernel, outs, flops=rows * lanes, bytes_accessed=9 * rows * lanes)(
        in_specs=[VMEM] * 2, out_specs=[VMEM] * 2
    )(kept, came)


def after(value, other):
    return lax.optimization_barrier((value, other))[0]


def on_device(inputs, out_grad, pre_act, weight):
    _, height, width, chans = inputs.shape
    taps, filt, _ = weight.shape
    cells = height * width
    blocks, groups = lax.axis_size("space"), lax.axis_size("filt")
    half, quarter = chans // 2, chans // 4
    place = jnp.stack([lax.axis_index("space"), lax.axis_index("filt")]).astype(jnp.int32)
    bf16, f32 = jnp.bfloat16, jnp.float32
    shape = jax.ShapeDtypeStruct
    flops = 2 * cells * taps * filt * chans
    lanes = 6 * filt
    windows_shape = shape((cells + 2 * width, lanes), bf16)
    tall = pltpu.VMEM((cells + 16, 2 * filt), f32)

    own = (out_grad.astype(f32) * silu_grad(pre_act.astype(f32))).astype(bf16)[0]
    near = swapped(own, "space", 1)
    two_pairs = [(i, i - 2) for i in range(2, blocks, 2)] + [(i, i + 2) for i in range(1, blocks - 2, 2)]
    two_off = lax.ppermute(own, "space", two_pairs)
    mine, sent = call(
        functools.partial(turn_kernel, blocks),
        (shape((half, cells), bf16), shape((quarter, cells), bf16)),
        bytes_accessed=MIB,
    )(in_specs=[SMEM, VMEM], out_specs=[VMEM] * 2)(place, after(inputs.reshape(cells, chans), own))
    came = swapped(sent, "space", 1)
    one_off = swapped(two_off, "space", 1)
    other = swapped(came, "filt", 1)

    pair, turned, outer, middle = call(
        functools.partial(near_kernel, width),
        (
            windows_shape,
            shape((chans, cells), bf16),
            shape((half, 18 * filt), f32),
            shape((half, 9 * filt), f32),
        ),
        (tall,),
        flops=flops,
        bytes_accessed=4 * MIB,
    )(in_specs=[SMEM] + [VMEM] * 5, out_specs=[VMEM] * 4)(place, own, near, mine, came, other)

    ends, kept, sent = call(
        functools.partial(far_kernel, width),
        (windows_shape, shape((quarter, taps * filt), f32), shape((quarter, taps * filt), bf16)),
        (tall,),
        flops=flops,
        bytes_accessed=4 * MIB,
    )(in_specs=[SMEM] + [VMEM] * 5, out_specs=[VMEM] * 3)(place, two_off, one_off, turned, outer, middle)
    came = swapped(sent, "space", 2)

    kept_in, sent_in = call(
        functools.partial(spread_kernel, width, groups),
        (shape((cells // 2, chans), f32), shape((cells // 2, chans), bf16)),
        (pltpu.VMEM((3, 2 * lanes, chans), bf16),),
        flops=flops,
        bytes_accessed=4 * MIB,
    )(in_specs=[SMEM] + [VMEM] * 3, out_specs=[VMEM] * 2)(place, pair, ends, weight)
    came_in = swapped(sent_in, "filt", 1)

    distance, distance_in = 4, 2
    while distance < blocks or distance_in < groups:
        if distance < blocks:
            kept, sent = halved(kept, came)
            came = swapped(sent, "space", distance)
            distance *= 2
        if distance_in < groups:
            kept_in, sent_in = halved(kept_in, after(came_in, sent))
            came_in = swapped(sent_in, "filt", distance_in)
            distance_in *= 2

    grad_scale = float(cells * blocks) ** (-0.5)
    grad_weight = call(
        functools.partial(last_weight_kernel, grad_scale, filt), shape((taps, chans // blocks, filt), f32)
    )(in_specs=[VMEM] * 2, out_specs=VMEM)(kept, came)
    grad_input = call(last_input_kernel, shape((cells // groups, chans), bf16))(
        in_specs=[VMEM] * 2, out_specs=VMEM
    )(kept_in, came_in)
    return grad_input.reshape(1, height // groups, width, chans), jnp.transpose(grad_weight, (1, 0, 2))


def solution(mesh):
    placed = (
        P("space", None, None, None),
        P("space", "filt", None),
        P("space", "filt", None),
        P(None, "filt", None),
    )
    return jax.shard_map(
        on_device,
        mesh=mesh,
        in_specs=placed,
        out_specs=(P("space", "filt", None, None), P("space", None, "filt")),
        check_vma=False,
    )
```

```python
import functools

import jax
import jax.numpy as jnp
from jax import lax
from jax.experimental import pallas as pl
from jax.experimental.pallas import tpu as pltpu
from jax.sharding import PartitionSpec as P

MIB = 1 << 20
VMEM = pl.BlockSpec(memory_space=pltpu.VMEM)
SMEM = pl.BlockSpec(memory_space=pltpu.SMEM)


def silu_grad(values):
    sig = jax.nn.sigmoid(values)
    return sig * (1.0 + values * (1.0 - sig))


def bits_of(count):
    return count.bit_length() - 1


def reversed_bits(value, width):
    return sum(((value >> bit) & 1) << (width - 1 - bit) for bit in range(width))


def call(kernel, outs, scratch=(), flops=0, bytes_accessed=0, limit=24):
    return functools.partial(
        pl.pallas_call,
        kernel,
        out_shape=outs,
        scratch_shapes=scratch,
        compiler_params=pltpu.CompilerParams(vmem_limit_bytes=limit * MIB),
        cost_estimate=pl.CostEstimate(flops=flops, bytes_accessed=bytes_accessed, transcendentals=0),
    )


def lay_windows(width, first, second, windows, tall):
    filt, cells = first.shape
    lanes = 2 * filt
    tall[pl.ds(8, cells), :] = jnp.concatenate([first, second], axis=0).astype(jnp.float32).T
    row = lax.broadcasted_iota(jnp.int32, (cells, lanes), 0)
    column = row & (width - 1) if width & (width - 1) == 0 else lax.rem(row, width)
    zero_rows = jnp.zeros((width, windows.shape[1]), jnp.bfloat16)
    windows[pl.ds(0, width), :] = zero_rows
    windows[pl.ds(width + cells, width), :] = zero_rows
    body = pl.ds(width, cells)
    windows[body, 0:lanes] = jnp.where(column != width - 1, tall[pl.ds(9, cells), :], 0.0).astype(jnp.bfloat16)
    windows[body, lanes : 2 * lanes] = tall[pl.ds(8, cells), :].astype(jnp.bfloat16)
    windows[body, 2 * lanes : 3 * lanes] = jnp.where(column != 0, tall[pl.ds(7, cells), :], 0.0).astype(jnp.bfloat16)


def turn_kernel(blocks, place, inputs, mine, sent):
    chans = inputs.shape[1]
    rows = chans // blocks
    half, part = mine.shape[0], sent.shape[0]
    count = bits_of(blocks)
    order = lax.broadcasted_iota(jnp.int32, (half + part, chans), 0)
    order = order + jnp.where(order >= half, (place[1] & 1) * part, 0)
    block = place[0] ^ reversed_bits(order >> bits_of(rows), count)
    source = (block << bits_of(rows)) | (order & (rows - 1))
    picked = (lax.broadcasted_iota(jnp.int32, (half + part, chans), 1) == source).astype(jnp.bfloat16)
    turned = lax.dot_general(picked, inputs[...], (((1,), (1,)), ((), ())), preferred_element_type=jnp.float32)
    turned = turned.astype(jnp.bfloat16)
    mine[...] = turned[0:half, :]
    sent[...] = turned[half:, :]


def order_kernel(place, weight, ordered):
    filt = weight.shape[1]
    odd = place[0] & 1
    zero = jnp.zeros(weight.shape[1:], jnp.bfloat16)
    for tap in range(9):
        b, c = divmod(tap, 3)
        rows = (weight[9 + tap], weight[18 * odd + tap], weight[18 - 18 * odd + tap], zero)
        for slot, value in zip((2 * c, 2 * c + 1, 2 * c + 6, 2 * c + 7), rows):
            ordered[b, pl.ds(slot * filt, filt), :] = value


def spread_kernel(width, groups, place, own, near, one_off, ordered, pair, ones, keep, send, tall):
    filt, cells = own.shape
    part = cells // groups
    index = place[1]
    lay_windows(width, own[...], near[...], pair, tall)
    lay_windows(width, one_off[...], one_off[...], ones, tall)
    count = bits_of(groups)
    for target in reversed(range(groups)):
        block = 0
        for bit in range(count):
            differs = (target >> (count - 1 - bit)) & 1
            block = block + (((index >> bit) & 1) ^ differs) * (1 << bit)
        total = 0.0
        for b in range(3):
            rows = pl.ds(pl.multiple_of(block * part + (2 - b) * width, width), part)
            window = jnp.concatenate([pair[rows, :], ones[rows, :]], axis=1)
            total = total + jnp.dot(window, ordered[b], preferred_element_type=jnp.float32)
        if target < groups // 2:
            keep[pl.ds(target * part, part), :] = total
        else:
            send[pl.ds((target - groups // 2) * part, part), :] = total.astype(jnp.bfloat16)


def mine_kernel(width, place, mine, pair, ones, two_off, twos, first, second, tall):
    filt, cells = two_off.shape
    lanes = 2 * filt
    wide = pair.shape[1]
    lay_windows(width, two_off[...], two_off[...], twos, tall)
    for b in range(3):
        rows = pl.ds((2 - b) * width, cells)
        first[:, b * wide : (b + 1) * wide] = jnp.dot(mine[...], pair[rows, :], preferred_element_type=jnp.float32)
        second[:, b * wide : (b + 1) * wide] = jnp.dot(mine[...], ones[rows, :], preferred_element_type=jnp.float32)


def theirs_kernel(width, filt, place, came, other, pair, twos, first, second, keep, *sends):
    half = first.shape[0]
    lanes = 2 * filt
    wide = pair.shape[1]
    cells = came.shape[1]
    first_core = place[1] & 1 == 0
    theirs = jnp.concatenate(
        [jnp.where(first_core, came[...], other[...]), jnp.where(first_core, other[...], came[...])], axis=0
    )
    left = lax.broadcasted_iota(jnp.int32, (half, lanes), 1) < filt
    part = half // (len(sends) + 1)

    def store(lo, hi, value):
        keep[:, lo:hi] = value[0:part, :]
        for number, send in enumerate(sends, 1):
            send[:, lo:hi] = value[number * part : (number + 1) * part, :].astype(jnp.bfloat16)

    for b in range(3):
        rows = pl.ds((2 - b) * width, cells)
        near_terms = jnp.dot(theirs, pair[rows, :], preferred_element_type=jnp.float32)
        far_terms = jnp.dot(theirs, twos[rows, :], preferred_element_type=jnp.float32)
        for c in range(3):
            tap = 3 * b + c
            cut = slice(c * lanes, (c + 1) * lanes)
            lo = b * wide + c * lanes
            crossed = jnp.where(left, pltpu.roll(near_terms[:, cut], filt, 1), far_terms[:, cut])
            store(lo, lo + lanes, first[:, lo : lo + lanes] + crossed)
            outer = second[:, lo : lo + lanes] + near_terms[:, cut]
            lo = 3 * wide + tap // 2 * lanes
            if tap == 8:
                store(lo, lo + filt, outer[:, 0:filt])
            elif tap % 2 == 0:
                before = outer
            else:
                store(lo, lo + lanes, jnp.where(left, before, pltpu.roll(outer, filt, 1)))


def halve_kernel(kept, came, keep, send):
    half = keep.shape[0]
    keep[...] = kept[0:half, :] + came[0:half, :].astype(jnp.float32)
    send[...] = (kept[half:, :] + came[half:, :].astype(jnp.float32)).astype(jnp.bfloat16)


def last_input_kernel(kept, came, out):
    out[...] = (kept[...] + came[...].astype(jnp.float32)).astype(out.dtype)


def last_weight_kernel(scale, filt, place, kept, *rest):
    *came, out = rest
    odd = place[0] & 1
    total = kept[...]
    for piece in came:
        total = total + piece[...].astype(jnp.float32)
    total = total * scale
    for tap in range(9):
        slots = ((2 * tap, 9 + tap), (2 * tap + 1, 18 * odd + tap), (18 + tap, 18 - 18 * odd + tap))
        for slot, target in slots:
            out[target] = total[:, slot * filt : (slot + 1) * filt]


def swapped(value, axis, distance):
    count = lax.axis_size(axis)
    return lax.ppermute(value, axis, [(i, i ^ distance) for i in range(count)])


def halved(kept, came):
    rows, lanes = kept.shape
    if rows // 2 % 16:
        total = kept + came.astype(jnp.float32)
        return total[: rows // 2], total[rows // 2 :].astype(jnp.bfloat16)
    outs = (
        jax.ShapeDtypeStruct((rows // 2, lanes), jnp.float32),
        jax.ShapeDtypeStruct((rows // 2, lanes), jnp.bfloat16),
    )
    return call(halve_kernel, outs, flops=rows * lanes, bytes_accessed=9 * rows * lanes)(
        in_specs=[VMEM] * 2, out_specs=[VMEM] * 2
    )(kept, came)


def after(value, other):
    return lax.optimization_barrier((value, other))[0]


def on_device(inputs, out_grad, pre_act, weight):
    _, height, width, chans = inputs.shape
    taps, filt, _ = weight.shape
    cells = height * width
    blocks, groups = lax.axis_size("space"), lax.axis_size("filt")
    half, quarter = chans // 2, chans // 4
    place = jnp.stack([lax.axis_index("space"), lax.axis_index("filt")]).astype(jnp.int32)
    bf16, f32 = jnp.bfloat16, jnp.float32
    shape = jax.ShapeDtypeStruct
    flops = 2 * cells * taps * filt * chans
    lanes = 6 * filt
    windows_shape = shape((cells + 2 * width, lanes), bf16)
    tall = pltpu.VMEM((cells + 16, 2 * filt), f32)

    own = (out_grad.astype(f32) * silu_grad(pre_act.astype(f32))).astype(bf16)[0]
    one_pairs = [(i, i + 1) for i in range(1, blocks - 1, 2)]
    one_off = lax.ppermute(own, "space", one_pairs + [(target, source) for source, target in one_pairs])
    near = swapped(own, "space", 1)
    mine, sent = call(
        functools.partial(turn_kernel, blocks),
        (shape((half, cells), bf16), shape((quarter, cells), bf16)),
        bytes_accessed=MIB,
    )(in_specs=[SMEM, VMEM], out_specs=[VMEM] * 2)(after(place, own), inputs.reshape(cells, chans))
    came = swapped(sent, "space", 1)
    two_pairs = [(i, i - 2) for i in range(2, blocks, 2)] + [(i, i + 2) for i in range(1, blocks - 2, 2)]
    two_off = lax.ppermute(own, "space", two_pairs)

    ordered = call(order_kernel, shape((3, 2 * lanes, chans), bf16), bytes_accessed=MIB)(
        in_specs=[SMEM, VMEM], out_specs=VMEM
    )(after(place, mine), weight)
    pair, ones, kept_in, sent_in = call(
        functools.partial(spread_kernel, width, groups),
        (windows_shape, windows_shape, shape((cells // 2, chans), f32), shape((cells // 2, chans), bf16)),
        (tall,),
        flops=flops,
        bytes_accessed=4 * MIB,
    )(in_specs=[SMEM] + [VMEM] * 4, out_specs=[VMEM] * 4)(place, own, near, one_off, ordered)
    other = swapped(after(came, sent_in), "filt", 1)
    came_in = swapped(sent_in, "filt", 1)

    twos, first, second = call(
        functools.partial(mine_kernel, width),
        (windows_shape, shape((half, 3 * lanes), f32), shape((half, 3 * lanes), f32)),
        (tall,),
        flops=flops,
        bytes_accessed=4 * MIB,
    )(in_specs=[SMEM] + [VMEM] * 4, out_specs=[VMEM] * 3)(place, mine, pair, ones, two_off)

    radix = min(4, blocks // 2)
    piece = half // radix
    kept, *sends = call(
        functools.partial(theirs_kernel, width, filt),
        (shape((piece, taps * filt), f32),) + (shape((piece, taps * filt), bf16),) * (radix - 1),
        flops=flops,
        bytes_accessed=4 * MIB,
    )(in_specs=[SMEM] + [VMEM] * 6, out_specs=[VMEM] * radix)(place, came, other, pair, twos, first, second)

    came_in = after(came_in, kept)
    distance = 2
    while True:
        spans = {2: (1,), 4: (2, 1, 3)}[radix]
        arrived = [swapped(sends[n - 1], "space", spans[n - 1] * distance) for n in range(1, radix)]
        distance *= radix
        if distance >= blocks:
            break
        total = kept
        for part in arrived:
            total = total + part.astype(f32)
        radix = min(4, blocks // distance)
        piece //= radix
        kept, *sends = (total[n * piece : (n + 1) * piece] for n in range(radix))
        sends = [value.astype(bf16) for value in sends]

    distance_in = 2
    while distance_in < groups:
        kept_in, sent_in = halved(kept_in, came_in)
        came_in = swapped(sent_in, "filt", distance_in)
        distance_in *= 2
    grad_input = call(last_input_kernel, shape((cells // groups, chans), bf16))(
        in_specs=[VMEM] * 2, out_specs=VMEM
    )(kept_in, came_in)
    grad_scale = float(cells * blocks) ** (-0.5)
    grad_weight = call(
        functools.partial(last_weight_kernel, grad_scale, filt), shape((taps, chans // blocks, filt), f32)
    )(in_specs=[SMEM] + [VMEM] * (len(arrived) + 1), out_specs=VMEM)(after(place, grad_input), kept, *arrived)
    return grad_input.reshape(1, height // groups, width, chans), jnp.transpose(grad_weight, (1, 0, 2))


def solution(mesh):
    placed = (
        P("space", None, None, None),
        P("space", "filt", None),
        P("space", "filt", None),
        P(None, "filt", None),
    )
    return jax.shard_map(
        on_device,
        mesh=mesh,
        in_specs=placed,
        out_specs=(P("space", "filt", None, None), P("space", None, "filt")),
        check_vma=False,
    )
```

```python
import functools

import jax
import jax.numpy as jnp
from jax import lax
from jax.experimental import pallas as pl
from jax.experimental.pallas import tpu as pltpu
from jax.sharding import PartitionSpec as P

MIB = 1 << 20
FIRST = 60
VMEM = pl.BlockSpec(memory_space=pltpu.VMEM)


def silu_grad(values):
    sig = jax.nn.sigmoid(values)
    return sig * (1.0 + values * (1.0 - sig))


def bits_of(count):
    return count.bit_length() - 1


def reversed_bits(value, width):
    return sum(((value >> bit) & 1) << (width - 1 - bit) for bit in range(width))


def call(kernel, outs, scratch=(), flops=0, bytes_accessed=0, limit=24):
    return functools.partial(
        pl.pallas_call,
        kernel,
        out_shape=outs,
        scratch_shapes=scratch,
        compiler_params=pltpu.CompilerParams(vmem_limit_bytes=limit * MIB),
        cost_estimate=pl.CostEstimate(flops=flops, bytes_accessed=bytes_accessed, transcendentals=0),
    )


def lay_windows(width, first, second, windows, tall):
    filt, cells = first.shape
    lanes = 2 * filt
    tall[pl.ds(8, cells), :] = jnp.concatenate([first, second], axis=0).astype(jnp.float32).T
    row = lax.broadcasted_iota(jnp.int32, (cells, lanes), 0)
    column = row & (width - 1) if width & (width - 1) == 0 else lax.rem(row, width)
    zero_rows = jnp.zeros((width, windows.shape[1]), jnp.bfloat16)
    windows[pl.ds(0, width), :] = zero_rows
    windows[pl.ds(width + cells, width), :] = zero_rows
    body = pl.ds(width, cells)
    windows[body, 0:lanes] = jnp.where(column != width - 1, tall[pl.ds(9, cells), :], 0.0).astype(jnp.bfloat16)
    windows[body, lanes : 2 * lanes] = tall[pl.ds(8, cells), :].astype(jnp.bfloat16)
    windows[body, 2 * lanes : 3 * lanes] = jnp.where(column != 0, tall[pl.ds(7, cells), :], 0.0).astype(jnp.bfloat16)


def first_kernel(blocks, out_grad, pre_act, inputs, mine, sent, grads, acts, cells_in, loaded):
    cells, chans = inputs.shape
    rows = chans // blocks
    filt = out_grad.shape[0]
    half, part = mine.shape[0], sent.shape[0] - filt
    step = cells // 4
    copies = [pltpu.make_async_copy(out_grad, grads, loaded.at[0]), pltpu.make_async_copy(pre_act, acts, loaded.at[1])]
    for number in range(4):
        rung = pl.ds(number * step, step)
        copies.append(pltpu.make_async_copy(inputs.at[rung, :], cells_in.at[rung, :], loaded.at[2 + number]))
    for copy in copies:
        copy.start()
    count = bits_of(blocks)
    order = lax.broadcasted_iota(jnp.int32, (half + part, chans), 0)
    order = order + jnp.where(order >= half, (lax.axis_index("filt") & 1) * part, 0)
    block = lax.axis_index("space") ^ reversed_bits(order >> bits_of(rows), count)
    source = (block << bits_of(rows)) | (order & (rows - 1))
    picked = (lax.broadcasted_iota(jnp.int32, (half + part, chans), 1) == source).astype(jnp.bfloat16)
    copies[0].wait()
    copies[1].wait()
    d_pre = grads[...].astype(jnp.float32) * silu_grad(acts[...].astype(jnp.float32))
    sent[0:filt, :] = d_pre.astype(sent.dtype)
    for number in range(4):
        copies[2 + number].wait()
        rung = pl.ds(number * step, step)
        turned = lax.dot_general(
            picked, cells_in[rung, :], (((1,), (1,)), ((), ())), preferred_element_type=jnp.float32
        ).astype(jnp.bfloat16)
        mine[:, rung] = turned[0:half, :]
        sent[filt:, rung] = turned[half:, :]


def order_kernel(weight, ordered):
    filt = weight.shape[1]
    odd = lax.axis_index("space") & 1
    zero = jnp.zeros(weight.shape[1:], jnp.bfloat16)
    for tap in range(9):
        b, c = divmod(tap, 3)
        rows = (weight[9 + tap], weight[18 * odd + tap], weight[18 - 18 * odd + tap], zero)
        for slot, value in zip((2 * c, 2 * c + 1, 2 * c + 6, 2 * c + 7), rows):
            ordered[b, pl.ds(slot * filt, filt), :] = value


def near_kernel(width, sent, came, mine, two_off, ordered, pair, twos, first, spread, tall):
    filt, cells = two_off.shape
    wide = pair.shape[1]
    lay_windows(width, two_off[...], two_off[...], twos, tall)
    lay_windows(width, sent[0:filt, :], came[0:filt, :], pair, tall)
    total = 0.0
    for b in range(3):
        rows = pl.ds((2 - b) * width, cells)
        first[:, b * wide : (b + 1) * wide] = jnp.dot(mine[...], pair[rows, :], preferred_element_type=jnp.float32)
        total = total + jnp.dot(pair[rows, :], ordered[b, 0:wide, :], preferred_element_type=jnp.float32)
    spread[...] = total


def one_kernel(width, one_off, mine, ones, second, tall):
    cells = mine.shape[1]
    wide = ones.shape[1]
    lay_windows(width, one_off[...], one_off[...], ones, tall)
    for b in range(3):
        rows = pl.ds((2 - b) * width, cells)
        second[:, b * wide : (b + 1) * wide] = jnp.dot(mine[...], ones[rows, :], preferred_element_type=jnp.float32)


def theirs_kernel(width, came, other, pair, twos, first, second, keep, *sends):
    half = first.shape[0]
    cells = came.shape[1]
    wide = pair.shape[1]
    lanes = wide // 3
    filt = lanes // 2
    first_core = lax.axis_index("filt") & 1 == 0
    here = came[filt:, :]
    theirs = jnp.concatenate(
        [jnp.where(first_core, here, other[...]), jnp.where(first_core, other[...], here)], axis=0
    )
    left = lax.broadcasted_iota(jnp.int32, (half, lanes), 1) < filt
    part = half // (len(sends) + 1)

    def store(lo, hi, value):
        keep[:, lo:hi] = value[0:part, :]
        for number, send in enumerate(sends, 1):
            send[:, lo:hi] = value[number * part : (number + 1) * part, :].astype(jnp.bfloat16)

    for b in range(3):
        rows = pl.ds((2 - b) * width, cells)
        near_terms = jnp.dot(theirs, pair[rows, :], preferred_element_type=jnp.float32)
        far_terms = jnp.dot(theirs, twos[rows, :], preferred_element_type=jnp.float32)
        for c in range(3):
            tap = 3 * b + c
            cut = slice(c * lanes, (c + 1) * lanes)
            lo = b * wide + c * lanes
            crossed = jnp.where(left, pltpu.roll(near_terms[:, cut], filt, 1), far_terms[:, cut])
            store(lo, lo + lanes, first[:, lo : lo + lanes] + crossed)
            outer = second[:, lo : lo + lanes] + near_terms[:, cut]
            lo = 3 * wide + tap // 2 * lanes
            if tap == 8:
                store(lo, lo + filt, outer[:, 0:filt])
            elif tap % 2 == 0:
                before = outer
            else:
                store(lo, lo + lanes, jnp.where(left, before, pltpu.roll(outer, filt, 1)))


def spread_kernel(width, ones, ordered, spread, send):
    cells = spread.shape[0]
    wide = ones.shape[1]
    total = spread[...]
    for b in range(3):
        window = ones[pl.ds((2 - b) * width, cells), :]
        total = total + jnp.dot(window, ordered[b, wide:, :], preferred_element_type=jnp.float32)
    send[...] = total.astype(jnp.bfloat16).reshape(send.shape)


def last_input_kernel(came, out):
    total = came[0].astype(jnp.float32)
    for number in range(1, came.shape[0]):
        total = total + came[number].astype(jnp.float32)
    out[...] = total.astype(out.dtype)


def last_weight_kernel(scale, filt, kept, *rest):
    *came, out = rest
    odd = lax.axis_index("space") & 1
    total = kept[...]
    for piece in came:
        total = total + piece[...].astype(jnp.float32)
    total = total * scale
    for tap in range(9):
        slots = ((2 * tap, 9 + tap), (2 * tap + 1, 18 * odd + tap), (18 + tap, 18 - 18 * odd + tap))
        for slot, target in slots:
            out[target] = total[:, slot * filt : (slot + 1) * filt]


def swapped(value, axis, distance):
    count = lax.axis_size(axis)
    return lax.ppermute(value, axis, [(i, i ^ distance) for i in range(count)])


def after(value, other):
    return lax.optimization_barrier((value, other))[0]


def on_device(inputs, out_grad, pre_act, weight):
    _, height, width, chans = inputs.shape
    taps, filt, _ = weight.shape
    cells = height * width
    blocks, groups = lax.axis_size("space"), lax.axis_size("filt")
    half, quarter = chans // 2, chans // 4
    bf16, f32 = jnp.bfloat16, jnp.float32
    shape = jax.ShapeDtypeStruct
    flops = 2 * cells * taps * filt * chans
    lanes = 6 * filt
    windows_shape = shape((cells + 2 * width, lanes), bf16)
    tall = pltpu.VMEM((cells + 16, 2 * filt), f32)

    mine, sent = call(
        functools.partial(first_kernel, blocks),
        (shape((half, cells), bf16), shape((filt + quarter, cells), bf16)),
        (
            pltpu.VMEM((filt, cells), bf16),
            pltpu.VMEM((filt, cells), bf16),
            pltpu.VMEM((cells, chans), bf16),
            pltpu.SemaphoreType.DMA((6,)),
        ),
        bytes_accessed=MIB,
        limit=FIRST,
    )(in_specs=[pl.BlockSpec(memory_space=pl.ANY)] * 3, out_specs=[VMEM] * 2)(
        out_grad[0], pre_act[0], inputs.reshape(cells, chans)
    )
    came = swapped(sent, "space", 1)
    own = sent[0:filt]
    two_pairs = [(i, i - 2) for i in range(2, blocks, 2)] + [(i, i + 2) for i in range(1, blocks - 2, 2)]
    two_off = lax.ppermute(own, "space", two_pairs)
    one_pairs = [(i, i + 1) for i in range(1, blocks - 1, 2)]
    one_off = lax.ppermute(own, "space", one_pairs + [(target, source) for source, target in one_pairs])
    other = swapped(came[filt:], "filt", 1)

    ordered = call(order_kernel, shape((3, 2 * lanes, chans), bf16), bytes_accessed=MIB)(
        in_specs=[VMEM], out_specs=VMEM
    )(after(weight, mine))
    pair, twos, first, spread = call(
        functools.partial(near_kernel, width),
        (windows_shape, windows_shape, shape((half, 3 * lanes), f32), shape((cells, chans), f32)),
        (tall,),
        flops=flops,
        bytes_accessed=4 * MIB,
    )(in_specs=[VMEM] * 5, out_specs=[VMEM] * 4)(sent, came, mine, two_off, ordered)
    ones, second = call(
        functools.partial(one_kernel, width),
        (windows_shape, shape((half, 3 * lanes), f32)),
        (tall,),
        flops=flops // 2,
        bytes_accessed=2 * MIB,
    )(in_specs=[VMEM] * 2, out_specs=[VMEM] * 2)(one_off, after(mine, first))
    radix = min(4, blocks // 2)
    piece = half // radix
    kept, *sends = call(
        functools.partial(theirs_kernel, width),
        (shape((piece, taps * filt), f32),) + (shape((piece, taps * filt), bf16),) * (radix - 1),
        flops=flops,
        bytes_accessed=4 * MIB,
    )(in_specs=[VMEM] * 6, out_specs=[VMEM] * radix)(came, other, pair, twos, first, second)
    sent_in = call(
        functools.partial(spread_kernel, width),
        shape((groups, cells // groups, chans), bf16),
        flops=flops // 3,
        bytes_accessed=4 * MIB,
    )(in_specs=[VMEM] * 3, out_specs=VMEM)(ones, ordered, spread)
    came_in = lax.all_to_all(sent_in, "filt", 0, 0, tiled=True)

    distance = 2
    while True:
        spans = {2: (1,), 4: (2, 1, 3)}[radix]
        arrived = [swapped(sends[n - 1], "space", spans[n - 1] * distance) for n in range(1, radix)]
        distance *= radix
        if distance >= blocks:
            break
        total = kept
        for part in arrived:
            total = total + part.astype(f32)
        radix = min(4, blocks // distance)
        piece //= radix
        kept, *sends = (total[n * piece : (n + 1) * piece] for n in range(radix))
        sends = [value.astype(bf16) for value in sends]

    grad_scale = float(cells * blocks) ** (-0.5)
    grad_weight = call(
        functools.partial(last_weight_kernel, grad_scale, filt), shape((taps, chans // blocks, filt), f32)
    )(in_specs=[VMEM] * (len(arrived) + 1), out_specs=VMEM)(kept, *arrived)
    grad_input = call(last_input_kernel, shape((cells // groups, chans), bf16))(in_specs=[VMEM], out_specs=VMEM)(came_in)
    return grad_input.reshape(1, height // groups, width, chans), jnp.transpose(grad_weight, (1, 0, 2))


def solution(mesh):
    placed = (
        P("space", None, None, None),
        P("space", "filt", None),
        P("space", "filt", None),
        P(None, "filt", None),
    )
    return jax.shard_map(
        on_device,
        mesh=mesh,
        in_specs=placed,
        out_specs=(P("space", "filt", None, None), P("space", None, "filt")),
        check_vma=False,
    )
```

```python
import functools

import jax
import jax.numpy as jnp
from jax import lax
from jax.experimental import pallas as pl
from jax.experimental.pallas import tpu as pltpu
from jax.sharding import PartitionSpec as P

MIB = 1 << 20
VMEM = pl.BlockSpec(memory_space=pltpu.VMEM)


def silu_grad(values):
    sig = jax.nn.sigmoid(values)
    return sig * (1.0 + values * (1.0 - sig))


def bits_of(count):
    return count.bit_length() - 1


def reversed_bits(value, width):
    return sum(((value >> bit) & 1) << (width - 1 - bit) for bit in range(width))


def call(kernel, outs, scratch=(), flops=0, bytes_accessed=0, limit=24):
    return functools.partial(
        pl.pallas_call,
        kernel,
        out_shape=outs,
        scratch_shapes=scratch,
        compiler_params=pltpu.CompilerParams(vmem_limit_bytes=limit * MIB),
        cost_estimate=pl.CostEstimate(flops=flops, bytes_accessed=bytes_accessed, transcendentals=0),
    )


def lay_windows(width, first, second, windows, tall):
    filt, cells = first.shape
    lanes = 2 * filt
    tall[pl.ds(8, cells), :] = jnp.concatenate([first, second], axis=0).astype(jnp.float32).T
    row = lax.broadcasted_iota(jnp.int32, (cells, lanes), 0)
    column = row & (width - 1) if width & (width - 1) == 0 else lax.rem(row, width)
    zero_rows = jnp.zeros((width, windows.shape[1]), jnp.bfloat16)
    windows[pl.ds(0, width), :] = zero_rows
    windows[pl.ds(width + cells, width), :] = zero_rows
    body = pl.ds(width, cells)
    windows[body, 0:lanes] = jnp.where(column != width - 1, tall[pl.ds(9, cells), :], 0.0).astype(jnp.bfloat16)
    windows[body, lanes : 2 * lanes] = tall[pl.ds(8, cells), :].astype(jnp.bfloat16)
    windows[body, 2 * lanes : 3 * lanes] = jnp.where(column != 0, tall[pl.ds(7, cells), :], 0.0).astype(jnp.bfloat16)


def turn_kernel(blocks, inputs, mine, part):
    chans = inputs.shape[1]
    rows = chans // blocks
    half, quarter = mine.shape[0], part.shape[0]
    order = lax.broadcasted_iota(jnp.int32, (half + quarter, chans), 0)
    other_half = order >= half
    row = order + jnp.where(other_half, (lax.axis_index("filt") & 1) * quarter - half, 0)
    side = (lax.axis_index("space") & 1) ^ other_half.astype(jnp.int32)
    source = (2 * (row >> bits_of(rows)) + side) * rows + (row & (rows - 1))
    picked = (lax.broadcasted_iota(jnp.int32, (half + quarter, chans), 1) == source).astype(jnp.bfloat16)
    turned = lax.dot_general(picked, inputs[...], (((1,), (1,)), ((), ())), preferred_element_type=jnp.float32)
    turned = turned.astype(jnp.bfloat16)
    mine[...] = turned[0:half, :]
    part[...] = turned[half:, :]


def order_kernel(weight, ordered):
    filt = weight.shape[1]
    odd = lax.axis_index("space") & 1
    zero = jnp.zeros(weight.shape[1:], jnp.bfloat16)
    for tap in range(9):
        b, c = divmod(tap, 3)
        rows = (weight[9 + tap], weight[18 * odd + tap], weight[18 - 18 * odd + tap], zero)
        for slot, value in zip((2 * c, 2 * c + 1, 2 * c + 6, 2 * c + 7), rows):
            ordered[b, pl.ds(slot * filt, filt), :] = value


def near_kernel(width, own, came, mine, ordered, pair, first, spread, tall):
    filt, cells = own.shape
    wide = pair.shape[1]
    lay_windows(width, own[...], came[0:filt, :], pair, tall)
    total = 0.0
    for b in range(3):
        rows = pl.ds((2 - b) * width, cells)
        first[:, b * wide : (b + 1) * wide] = jnp.dot(mine[...], pair[rows, :], preferred_element_type=jnp.float32)
        total = total + jnp.dot(pair[rows, :], ordered[b, 0:wide, :], preferred_element_type=jnp.float32)
    spread[...] = total


def outer_kernel(width, two_off, mine, ones, twos, second, tall):
    cells = mine.shape[1]
    wide = ones.shape[1]
    lay_windows(width, two_off[...], two_off[...], twos, tall)
    for b in range(3):
        rows = pl.ds((2 - b) * width, cells)
        second[:, b * wide : (b + 1) * wide] = jnp.dot(mine[...], ones[rows, :], preferred_element_type=jnp.float32)


def theirs_kernel(width, came, other, pair, twos, first, second, send):
    half = first.shape[0]
    cells = came.shape[1]
    wide = pair.shape[1]
    lanes = wide // 3
    filt = lanes // 2
    first_core = lax.axis_index("filt") & 1 == 0
    here = came[filt:, :]
    theirs = jnp.concatenate(
        [jnp.where(first_core, here, other[...]), jnp.where(first_core, other[...], here)], axis=0
    )
    left = lax.broadcasted_iota(jnp.int32, (half, lanes), 1) < filt

    def store(lo, hi, value):
        send[:, lo:hi] = value.astype(jnp.bfloat16)

    for b in range(3):
        rows = pl.ds((2 - b) * width, cells)
        near_terms = jnp.dot(theirs, pair[rows, :], preferred_element_type=jnp.float32)
        far_terms = jnp.dot(theirs, twos[rows, :], preferred_element_type=jnp.float32)
        for c in range(3):
            tap = 3 * b + c
            cut = slice(c * lanes, (c + 1) * lanes)
            lo = b * wide + c * lanes
            crossed = jnp.where(left, pltpu.roll(near_terms[:, cut], filt, 1), far_terms[:, cut])
            store(lo, lo + lanes, first[:, lo : lo + lanes] + crossed)
            outer = second[:, lo : lo + lanes] + near_terms[:, cut]
            lo = 3 * wide + tap // 2 * lanes
            if tap == 8:
                store(lo, lo + filt, outer[:, 0:filt])
            elif tap % 2 == 0:
                before = outer
            else:
                store(lo, lo + lanes, jnp.where(left, before, pltpu.roll(outer, filt, 1)))


def spread_kernel(width, groups, one_off, ordered, spread, ones, keep, send, tall):
    cells = spread.shape[0]
    wide = ones.shape[1]
    lay_windows(width, one_off[...], one_off[...], ones, tall)
    part = cells // groups
    index = lax.axis_index("filt")
    count = bits_of(groups)
    for target in reversed(range(groups)):
        block = 0
        for bit in range(count):
            differs = (target >> (count - 1 - bit)) & 1
            block = block + (((index >> bit) & 1) ^ differs) * (1 << bit)
        start = pl.multiple_of(block * part, part)
        total = spread[pl.ds(start, part), :]
        for b in range(3):
            rows = pl.ds(pl.multiple_of(start + (2 - b) * width, width), part)
            total = total + jnp.dot(ones[rows, :], ordered[b, wide:, :], preferred_element_type=jnp.float32)
        if target < groups // 2:
            keep[pl.ds(target * part, part), :] = total
        else:
            send[pl.ds((target - groups // 2) * part, part), :] = total.astype(jnp.bfloat16)


def halve_kernel(kept, came, keep, send):
    half = keep.shape[0]
    keep[...] = kept[0:half, :] + came[0:half, :].astype(jnp.float32)
    send[...] = (kept[half:, :] + came[half:, :].astype(jnp.float32)).astype(jnp.bfloat16)


def last_input_kernel(kept, came, out):
    out[...] = (kept[...] + came[...].astype(jnp.float32)).astype(out.dtype)


def last_weight_kernel(scale, filt, came, out):
    odd = lax.axis_index("space") & 1
    total = came[0].astype(jnp.float32)
    for number in range(1, came.shape[0]):
        total = total + came[number].astype(jnp.float32)
    total = total * scale
    for tap in range(9):
        slots = ((2 * tap, 9 + tap), (2 * tap + 1, 18 * odd + tap), (18 + tap, 18 - 18 * odd + tap))
        for slot, target in slots:
            out[target] = total[:, slot * filt : (slot + 1) * filt]


def swapped(value, axis, distance):
    count = lax.axis_size(axis)
    return lax.ppermute(value, axis, [(i, i ^ distance) for i in range(count)])


def halved(kept, came):
    rows, lanes = kept.shape
    if rows // 2 % 16:
        total = kept + came.astype(jnp.float32)
        return total[: rows // 2], total[rows // 2 :].astype(jnp.bfloat16)
    outs = (
        jax.ShapeDtypeStruct((rows // 2, lanes), jnp.float32),
        jax.ShapeDtypeStruct((rows // 2, lanes), jnp.bfloat16),
    )
    return call(halve_kernel, outs, flops=rows * lanes, bytes_accessed=9 * rows * lanes)(
        in_specs=[VMEM] * 2, out_specs=[VMEM] * 2
    )(kept, came)


def after(value, other):
    return lax.optimization_barrier((value, other))[0]


def on_device(inputs, out_grad, pre_act, weight):
    _, height, width, chans = inputs.shape
    taps, filt, _ = weight.shape
    cells = height * width
    blocks, groups = lax.axis_size("space"), lax.axis_size("filt")
    half, quarter = chans // 2, chans // 4
    bf16, f32 = jnp.bfloat16, jnp.float32
    shape = jax.ShapeDtypeStruct
    flops = 2 * cells * taps * filt * chans
    lanes = 6 * filt
    windows_shape = shape((cells + 2 * width, lanes), bf16)
    tall = pltpu.VMEM((cells + 16, 2 * filt), f32)

    mine, part = call(
        functools.partial(turn_kernel, blocks),
        (shape((half, cells), bf16), shape((quarter, cells), bf16)),
        bytes_accessed=MIB,
    )(in_specs=[VMEM], out_specs=[VMEM] * 2)(inputs.reshape(cells, chans))
    own = (out_grad[0].astype(f32) * silu_grad(pre_act[0].astype(f32))).astype(bf16)
    sent = jnp.concatenate([own, part], axis=0)
    came = swapped(sent, "space", 1)
    two_pairs = [(i, i - 2) for i in range(2, blocks, 2)] + [(i, i + 2) for i in range(1, blocks - 2, 2)]
    two_off = lax.ppermute(own, "space", two_pairs)
    one_pairs = [(i, i + 1) for i in range(1, blocks - 1, 2)]
    one_off = lax.ppermute(own, "space", one_pairs + [(target, source) for source, target in one_pairs])
    other = swapped(came[filt:], "filt", 1)

    ordered = call(order_kernel, shape((3, 2 * lanes, chans), bf16), bytes_accessed=MIB)(
        in_specs=[VMEM], out_specs=VMEM
    )(after(weight, mine))
    pair, first, spread = call(
        functools.partial(near_kernel, width),
        (windows_shape, shape((half, 3 * lanes), f32), shape((cells, chans), f32)),
        (tall,),
        flops=flops,
        bytes_accessed=4 * MIB,
    )(in_specs=[VMEM] * 4, out_specs=[VMEM] * 3)(own, came, mine, ordered)
    ones, kept_in, sent_in = call(
        functools.partial(spread_kernel, width, groups),
        (windows_shape, shape((cells // 2, chans), f32), shape((cells // 2, chans), bf16)),
        (tall,),
        flops=flops // 3,
        bytes_accessed=4 * MIB,
    )(in_specs=[VMEM] * 3, out_specs=[VMEM] * 3)(one_off, ordered, spread)
    came_in = swapped(sent_in, "filt", 1)
    twos, second = call(
        functools.partial(outer_kernel, width),
        (windows_shape, shape((half, 3 * lanes), f32)),
        (tall,),
        flops=4 * flops,
        bytes_accessed=2 * MIB,
    )(in_specs=[VMEM] * 3, out_specs=[VMEM] * 2)(two_off, mine, ones)
    terms = call(
        functools.partial(theirs_kernel, width),
        shape((half, taps * filt), bf16),
        flops=4 * flops,
        bytes_accessed=4 * MIB,
    )(in_specs=[VMEM] * 6, out_specs=VMEM)(came, other, pair, twos, first, second)
    members = [list(range(side, blocks, 2)) for side in range(2)]
    pieces = lax.all_to_all(
        terms.reshape(blocks // 2, chans // blocks, taps * filt), "space", 0, 0, axis_index_groups=members, tiled=True
    )
    came_in = after(came_in, terms)
    distance_in = 2
    while distance_in < groups:
        kept_in, sent_in = halved(kept_in, came_in)
        came_in = swapped(sent_in, "filt", distance_in)
        distance_in *= 2
    grad_input = call(last_input_kernel, shape((cells // groups, chans), bf16))(
        in_specs=[VMEM] * 2, out_specs=VMEM
    )(kept_in, came_in)
    grad_scale = float(cells * blocks) ** (-0.5)
    grad_weight = call(
        functools.partial(last_weight_kernel, grad_scale, filt), shape((taps, chans // blocks, filt), f32)
    )(in_specs=[VMEM], out_specs=VMEM)(after(pieces, grad_input))
    return grad_input.reshape(1, height // groups, width, chans), jnp.transpose(grad_weight, (1, 0, 2))


def solution(mesh):
    placed = (
        P("space", None, None, None),
        P("space", "filt", None),
        P("space", "filt", None),
        P(None, "filt", None),
    )
    return jax.shard_map(
        on_device,
        mesh=mesh,
        in_specs=placed,
        out_specs=(P("space", "filt", None, None), P("space", None, "filt")),
        check_vma=False,
    )
```

```python
import functools

import jax
import jax.numpy as jnp
from jax import lax
from jax.experimental import pallas as pl
from jax.experimental.pallas import tpu as pltpu
from jax.sharding import PartitionSpec as P

MIB = 1 << 20
EARLY, SPREAD, LATE, FINAL, ORDER = 3, 3, 3, 3, 3
VMEM = pl.BlockSpec(memory_space=pltpu.VMEM)


def silu_grad(values):
    sig = jax.nn.sigmoid(values)
    return sig * (1.0 + values * (1.0 - sig))


def bits_of(count):
    return count.bit_length() - 1


def reversed_bits(value, width):
    return sum(((value >> bit) & 1) << (width - 1 - bit) for bit in range(width))


def call(kernel, outs, scratch=(), flops=0, bytes_accessed=0, limit=24):
    return functools.partial(
        pl.pallas_call,
        kernel,
        out_shape=outs,
        scratch_shapes=scratch,
        compiler_params=pltpu.CompilerParams(vmem_limit_bytes=limit * MIB),
        cost_estimate=pl.CostEstimate(flops=flops, bytes_accessed=bytes_accessed, transcendentals=0),
    )


def lay_windows(width, first, second, windows, tall):
    filt, cells = first.shape
    lanes = 2 * filt
    tall[pl.ds(8, cells), :] = jnp.concatenate([first, second], axis=0).astype(jnp.float32).T
    row = lax.broadcasted_iota(jnp.int32, (cells, lanes), 0)
    column = row & (width - 1) if width & (width - 1) == 0 else lax.rem(row, width)
    zero_rows = jnp.zeros((width, windows.shape[1]), jnp.bfloat16)
    windows[pl.ds(0, width), :] = zero_rows
    windows[pl.ds(width + cells, width), :] = zero_rows
    body = pl.ds(width, cells)
    windows[body, 0:lanes] = jnp.where(column != width - 1, tall[pl.ds(9, cells), :], 0.0).astype(jnp.bfloat16)
    windows[body, lanes : 2 * lanes] = tall[pl.ds(8, cells), :].astype(jnp.bfloat16)
    windows[body, 2 * lanes : 3 * lanes] = jnp.where(column != 0, tall[pl.ds(7, cells), :], 0.0).astype(jnp.bfloat16)


def turn_kernel(blocks, inputs, mine, part):
    chans = inputs.shape[1]
    rows = chans // blocks
    half, quarter = mine.shape[0], part.shape[0]
    count = bits_of(blocks)
    order = lax.broadcasted_iota(jnp.int32, (half + quarter, chans), 0)
    order = order + jnp.where(order >= half, (lax.axis_index("filt") & 1) * quarter, 0)
    block = lax.axis_index("space") ^ reversed_bits(order >> bits_of(rows), count)
    source = (block << bits_of(rows)) | (order & (rows - 1))
    picked = (lax.broadcasted_iota(jnp.int32, (half + quarter, chans), 1) == source).astype(jnp.bfloat16)
    turned = lax.dot_general(picked, inputs[...], (((1,), (1,)), ((), ())), preferred_element_type=jnp.float32)
    turned = turned.astype(jnp.bfloat16)
    mine[...] = turned[0:half, :]
    part[...] = turned[half:, :]


def order_kernel(weight, early, late):
    filt = weight.shape[1]
    odd = lax.axis_index("space") & 1
    for tap in range(9):
        b, c = divmod(tap, 3)
        low, high = pl.ds(2 * c * filt, filt), pl.ds((2 * c + 1) * filt, filt)
        early[b, low, :] = jnp.zeros(weight.shape[1:], jnp.bfloat16)
        early[b, high, :] = weight[9 + tap]
        late[b, low, :] = weight[18 * odd + tap]
        late[b, high, :] = weight[18 - 18 * odd + tap]


def early_kernel(width, own, two_off, mine, came, other, weight, turned, terms, spread, windows, tall):
    cells = own.shape[1]
    half = mine.shape[0]
    wide = windows.shape[1]
    first_core = lax.axis_index("filt") & 1 == 0
    turned[0:half, :] = mine[...]
    turned[half : half + half // 2, :] = jnp.where(first_core, came[...], other[...])
    turned[half + half // 2 :, :] = jnp.where(first_core, other[...], came[...])
    lay_windows(width, two_off[...], own[...], windows, tall)
    total = 0.0
    for b in range(3):
        window = windows[pl.ds((2 - b) * width, cells), :]
        terms[:, b * wide : (b + 1) * wide] = jnp.dot(turned[...], window, preferred_element_type=jnp.float32)
        total = total + jnp.dot(window, weight[b], preferred_element_type=jnp.float32)
    spread[...] = total


def spread_kernel(width, groups, near, one_off, weight, spread, windows, keep, send, tall):
    cells = spread.shape[0]
    lay_windows(width, near[...], one_off[...], windows, tall)
    part = cells // groups
    index = lax.axis_index("filt")
    count = bits_of(groups)
    for target in reversed(range(groups)):
        block = 0
        for bit in range(count):
            differs = (target >> (count - 1 - bit)) & 1
            block = block + (((index >> bit) & 1) ^ differs) * (1 << bit)
        start = pl.multiple_of(block * part, part)
        total = spread[pl.ds(start, part), :]
        for b in range(3):
            rows = pl.ds(pl.multiple_of(start + (2 - b) * width, width), part)
            total = total + jnp.dot(windows[rows, :], weight[b], preferred_element_type=jnp.float32)
        if target < groups // 2:
            keep[pl.ds(target * part, part), :] = total
        else:
            send[pl.ds((target - groups // 2) * part, part), :] = total.astype(jnp.bfloat16)


def late_kernel(width, turned, windows, early, keep, *sends):
    half = turned.shape[0] // 2
    cells = turned.shape[1]
    wide = windows.shape[1]
    lanes = wide // 3
    filt = lanes // 2
    left = lax.broadcasted_iota(jnp.int32, (half, lanes), 1) < filt
    part = half // (len(sends) + 1)

    def store(lo, hi, value):
        keep[:, lo:hi] = value[0:part, :]
        for number, send in enumerate(sends, 1):
            send[:, lo:hi] = value[number * part : (number + 1) * part, :].astype(jnp.bfloat16)

    for b in range(3):
        window = windows[pl.ds((2 - b) * width, cells), :]
        terms = jnp.dot(turned[...], window, preferred_element_type=jnp.float32)
        for c in range(3):
            tap = 3 * b + c
            cut = slice(c * lanes, (c + 1) * lanes)
            lo = b * wide + c * lanes
            store(lo, lo + lanes, terms[0:half, cut] + early[half:, lo : lo + lanes])
            near_side, own_side = terms[half:, cut], early[0:half, lo : lo + lanes]
            lo = 3 * wide + tap // 2 * lanes
            if tap == 8:
                middle = near_side + pltpu.roll(own_side, filt, 1)
                store(lo, lo + filt, middle[:, 0:filt])
            elif tap % 2 == 0:
                before = near_side + pltpu.roll(own_side, filt, 1)
            else:
                store(lo, lo + lanes, jnp.where(left, before, pltpu.roll(near_side, filt, 1) + own_side))


def halve_kernel(kept, came, keep, send):
    half = keep.shape[0]
    keep[...] = kept[0:half, :] + came[0:half, :].astype(jnp.float32)
    send[...] = (kept[half:, :] + came[half:, :].astype(jnp.float32)).astype(jnp.bfloat16)


def last_input_kernel(kept, came, out):
    out[...] = (kept[...] + came[...].astype(jnp.float32)).astype(out.dtype)


def last_weight_kernel(scale, filt, kept, *rest):
    *came, out = rest
    odd = lax.axis_index("space") & 1
    total = kept[...]
    for piece in came:
        total = total + piece[...].astype(jnp.float32)
    total = total * scale
    for tap in range(9):
        slots = ((18 + tap, 9 + tap), (2 * tap, 18 * odd + tap), (2 * tap + 1, 18 - 18 * odd + tap))
        for slot, target in slots:
            out[target] = total[:, slot * filt : (slot + 1) * filt]


def swapped(value, axis, distance):
    count = lax.axis_size(axis)
    return lax.ppermute(value, axis, [(i, i ^ distance) for i in range(count)])


def halved(kept, came):
    rows, lanes = kept.shape
    if rows // 2 % 16:
        total = kept + came.astype(jnp.float32)
        return total[: rows // 2], total[rows // 2 :].astype(jnp.bfloat16)
    outs = (
        jax.ShapeDtypeStruct((rows // 2, lanes), jnp.float32),
        jax.ShapeDtypeStruct((rows // 2, lanes), jnp.bfloat16),
    )
    return call(halve_kernel, outs, flops=rows * lanes, bytes_accessed=9 * rows * lanes)(
        in_specs=[VMEM] * 2, out_specs=[VMEM] * 2
    )(kept, came)


def after(value, other):
    return lax.optimization_barrier((value, other))[0]


def on_device(inputs, out_grad, pre_act, weight):
    _, height, width, chans = inputs.shape
    taps, filt, _ = weight.shape
    cells = height * width
    blocks, groups = lax.axis_size("space"), lax.axis_size("filt")
    half, quarter = chans // 2, chans // 4
    bf16, f32 = jnp.bfloat16, jnp.float32
    shape = jax.ShapeDtypeStruct
    flops = 2 * cells * taps * filt * chans
    lanes = 6 * filt
    windows_shape = shape((cells + 2 * width, lanes), bf16)
    tall = pltpu.VMEM((cells + 16, 2 * filt), f32)

    own = (out_grad[0].astype(f32) * silu_grad(pre_act[0].astype(f32))).astype(bf16)
    mine, part = call(
        functools.partial(turn_kernel, blocks),
        (shape((half, cells), bf16), shape((quarter, cells), bf16)),
        bytes_accessed=MIB,
    )(in_specs=[VMEM], out_specs=[VMEM] * 2)(inputs.reshape(cells, chans))
    came = swapped(part, "space", 1)
    near = swapped(own, "space", 1)
    two_pairs = [(i, i - 2) for i in range(2, blocks, 2)] + [(i, i + 2) for i in range(1, blocks - 2, 2)]
    two_off = lax.ppermute(own, "space", two_pairs)
    one_pairs = [(i, i + 1) for i in range(1, blocks - 1, 2)]
    one_off = lax.ppermute(own, "space", one_pairs + [(target, source) for source, target in one_pairs])
    other = swapped(came, "filt", 1)

    weight_shape = shape((3, lanes, chans), bf16)
    early_weight, late_weight = call(order_kernel, (weight_shape, weight_shape), flops=ORDER * flops, bytes_accessed=MIB)(
        in_specs=[VMEM], out_specs=[VMEM] * 2
    )(after(weight, mine))
    turned, early, spread = call(
        functools.partial(early_kernel, width),
        (shape((chans, cells), bf16), shape((chans, 3 * lanes), f32), shape((cells, chans), f32)),
        (pltpu.VMEM(windows_shape.shape, bf16), tall),
        flops=EARLY * flops,
        bytes_accessed=4 * MIB,
    )(in_specs=[VMEM] * 6, out_specs=[VMEM] * 3)(own, two_off, mine, came, other, early_weight)
    windows, kept_in, sent_in = call(
        functools.partial(spread_kernel, width, groups),
        (windows_shape, shape((cells // 2, chans), f32), shape((cells // 2, chans), bf16)),
        (tall,),
        flops=SPREAD * flops,
        bytes_accessed=4 * MIB,
    )(in_specs=[VMEM] * 4, out_specs=[VMEM] * 3)(near, one_off, late_weight, spread)
    came_in = swapped(sent_in, "filt", 1)
    radix = min(4, blocks // 2)
    piece = half // radix
    kept, *sends = call(
        functools.partial(late_kernel, width),
        (shape((piece, taps * filt), f32),) + (shape((piece, taps * filt), bf16),) * (radix - 1),
        flops=LATE * flops,
        bytes_accessed=4 * MIB,
    )(in_specs=[VMEM] * 3, out_specs=[VMEM] * radix)(turned, windows, early)
    came_in = after(came_in, kept)

    distance = 2
    while True:
        spans = {2: (1,), 4: (2, 1, 3)}[radix]
        arrived = [swapped(sends[n - 1], "space", spans[n - 1] * distance) for n in range(1, radix)]
        distance *= radix
        if distance >= blocks:
            break
        total = kept
        for value in arrived:
            total = total + value.astype(f32)
        radix = min(4, blocks // distance)
        piece //= radix
        kept, *sends = (total[n * piece : (n + 1) * piece] for n in range(radix))
        sends = [value.astype(bf16) for value in sends]

    distance_in = 2
    while distance_in < groups:
        kept_in, sent_in = halved(kept_in, came_in)
        came_in = swapped(sent_in, "filt", distance_in)
        distance_in *= 2
    grad_scale = float(cells * blocks) ** (-0.5)
    grad_weight = call(
        functools.partial(last_weight_kernel, grad_scale, filt),
        shape((taps, chans // blocks, filt), f32),
        flops=FINAL * flops,
    )(in_specs=[VMEM] * (len(arrived) + 1), out_specs=VMEM)(kept, *arrived)
    grad_input = call(last_input_kernel, shape((cells // groups, chans), bf16))(
        in_specs=[VMEM] * 2, out_specs=VMEM
    )(after(kept_in, grad_weight), came_in)
    return grad_input.reshape(1, height // groups, width, chans), jnp.transpose(grad_weight, (1, 0, 2))


def solution(mesh):
    placed = (
        P("space", None, None, None),
        P("space", "filt", None),
        P("space", "filt", None),
        P(None, "filt", None),
    )
    return jax.shard_map(
        on_device,
        mesh=mesh,
        in_specs=placed,
        out_specs=(P("space", "filt", None, None), P("space", None, "filt")),
        check_vma=False,
    )
```

```python
import functools

import jax
import jax.numpy as jnp
from jax import lax
from jax.experimental import pallas as pl
from jax.experimental.pallas import tpu as pltpu
from jax.sharding import PartitionSpec as P

MIB = 1 << 20
TURN, EARLY, TWO, SPREAD, LATE, FINAL, ORDER = 3, 3, 3, 3, 3, 3, 3
VMEM = pl.BlockSpec(memory_space=pltpu.VMEM)


def silu_grad(values):
    sig = jax.nn.sigmoid(values)
    return sig * (1.0 + values * (1.0 - sig))


def bits_of(count):
    return count.bit_length() - 1


def reversed_bits(value, width):
    return sum(((value >> bit) & 1) << (width - 1 - bit) for bit in range(width))


def call(kernel, outs, scratch=(), flops=0, bytes_accessed=0, limit=24):
    return functools.partial(
        pl.pallas_call,
        kernel,
        out_shape=outs,
        scratch_shapes=scratch,
        compiler_params=pltpu.CompilerParams(vmem_limit_bytes=limit * MIB),
        cost_estimate=pl.CostEstimate(flops=flops, bytes_accessed=bytes_accessed, transcendentals=0),
    )


def lay_windows(width, first, second, windows, tall):
    filt, cells = first.shape
    lanes = 2 * filt
    tall[pl.ds(8, cells), :] = jnp.concatenate([first, second], axis=0).astype(jnp.float32).T
    row = lax.broadcasted_iota(jnp.int32, (cells, lanes), 0)
    column = row & (width - 1) if width & (width - 1) == 0 else lax.rem(row, width)
    zero_rows = jnp.zeros((width, windows.shape[1]), jnp.bfloat16)
    windows[pl.ds(0, width), :] = zero_rows
    windows[pl.ds(width + cells, width), :] = zero_rows
    body = pl.ds(width, cells)
    windows[body, 0:lanes] = jnp.where(column != width - 1, tall[pl.ds(9, cells), :], 0.0).astype(jnp.bfloat16)
    windows[body, lanes : 2 * lanes] = tall[pl.ds(8, cells), :].astype(jnp.bfloat16)
    windows[body, 2 * lanes : 3 * lanes] = jnp.where(column != 0, tall[pl.ds(7, cells), :], 0.0).astype(jnp.bfloat16)


def turn_kernel(blocks, inputs, mine, part):
    chans = inputs.shape[1]
    rows = chans // blocks
    half, quarter = mine.shape[0], part.shape[0]
    count = bits_of(blocks)
    order = lax.broadcasted_iota(jnp.int32, (half + quarter, chans), 0)
    order = order + jnp.where(order >= half, (lax.axis_index("filt") & 1) * quarter, 0)
    block = lax.axis_index("space") ^ reversed_bits(order >> bits_of(rows), count)
    source = (block << bits_of(rows)) | (order & (rows - 1))
    picked = (lax.broadcasted_iota(jnp.int32, (half + quarter, chans), 1) == source).astype(jnp.bfloat16)
    turned = lax.dot_general(picked, inputs[...], (((1,), (1,)), ((), ())), preferred_element_type=jnp.float32)
    turned = turned.astype(jnp.bfloat16)
    mine[...] = turned[0:half, :]
    part[...] = turned[half:, :]


def grads_kernel(out_grad, pre_act, _, own):
    own[...] = (out_grad[...].astype(jnp.float32) * silu_grad(pre_act[...].astype(jnp.float32))).astype(own.dtype)


def order_kernel(weight, early, late):
    filt = weight.shape[1]
    odd = lax.axis_index("space") & 1
    for tap in range(9):
        b, c = divmod(tap, 3)
        low, high = pl.ds(2 * c * filt, filt), pl.ds((2 * c + 1) * filt, filt)
        early[b, low, :] = weight[9 + tap]
        early[b, high, :] = jnp.zeros(weight.shape[1:], jnp.bfloat16)
        late[b, low, :] = weight[18 * odd + tap]
        late[b, high, :] = weight[18 - 18 * odd + tap]


def early_kernel(width, own, mine, came, other, weight, turned, terms, spread, windows, tall):
    cells = own.shape[1]
    half = mine.shape[0]
    wide = windows.shape[1]
    first_core = lax.axis_index("filt") & 1 == 0
    turned[0:half, :] = mine[...]
    turned[half : half + half // 2, :] = jnp.where(first_core, came[...], other[...])
    turned[half + half // 2 :, :] = jnp.where(first_core, other[...], came[...])
    lay_windows(width, own[...], own[...], windows, tall)
    total = 0.0
    for b in range(3):
        window = windows[pl.ds((2 - b) * width, cells), :]
        terms[:, b * wide : (b + 1) * wide] = jnp.dot(turned[...], window, preferred_element_type=jnp.float32)
        total = total + jnp.dot(window, weight[b], preferred_element_type=jnp.float32)
    spread[...] = total


def spread_kernel(width, groups, near, one_off, weight, spread, windows, keep, send, tall):
    cells = spread.shape[0]
    lay_windows(width, near[...], one_off[...], windows, tall)
    part = cells // groups
    index = lax.axis_index("filt")
    count = bits_of(groups)
    for target in reversed(range(groups)):
        block = 0
        for bit in range(count):
            differs = (target >> (count - 1 - bit)) & 1
            block = block + (((index >> bit) & 1) ^ differs) * (1 << bit)
        start = pl.multiple_of(block * part, part)
        total = spread[pl.ds(start, part), :]
        for b in range(3):
            rows = pl.ds(pl.multiple_of(start + (2 - b) * width, width), part)
            total = total + jnp.dot(windows[rows, :], weight[b], preferred_element_type=jnp.float32)
        if target < groups // 2:
            keep[pl.ds(target * part, part), :] = total
        else:
            send[pl.ds((target - groups // 2) * part, part), :] = total.astype(jnp.bfloat16)


def two_kernel(width, turned, two_off, terms, windows, tall):
    half = turned.shape[0] // 2
    cells = turned.shape[1]
    wide = windows.shape[1]
    lay_windows(width, two_off[...], two_off[...], windows, tall)
    for b in range(3):
        window = windows[pl.ds((2 - b) * width, cells), :]
        terms[:, b * wide : (b + 1) * wide] = jnp.dot(
            turned[pl.ds(half, half), :], window, preferred_element_type=jnp.float32
        )


def late_kernel(width, turned, windows, two, early, keep, *sends):
    half = turned.shape[0] // 2
    cells = turned.shape[1]
    wide = windows.shape[1]
    lanes = wide // 3
    filt = lanes // 2
    left = lax.broadcasted_iota(jnp.int32, (half, lanes), 1) < filt
    part = half // (len(sends) + 1)

    def store(lo, hi, value):
        keep[:, lo:hi] = value[0:part, :]
        for number, send in enumerate(sends, 1):
            send[:, lo:hi] = value[number * part : (number + 1) * part, :].astype(jnp.bfloat16)

    for b in range(3):
        window = windows[pl.ds((2 - b) * width, cells), :]
        terms = jnp.dot(turned[...], window, preferred_element_type=jnp.float32)
        for c in range(3):
            tap = 3 * b + c
            cut = slice(c * lanes, (c + 1) * lanes)
            lo = b * wide + c * lanes
            crossed = jnp.where(left, two[:, lo : lo + lanes], early[half:, lo : lo + lanes])
            store(lo, lo + lanes, terms[0:half, cut] + crossed)
            middle = terms[half:, cut] + early[0:half, lo : lo + lanes]
            lo = 3 * wide + tap // 2 * lanes
            if tap == 8:
                store(lo, lo + filt, middle[:, 0:filt])
            elif tap % 2 == 0:
                before = middle
            else:
                store(lo, lo + lanes, jnp.where(left, before, pltpu.roll(middle, filt, 1)))


def halve_kernel(kept, came, keep, send):
    half = keep.shape[0]
    keep[...] = kept[0:half, :] + came[0:half, :].astype(jnp.float32)
    send[...] = (kept[half:, :] + came[half:, :].astype(jnp.float32)).astype(jnp.bfloat16)


def sum_kernel(scale, kept, *rest):
    *came, out = rest
    total = kept[...]
    for piece in came:
        total = total + piece[...].astype(jnp.float32)
    out[...] = total * scale


def last_kernel(filt, summed, kept, came, out, grad_input):
    grad_input[...] = (kept[...] + came[...].astype(jnp.float32)).astype(grad_input.dtype)
    odd = lax.axis_index("space") & 1
    total = summed[...]
    for tap in range(9):
        slots = ((18 + tap, 9 + tap), (2 * tap, 18 * odd + tap), (2 * tap + 1, 18 - 18 * odd + tap))
        for slot, target in slots:
            out[target] = total[:, slot * filt : (slot + 1) * filt]


def swapped(value, axis, distance):
    count = lax.axis_size(axis)
    return lax.ppermute(value, axis, [(i, i ^ distance) for i in range(count)])


def halved(kept, came):
    rows, lanes = kept.shape
    if rows // 2 % 16:
        total = kept + came.astype(jnp.float32)
        return total[: rows // 2], total[rows // 2 :].astype(jnp.bfloat16)
    outs = (
        jax.ShapeDtypeStruct((rows // 2, lanes), jnp.float32),
        jax.ShapeDtypeStruct((rows // 2, lanes), jnp.bfloat16),
    )
    return call(halve_kernel, outs, flops=rows * lanes, bytes_accessed=9 * rows * lanes)(
        in_specs=[VMEM] * 2, out_specs=[VMEM] * 2
    )(kept, came)


def after(value, other):
    return lax.optimization_barrier((value, other))[0]


def on_device(inputs, out_grad, pre_act, weight):
    _, height, width, chans = inputs.shape
    taps, filt, _ = weight.shape
    cells = height * width
    blocks, groups = lax.axis_size("space"), lax.axis_size("filt")
    half, quarter = chans // 2, chans // 4
    bf16, f32 = jnp.bfloat16, jnp.float32
    shape = jax.ShapeDtypeStruct
    flops = 2 * cells * taps * filt * chans
    lanes = 6 * filt
    windows_shape = shape((cells + 2 * width, lanes), bf16)
    tall = pltpu.VMEM((cells + 16, 2 * filt), f32)

    mine, part = call(
        functools.partial(turn_kernel, blocks),
        (shape((half, cells), bf16), shape((quarter, cells), bf16)),
        flops=TURN * flops,
    )(in_specs=[VMEM], out_specs=[VMEM] * 2)(inputs.reshape(cells, chans))
    own = call(grads_kernel, shape((filt, cells), bf16))(in_specs=[VMEM] * 3, out_specs=VMEM)(
        out_grad[0], pre_act[0], part
    )
    came = swapped(after(part, own), "space", 1)
    near = swapped(own, "space", 1)
    two_pairs = [(i, i - 2) for i in range(2, blocks, 2)] + [(i, i + 2) for i in range(1, blocks - 2, 2)]
    two_off = lax.ppermute(own, "space", two_pairs)
    one_pairs = [(i, i + 1) for i in range(1, blocks - 1, 2)]
    one_off = lax.ppermute(own, "space", one_pairs + [(target, source) for source, target in one_pairs])
    other = swapped(came, "filt", 1)

    weight_shape = shape((3, lanes, chans), bf16)
    early_weight, late_weight = call(order_kernel, (weight_shape, weight_shape), flops=ORDER * flops, bytes_accessed=MIB)(
        in_specs=[VMEM], out_specs=[VMEM] * 2
    )(after(weight, mine))
    turned, early, spread = call(
        functools.partial(early_kernel, width),
        (shape((chans, cells), bf16), shape((chans, 3 * lanes), f32), shape((cells, chans), f32)),
        (pltpu.VMEM(windows_shape.shape, bf16), tall),
        flops=EARLY * flops,
        bytes_accessed=4 * MIB,
    )(in_specs=[VMEM] * 5, out_specs=[VMEM] * 3)(own, mine, came, other, early_weight)
    two = call(
        functools.partial(two_kernel, width),
        shape((half, 3 * lanes), f32),
        (pltpu.VMEM(windows_shape.shape, bf16), tall),
        flops=TWO * flops,
    )(in_specs=[VMEM] * 2, out_specs=VMEM)(turned, two_off)
    windows, kept_in, sent_in = call(
        functools.partial(spread_kernel, width, groups),
        (windows_shape, shape((cells // 2, chans), f32), shape((cells // 2, chans), bf16)),
        (tall,),
        flops=SPREAD * flops,
        bytes_accessed=4 * MIB,
    )(in_specs=[VMEM] * 4, out_specs=[VMEM] * 3)(near, one_off, late_weight, after(spread, two))
    came_in = swapped(sent_in, "filt", 1)
    radix = min(4, blocks // 2)
    piece = half // radix
    kept, *sends = call(
        functools.partial(late_kernel, width),
        (shape((piece, taps * filt), f32),) + (shape((piece, taps * filt), bf16),) * (radix - 1),
        flops=LATE * flops,
        bytes_accessed=4 * MIB,
    )(in_specs=[VMEM] * 4, out_specs=[VMEM] * radix)(turned, windows, two, early)
    came_in = after(came_in, kept)

    distance = 2
    while True:
        spans = {2: (1,), 4: (2, 1, 3)}[radix]
        arrived = [swapped(sends[n - 1], "space", spans[n - 1] * distance) for n in range(1, radix)]
        distance *= radix
        if distance >= blocks:
            break
        total = kept
        for value in arrived:
            total = total + value.astype(f32)
        radix = min(4, blocks // distance)
        piece //= radix
        kept, *sends = (total[n * piece : (n + 1) * piece] for n in range(radix))
        sends = [value.astype(bf16) for value in sends]

    distance_in = 2
    while distance_in < groups:
        kept_in, sent_in = halved(kept_in, came_in)
        came_in = swapped(sent_in, "filt", distance_in)
        distance_in *= 2
    grad_scale = float(cells * blocks) ** (-0.5)
    summed = call(
        functools.partial(sum_kernel, grad_scale), shape((chans // blocks, taps * filt), f32), flops=FINAL * flops
    )(in_specs=[VMEM] * (len(arrived) + 1), out_specs=VMEM)(kept, *arrived)
    grad_weight, grad_input = call(
        functools.partial(last_kernel, filt),
        (shape((taps, chans // blocks, filt), f32), shape((cells // groups, chans), bf16)),
    )(in_specs=[VMEM] * 3, out_specs=[VMEM] * 2)(summed, kept_in, came_in)
    return grad_input.reshape(1, height // groups, width, chans), jnp.transpose(grad_weight, (1, 0, 2))


def solution(mesh):
    placed = (
        P("space", None, None, None),
        P("space", "filt", None),
        P("space", "filt", None),
        P(None, "filt", None),
    )
    return jax.shard_map(
        on_device,
        mesh=mesh,
        in_specs=placed,
        out_specs=(P("space", "filt", None, None), P("space", None, "filt")),
        check_vma=False,
    )
```

```python
import functools

import jax
import jax.numpy as jnp
from jax import lax
from jax.experimental import pallas as pl
from jax.experimental.pallas import tpu as pltpu
from jax.sharding import PartitionSpec as P

MIB = 1 << 20
TURN, EARLY, TWO, SPREAD, LATE, FINAL, ORDER = 3, 3, 3, 3, 3, 3, 3
VMEM = pl.BlockSpec(memory_space=pltpu.VMEM)


def silu_grad(values):
    sig = jax.nn.sigmoid(values)
    return sig * (1.0 + values * (1.0 - sig))


def bits_of(count):
    return count.bit_length() - 1


def reversed_bits(value, width):
    return sum(((value >> bit) & 1) << (width - 1 - bit) for bit in range(width))


def call(kernel, outs, scratch=(), flops=0, bytes_accessed=0, limit=24):
    return functools.partial(
        pl.pallas_call,
        kernel,
        out_shape=outs,
        scratch_shapes=scratch,
        compiler_params=pltpu.CompilerParams(vmem_limit_bytes=limit * MIB),
        cost_estimate=pl.CostEstimate(flops=flops, bytes_accessed=bytes_accessed, transcendentals=0),
    )


def lay_windows(width, first, second, windows, tall):
    filt, cells = first.shape
    lanes = 2 * filt
    tall[pl.ds(8, cells), :] = jnp.concatenate([first, second], axis=0).astype(jnp.float32).T
    row = lax.broadcasted_iota(jnp.int32, (cells, lanes), 0)
    column = row & (width - 1) if width & (width - 1) == 0 else lax.rem(row, width)
    zero_rows = jnp.zeros((width, windows.shape[1]), jnp.bfloat16)
    windows[pl.ds(0, width), :] = zero_rows
    windows[pl.ds(width + cells, width), :] = zero_rows
    body = pl.ds(width, cells)
    windows[body, 0:lanes] = jnp.where(column != width - 1, tall[pl.ds(9, cells), :], 0.0).astype(jnp.bfloat16)
    windows[body, lanes : 2 * lanes] = tall[pl.ds(8, cells), :].astype(jnp.bfloat16)
    windows[body, 2 * lanes : 3 * lanes] = jnp.where(column != 0, tall[pl.ds(7, cells), :], 0.0).astype(jnp.bfloat16)


def turn_kernel(blocks, inputs, mine, part):
    chans = inputs.shape[1]
    rows = chans // blocks
    half, quarter = mine.shape[0], part.shape[0]
    count = bits_of(blocks)
    order = lax.broadcasted_iota(jnp.int32, (half + quarter, chans), 0)
    order = order + jnp.where(order >= half, (lax.axis_index("filt") & 1) * quarter, 0)
    block = lax.axis_index("space") ^ reversed_bits(order >> bits_of(rows), count)
    source = (block << bits_of(rows)) | (order & (rows - 1))
    picked = (lax.broadcasted_iota(jnp.int32, (half + quarter, chans), 1) == source).astype(jnp.bfloat16)
    turned = lax.dot_general(picked, inputs[...], (((1,), (1,)), ((), ())), preferred_element_type=jnp.float32)
    turned = turned.astype(jnp.bfloat16)
    mine[...] = turned[0:half, :]
    part[...] = turned[half:, :]


def grads_kernel(out_grad, pre_act, _, own):
    own[...] = (out_grad[...].astype(jnp.float32) * silu_grad(pre_act[...].astype(jnp.float32))).astype(own.dtype)


def order_kernel(weight, early, late):
    filt = weight.shape[1]
    odd = lax.axis_index("space") & 1
    for tap in range(9):
        b, c = divmod(tap, 3)
        low, high = pl.ds(2 * c * filt, filt), pl.ds((2 * c + 1) * filt, filt)
        early[b, low, :] = weight[9 + tap]
        early[b, high, :] = jnp.zeros(weight.shape[1:], jnp.bfloat16)
        late[b, low, :] = weight[18 * odd + tap]
        late[b, high, :] = weight[18 - 18 * odd + tap]


def early_kernel(width, own, mine, came, other, weight, turned, terms, spread, windows, tall):
    cells = own.shape[1]
    half = mine.shape[0]
    wide = windows.shape[1]
    first_core = lax.axis_index("filt") & 1 == 0
    turned[0:half, :] = mine[...]
    turned[half : half + half // 2, :] = jnp.where(first_core, came[...], other[...])
    turned[half + half // 2 :, :] = jnp.where(first_core, other[...], came[...])
    lay_windows(width, own[...], own[...], windows, tall)
    total = 0.0
    for b in range(3):
        window = windows[pl.ds((2 - b) * width, cells), :]
        terms[:, b * wide : (b + 1) * wide] = jnp.dot(turned[...], window, preferred_element_type=jnp.float32)
        total = total + jnp.dot(window, weight[b], preferred_element_type=jnp.float32)
    spread[...] = total


def spread_kernel(width, groups, near, one_off, weight, spread, windows, keep, send, tall):
    cells = spread.shape[0]
    lay_windows(width, near[...], one_off[...], windows, tall)
    part = cells // groups
    index = lax.axis_index("filt")
    count = bits_of(groups)
    for target in reversed(range(groups)):
        block = 0
        for bit in range(count):
            differs = (target >> (count - 1 - bit)) & 1
            block = block + (((index >> bit) & 1) ^ differs) * (1 << bit)
        start = pl.multiple_of(block * part, part)
        total = spread[pl.ds(start, part), :]
        for b in range(3):
            rows = pl.ds(pl.multiple_of(start + (2 - b) * width, width), part)
            total = total + jnp.dot(windows[rows, :], weight[b], preferred_element_type=jnp.float32)
        if target < groups // 2:
            keep[pl.ds(target * part, part), :] = total
        else:
            send[pl.ds((target - groups // 2) * part, part), :] = total.astype(jnp.bfloat16)


def two_kernel(width, turned, two_off, terms, windows, tall):
    half = turned.shape[0] // 2
    cells = turned.shape[1]
    wide = windows.shape[1]
    lay_windows(width, two_off[...], two_off[...], windows, tall)
    for b in range(3):
        window = windows[pl.ds((2 - b) * width, cells), :]
        terms[:, b * wide : (b + 1) * wide] = jnp.dot(
            turned[pl.ds(half, half), :], window, preferred_element_type=jnp.float32
        )


def late_kernel(width, turned, windows, two, early, keep, *sends):
    half = turned.shape[0] // 2
    cells = turned.shape[1]
    wide = windows.shape[1]
    lanes = wide // 3
    filt = lanes // 2
    left = lax.broadcasted_iota(jnp.int32, (half, lanes), 1) < filt
    part = half // (len(sends) + 1)

    def store(lo, hi, value):
        keep[:, lo:hi] = value[0:part, :]
        for number, send in enumerate(sends, 1):
            send[:, lo:hi] = value[number * part : (number + 1) * part, :].astype(jnp.bfloat16)

    for b in range(3):
        window = windows[pl.ds((2 - b) * width, cells), :]
        terms = jnp.dot(turned[...], window, preferred_element_type=jnp.float32)
        for c in range(3):
            tap = 3 * b + c
            cut = slice(c * lanes, (c + 1) * lanes)
            lo = b * wide + c * lanes
            crossed = jnp.where(left, two[:, lo : lo + lanes], early[half:, lo : lo + lanes])
            store(lo, lo + lanes, terms[0:half, cut] + crossed)
            middle = terms[half:, cut] + early[0:half, lo : lo + lanes]
            lo = 3 * wide + tap // 2 * lanes
            if tap == 8:
                store(lo, lo + filt, middle[:, 0:filt])
            elif tap % 2 == 0:
                before = middle
            else:
                store(lo, lo + lanes, jnp.where(left, before, pltpu.roll(middle, filt, 1)))


def halve_kernel(kept, came, keep, send):
    half = keep.shape[0]
    keep[...] = kept[0:half, :] + came[0:half, :].astype(jnp.float32)
    send[...] = (kept[half:, :] + came[half:, :].astype(jnp.float32)).astype(jnp.bfloat16)


def sum_kernel(scale, kept, *rest):
    *came, out = rest
    total = kept[...]
    for piece in came:
        total = total + piece[...].astype(jnp.float32)
    out[...] = total * scale


def last_kernel(filt, summed, kept, came, out, grad_input):
    grad_input[...] = (kept[...] + came[...].astype(jnp.float32)).astype(grad_input.dtype)
    odd = lax.axis_index("space") & 1
    total = summed[...]
    for tap in range(9):
        slots = ((18 + tap, 9 + tap), (2 * tap, 18 * odd + tap), (2 * tap + 1, 18 - 18 * odd + tap))
        for slot, target in slots:
            out[target] = total[:, slot * filt : (slot + 1) * filt]


def swapped(value, axis, distance):
    count = lax.axis_size(axis)
    return lax.ppermute(value, axis, [(i, i ^ distance) for i in range(count)])


def halved(kept, came):
    rows, lanes = kept.shape
    if rows // 2 % 16:
        total = kept + came.astype(jnp.float32)
        return total[: rows // 2], total[rows // 2 :].astype(jnp.bfloat16)
    outs = (
        jax.ShapeDtypeStruct((rows // 2, lanes), jnp.float32),
        jax.ShapeDtypeStruct((rows // 2, lanes), jnp.bfloat16),
    )
    return call(halve_kernel, outs, flops=rows * lanes, bytes_accessed=9 * rows * lanes)(
        in_specs=[VMEM] * 2, out_specs=[VMEM] * 2
    )(kept, came)


def after(value, other):
    return lax.optimization_barrier((value, other))[0]


def on_device(inputs, out_grad, pre_act, weight):
    _, height, width, chans = inputs.shape
    taps, filt, _ = weight.shape
    cells = height * width
    blocks, groups = lax.axis_size("space"), lax.axis_size("filt")
    half, quarter = chans // 2, chans // 4
    bf16, f32 = jnp.bfloat16, jnp.float32
    shape = jax.ShapeDtypeStruct
    flops = 2 * cells * taps * filt * chans
    lanes = 6 * filt
    windows_shape = shape((cells + 2 * width, lanes), bf16)
    tall = pltpu.VMEM((cells + 16, 2 * filt), f32)

    mine, part = call(
        functools.partial(turn_kernel, blocks),
        (shape((half, cells), bf16), shape((quarter, cells), bf16)),
        flops=TURN * flops,
    )(in_specs=[VMEM], out_specs=[VMEM] * 2)(inputs.reshape(cells, chans))
    own = call(grads_kernel, shape((filt, cells), bf16))(in_specs=[VMEM] * 3, out_specs=VMEM)(
        out_grad[0], pre_act[0], part
    )
    came = swapped(after(part, own), "space", 1)
    near = swapped(own, "space", 1)
    weight_shape = shape((3, lanes, chans), bf16)
    early_weight, late_weight = call(order_kernel, (weight_shape, weight_shape), flops=int(ORDER * flops), bytes_accessed=MIB)(
        in_specs=[VMEM], out_specs=[VMEM] * 2
    )(after(weight, mine))
    two_pairs = [(i, i - 2) for i in range(2, blocks, 2)] + [(i, i + 2) for i in range(1, blocks - 2, 2)]
    two_off = lax.ppermute(after(own, early_weight), "space", two_pairs)
    one_pairs = [(i, i + 1) for i in range(1, blocks - 1, 2)]
    one_off = lax.ppermute(own, "space", one_pairs + [(target, source) for source, target in one_pairs])
    other = swapped(came, "filt", 1)

    turned, early, spread = call(
        functools.partial(early_kernel, width),
        (shape((chans, cells), bf16), shape((chans, 3 * lanes), f32), shape((cells, chans), f32)),
        (pltpu.VMEM(windows_shape.shape, bf16), tall),
        flops=EARLY * flops,
        bytes_accessed=4 * MIB,
    )(in_specs=[VMEM] * 5, out_specs=[VMEM] * 3)(own, mine, came, other, early_weight)
    two = call(
        functools.partial(two_kernel, width),
        shape((half, 3 * lanes), f32),
        (pltpu.VMEM(windows_shape.shape, bf16), tall),
        flops=TWO * flops,
    )(in_specs=[VMEM] * 2, out_specs=VMEM)(turned, two_off)
    windows, kept_in, sent_in = call(
        functools.partial(spread_kernel, width, groups),
        (windows_shape, shape((cells // 2, chans), f32), shape((cells // 2, chans), bf16)),
        (tall,),
        flops=SPREAD * flops,
        bytes_accessed=4 * MIB,
    )(in_specs=[VMEM] * 4, out_specs=[VMEM] * 3)(near, one_off, late_weight, spread)
    came_in = swapped(sent_in, "filt", 1)
    radix = min(4, blocks // 2)
    piece = half // radix
    kept, *sends = call(
        functools.partial(late_kernel, width),
        (shape((piece, taps * filt), f32),) + (shape((piece, taps * filt), bf16),) * (radix - 1),
        flops=LATE * flops,
        bytes_accessed=4 * MIB,
    )(in_specs=[VMEM] * 4, out_specs=[VMEM] * radix)(turned, windows, two, early)
    came_in = after(came_in, kept)

    distance = 2
    while True:
        spans = {2: (1,), 4: (2, 1, 3)}[radix]
        arrived = [swapped(sends[n - 1], "space", spans[n - 1] * distance) for n in range(1, radix)]
        distance *= radix
        if distance >= blocks:
            break
        total = kept
        for value in arrived:
            total = total + value.astype(f32)
        radix = min(4, blocks // distance)
        piece //= radix
        kept, *sends = (total[n * piece : (n + 1) * piece] for n in range(radix))
        sends = [value.astype(bf16) for value in sends]

    distance_in = 2
    while distance_in < groups:
        kept_in, sent_in = halved(kept_in, came_in)
        came_in = swapped(sent_in, "filt", distance_in)
        distance_in *= 2
    grad_scale = float(cells * blocks) ** (-0.5)
    summed = call(
        functools.partial(sum_kernel, grad_scale), shape((chans // blocks, taps * filt), f32), flops=FINAL * flops
    )(in_specs=[VMEM] * (len(arrived) + 1), out_specs=VMEM)(kept, *arrived)
    grad_weight, grad_input = call(
        functools.partial(last_kernel, filt),
        (shape((taps, chans // blocks, filt), f32), shape((cells // groups, chans), bf16)),
    )(in_specs=[VMEM] * 3, out_specs=[VMEM] * 2)(summed, kept_in, came_in)
    return grad_input.reshape(1, height // groups, width, chans), jnp.transpose(grad_weight, (1, 0, 2))


def solution(mesh):
    placed = (
        P("space", None, None, None),
        P("space", "filt", None),
        P("space", "filt", None),
        P(None, "filt", None),
    )
    return jax.shard_map(
        on_device,
        mesh=mesh,
        in_specs=placed,
        out_specs=(P("space", "filt", None, None), P("space", None, "filt")),
        check_vma=False,
    )
```

```python
import functools

import jax
import jax.numpy as jnp
from jax import lax
from jax.experimental import pallas as pl
from jax.experimental.pallas import tpu as pltpu
from jax.sharding import PartitionSpec as P

MIB = 1 << 20
PICK, TURN, EARLY, TWO, SPREAD, LATE, FINAL, ORDER = 3, 1, 3, 3, 3, 3, 3, 3
VMEM = pl.BlockSpec(memory_space=pltpu.VMEM)


def silu_grad(values):
    sig = jax.nn.sigmoid(values)
    return sig * (1.0 + values * (1.0 - sig))


def bits_of(count):
    return count.bit_length() - 1


def reversed_bits(value, width):
    return sum(((value >> bit) & 1) << (width - 1 - bit) for bit in range(width))


def call(kernel, outs, scratch=(), flops=0, bytes_accessed=0, limit=24):
    return functools.partial(
        pl.pallas_call,
        kernel,
        out_shape=outs,
        scratch_shapes=scratch,
        compiler_params=pltpu.CompilerParams(vmem_limit_bytes=limit * MIB),
        cost_estimate=pl.CostEstimate(flops=flops, bytes_accessed=bytes_accessed, transcendentals=0),
    )


def lay_windows(width, first, second, windows, tall):
    filt, cells = first.shape
    lanes = 2 * filt
    tall[pl.ds(8, cells), :] = jnp.concatenate([first, second], axis=0).astype(jnp.float32).T
    row = lax.broadcasted_iota(jnp.int32, (cells, lanes), 0)
    column = row & (width - 1) if width & (width - 1) == 0 else lax.rem(row, width)
    zero_rows = jnp.zeros((width, windows.shape[1]), jnp.bfloat16)
    windows[pl.ds(0, width), :] = zero_rows
    windows[pl.ds(width + cells, width), :] = zero_rows
    body = pl.ds(width, cells)
    windows[body, 0:lanes] = jnp.where(column != width - 1, tall[pl.ds(9, cells), :], 0.0).astype(jnp.bfloat16)
    windows[body, lanes : 2 * lanes] = tall[pl.ds(8, cells), :].astype(jnp.bfloat16)
    windows[body, 2 * lanes : 3 * lanes] = jnp.where(column != 0, tall[pl.ds(7, cells), :], 0.0).astype(jnp.bfloat16)


def pick_kernel(blocks, picked):
    size, chans = picked.shape
    rows = chans // blocks
    half = chans // 2
    count = bits_of(blocks)
    order = lax.broadcasted_iota(jnp.int32, (size, chans), 0)
    order = order + jnp.where(order >= half, (lax.axis_index("filt") & 1) * (size - half), 0)
    block = lax.axis_index("space") ^ reversed_bits(order >> bits_of(rows), count)
    source = (block << bits_of(rows)) | (order & (rows - 1))
    picked[...] = (lax.broadcasted_iota(jnp.int32, (size, chans), 1) == source).astype(jnp.bfloat16)


def turn_kernel(picked, inputs, _, mine, part):
    half = mine.shape[0]
    turned = lax.dot_general(picked[...], inputs[...], (((1,), (1,)), ((), ())), preferred_element_type=jnp.float32)
    turned = turned.astype(jnp.bfloat16)
    mine[...] = turned[0:half, :]
    part[...] = turned[half:, :]


def grads_kernel(out_grad, pre_act, own):
    own[...] = (out_grad[...].astype(jnp.float32) * silu_grad(pre_act[...].astype(jnp.float32))).astype(own.dtype)


def order_kernel(weight, early, late):
    filt = weight.shape[1]
    odd = lax.axis_index("space") & 1
    for tap in range(9):
        b, c = divmod(tap, 3)
        low, high = pl.ds(2 * c * filt, filt), pl.ds((2 * c + 1) * filt, filt)
        early[b, low, :] = weight[9 + tap]
        early[b, high, :] = jnp.zeros(weight.shape[1:], jnp.bfloat16)
        late[b, low, :] = weight[18 * odd + tap]
        late[b, high, :] = weight[18 - 18 * odd + tap]


def early_kernel(width, own, mine, came, other, weight, turned, terms, spread, windows, tall):
    cells = own.shape[1]
    half = mine.shape[0]
    wide = windows.shape[1]
    first_core = lax.axis_index("filt") & 1 == 0
    turned[0:half, :] = mine[...]
    turned[half : half + half // 2, :] = jnp.where(first_core, came[...], other[...])
    turned[half + half // 2 :, :] = jnp.where(first_core, other[...], came[...])
    lay_windows(width, own[...], own[...], windows, tall)
    total = 0.0
    for b in range(3):
        window = windows[pl.ds((2 - b) * width, cells), :]
        terms[:, b * wide : (b + 1) * wide] = jnp.dot(turned[...], window, preferred_element_type=jnp.float32)
        total = total + jnp.dot(window, weight[b], preferred_element_type=jnp.float32)
    spread[...] = total


def spread_kernel(width, groups, near, one_off, weight, spread, windows, keep, send, tall):
    cells = spread.shape[0]
    lay_windows(width, near[...], one_off[...], windows, tall)
    part = cells // groups
    index = lax.axis_index("filt")
    count = bits_of(groups)
    for target in reversed(range(groups)):
        block = 0
        for bit in range(count):
            differs = (target >> (count - 1 - bit)) & 1
            block = block + (((index >> bit) & 1) ^ differs) * (1 << bit)
        start = pl.multiple_of(block * part, part)
        total = spread[pl.ds(start, part), :]
        for b in range(3):
            rows = pl.ds(pl.multiple_of(start + (2 - b) * width, width), part)
            total = total + jnp.dot(windows[rows, :], weight[b], preferred_element_type=jnp.float32)
        if target < groups // 2:
            keep[pl.ds(target * part, part), :] = total
        else:
            send[pl.ds((target - groups // 2) * part, part), :] = total.astype(jnp.bfloat16)


def two_kernel(width, turned, two_off, terms, windows, tall):
    half = turned.shape[0] // 2
    cells = turned.shape[1]
    wide = windows.shape[1]
    lay_windows(width, two_off[...], two_off[...], windows, tall)
    for b in range(3):
        window = windows[pl.ds((2 - b) * width, cells), :]
        terms[:, b * wide : (b + 1) * wide] = jnp.dot(
            turned[pl.ds(half, half), :], window, preferred_element_type=jnp.float32
        )


def late_kernel(width, turned, windows, two, early, keep, *sends):
    half = turned.shape[0] // 2
    cells = turned.shape[1]
    wide = windows.shape[1]
    lanes = wide // 3
    filt = lanes // 2
    left = lax.broadcasted_iota(jnp.int32, (half, lanes), 1) < filt
    part = half // (len(sends) + 1)

    def store(lo, hi, value):
        keep[:, lo:hi] = value[0:part, :]
        for number, send in enumerate(sends, 1):
            send[:, lo:hi] = value[number * part : (number + 1) * part, :].astype(jnp.bfloat16)

    for b in range(3):
        window = windows[pl.ds((2 - b) * width, cells), :]
        terms = jnp.dot(turned[...], window, preferred_element_type=jnp.float32)
        for c in range(3):
            tap = 3 * b + c
            cut = slice(c * lanes, (c + 1) * lanes)
            lo = b * wide + c * lanes
            crossed = jnp.where(left, two[:, lo : lo + lanes], early[half:, lo : lo + lanes])
            store(lo, lo + lanes, terms[0:half, cut] + crossed)
            middle = terms[half:, cut] + early[0:half, lo : lo + lanes]
            lo = 3 * wide + tap // 2 * lanes
            if tap == 8:
                store(lo, lo + filt, middle[:, 0:filt])
            elif tap % 2 == 0:
                before = middle
            else:
                store(lo, lo + lanes, jnp.where(left, before, pltpu.roll(middle, filt, 1)))


def halve_kernel(kept, came, keep, send):
    half = keep.shape[0]
    keep[...] = kept[0:half, :] + came[0:half, :].astype(jnp.float32)
    send[...] = (kept[half:, :] + came[half:, :].astype(jnp.float32)).astype(jnp.bfloat16)


def sum_kernel(scale, kept, *rest):
    *came, out = rest
    total = kept[...]
    for piece in came:
        total = total + piece[...].astype(jnp.float32)
    out[...] = total * scale


def last_kernel(filt, summed, kept, came, out, grad_input, taps, rows, done):
    odd = lax.axis_index("space") & 1
    rows[...] = (kept[...] + came[...].astype(jnp.float32)).astype(rows.dtype)
    copies = [pltpu.make_async_copy(rows, grad_input, done.at[3])]
    copies[0].start()
    total = summed[...]
    for group, (first, step, target) in enumerate(((18, 1, 1), (0, 2, 2 * odd), (1, 2, 2 - 2 * odd))):
        for tap in range(9):
            slot = first + step * tap
            taps[group, tap] = total[:, slot * filt : (slot + 1) * filt]
        copy = pltpu.make_async_copy(taps.at[group], out.at[pl.ds(target * 9, 9)], done.at[group])
        copy.start()
        copies.append(copy)
    for copy in copies:
        copy.wait()


def swapped(value, axis, distance):
    count = lax.axis_size(axis)
    return lax.ppermute(value, axis, [(i, i ^ distance) for i in range(count)])


def halved(kept, came):
    rows, lanes = kept.shape
    if rows // 2 % 16:
        total = kept + came.astype(jnp.float32)
        return total[: rows // 2], total[rows // 2 :].astype(jnp.bfloat16)
    outs = (
        jax.ShapeDtypeStruct((rows // 2, lanes), jnp.float32),
        jax.ShapeDtypeStruct((rows // 2, lanes), jnp.bfloat16),
    )
    return call(halve_kernel, outs, flops=rows * lanes, bytes_accessed=9 * rows * lanes)(
        in_specs=[VMEM] * 2, out_specs=[VMEM] * 2
    )(kept, came)


def after(value, other):
    return lax.optimization_barrier((value, other))[0]


def on_device(inputs, out_grad, pre_act, weight):
    _, height, width, chans = inputs.shape
    taps, filt, _ = weight.shape
    cells = height * width
    blocks, groups = lax.axis_size("space"), lax.axis_size("filt")
    half, quarter = chans // 2, chans // 4
    bf16, f32 = jnp.bfloat16, jnp.float32
    shape = jax.ShapeDtypeStruct
    flops = 2 * cells * taps * filt * chans
    lanes = 6 * filt
    windows_shape = shape((cells + 2 * width, lanes), bf16)
    tall = pltpu.VMEM((cells + 16, 2 * filt), f32)

    picked = call(
        functools.partial(pick_kernel, blocks), shape((half + quarter, chans), bf16), flops=PICK * flops
    )(in_specs=[], out_specs=VMEM)()
    own = call(grads_kernel, shape((filt, cells), bf16))(in_specs=[VMEM] * 2, out_specs=VMEM)(out_grad[0], pre_act[0])
    mine, part = call(
        turn_kernel,
        (shape((half, cells), bf16), shape((quarter, cells), bf16)),
        flops=TURN * flops,
    )(in_specs=[VMEM] * 3, out_specs=[VMEM] * 2)(picked, inputs.reshape(cells, chans), own)
    came = swapped(part, "space", 1)
    one_pairs = [(i, i + 1) for i in range(1, blocks - 1, 2)]
    one_off = lax.ppermute(own, "space", one_pairs + [(target, source) for source, target in one_pairs])
    later = after(own, mine)
    near = swapped(later, "space", 1)
    two_pairs = [(i, i - 2) for i in range(2, blocks, 2)] + [(i, i + 2) for i in range(1, blocks - 2, 2)]
    two_off = lax.ppermute(later, "space", two_pairs)
    other = swapped(came, "filt", 1)

    weight_shape = shape((3, lanes, chans), bf16)
    early_weight, late_weight = call(order_kernel, (weight_shape, weight_shape), flops=ORDER * flops, bytes_accessed=MIB)(
        in_specs=[VMEM], out_specs=[VMEM] * 2
    )(after(weight, mine))
    turned, early, spread = call(
        functools.partial(early_kernel, width),
        (shape((chans, cells), bf16), shape((chans, 3 * lanes), f32), shape((cells, chans), f32)),
        (pltpu.VMEM(windows_shape.shape, bf16), tall),
        flops=EARLY * flops,
        bytes_accessed=4 * MIB,
    )(in_specs=[VMEM] * 5, out_specs=[VMEM] * 3)(own, mine, came, other, early_weight)
    two = call(
        functools.partial(two_kernel, width),
        shape((half, 3 * lanes), f32),
        (pltpu.VMEM(windows_shape.shape, bf16), tall),
        flops=TWO * flops,
    )(in_specs=[VMEM] * 2, out_specs=VMEM)(turned, two_off)
    windows, kept_in, sent_in = call(
        functools.partial(spread_kernel, width, groups),
        (windows_shape, shape((cells // 2, chans), f32), shape((cells // 2, chans), bf16)),
        (tall,),
        flops=SPREAD * flops,
        bytes_accessed=4 * MIB,
    )(in_specs=[VMEM] * 4, out_specs=[VMEM] * 3)(near, one_off, late_weight, after(spread, two))
    came_in = swapped(sent_in, "filt", 1)
    radix = min(4, blocks // 2)
    piece = half // radix
    kept, *sends = call(
        functools.partial(late_kernel, width),
        (shape((piece, taps * filt), f32),) + (shape((piece, taps * filt), bf16),) * (radix - 1),
        flops=LATE * flops,
        bytes_accessed=4 * MIB,
    )(in_specs=[VMEM] * 4, out_specs=[VMEM] * radix)(turned, windows, two, early)
    came_in = after(came_in, kept)

    distance = 2
    while True:
        spans = {2: (1,), 4: (2, 1, 3)}[radix]
        arrived = [swapped(sends[n - 1], "space", spans[n - 1] * distance) for n in range(1, radix)]
        distance *= radix
        if distance >= blocks:
            break
        total = kept
        for value in arrived:
            total = total + value.astype(f32)
        radix = min(4, blocks // distance)
        piece //= radix
        kept, *sends = (total[n * piece : (n + 1) * piece] for n in range(radix))
        sends = [value.astype(bf16) for value in sends]

    distance_in = 2
    while distance_in < groups:
        kept_in, sent_in = halved(kept_in, came_in)
        came_in = swapped(sent_in, "filt", distance_in)
        distance_in *= 2
    grad_scale = float(cells * blocks) ** (-0.5)
    summed = call(
        functools.partial(sum_kernel, grad_scale), shape((chans // blocks, taps * filt), f32), flops=FINAL * flops
    )(in_specs=[VMEM] * (len(arrived) + 1), out_specs=VMEM)(kept, *arrived)
    any_space = pl.BlockSpec(memory_space=pl.ANY)
    rows_shape = (cells // groups, chans)
    grad_weight, grad_input = call(
        functools.partial(last_kernel, filt),
        (shape((taps, chans // blocks, filt), f32), shape(rows_shape, bf16)),
        (
            pltpu.VMEM((3, 9, chans // blocks, filt), f32),
            pltpu.VMEM(rows_shape, bf16),
            pltpu.SemaphoreType.DMA((4,)),
        ),
    )(in_specs=[VMEM] * 3, out_specs=[any_space] * 2)(summed, kept_in, came_in)
    return grad_input.reshape(1, height // groups, width, chans), jnp.transpose(grad_weight, (1, 0, 2))


def solution(mesh):
    placed = (
        P("space", None, None, None),
        P("space", "filt", None),
        P("space", "filt", None),
        P(None, "filt", None),
    )
    return jax.shard_map(
        on_device,
        mesh=mesh,
        in_specs=placed,
        out_specs=(P("space", "filt", None, None), P("space", None, "filt")),
        check_vma=False,
    )
```

```python
import functools

import jax
import jax.numpy as jnp
from jax import lax
from jax.experimental import pallas as pl
from jax.experimental.pallas import tpu as pltpu
from jax.sharding import PartitionSpec as P

MIB = 1 << 20
PICK, TURN, NEAR, THEIRS, ONE, FINAL, ORDER = 3, 1, 3, 3, 3, 3, 3
VMEM = pl.BlockSpec(memory_space=pltpu.VMEM)


def silu_grad(values):
    sig = jax.nn.sigmoid(values)
    return sig * (1.0 + values * (1.0 - sig))


def bits_of(count):
    return count.bit_length() - 1


def reversed_bits(value, width):
    return sum(((value >> bit) & 1) << (width - 1 - bit) for bit in range(width))


def call(kernel, outs, scratch=(), flops=0, bytes_accessed=0, limit=24):
    return functools.partial(
        pl.pallas_call,
        kernel,
        out_shape=outs,
        scratch_shapes=scratch,
        compiler_params=pltpu.CompilerParams(vmem_limit_bytes=limit * MIB),
        cost_estimate=pl.CostEstimate(flops=flops, bytes_accessed=bytes_accessed, transcendentals=0),
    )


def lay_windows(width, first, second, windows, tall):
    filt, cells = first.shape
    lanes = 2 * filt
    tall[pl.ds(8, cells), :] = jnp.concatenate([first, second], axis=0).astype(jnp.float32).T
    row = lax.broadcasted_iota(jnp.int32, (cells, lanes), 0)
    column = row & (width - 1) if width & (width - 1) == 0 else lax.rem(row, width)
    zero_rows = jnp.zeros((width, windows.shape[1]), jnp.bfloat16)
    windows[pl.ds(0, width), :] = zero_rows
    windows[pl.ds(width + cells, width), :] = zero_rows
    body = pl.ds(width, cells)
    windows[body, 0:lanes] = jnp.where(column != width - 1, tall[pl.ds(9, cells), :], 0.0).astype(jnp.bfloat16)
    windows[body, lanes : 2 * lanes] = tall[pl.ds(8, cells), :].astype(jnp.bfloat16)
    windows[body, 2 * lanes : 3 * lanes] = jnp.where(column != 0, tall[pl.ds(7, cells), :], 0.0).astype(jnp.bfloat16)


def pick_kernel(blocks, picked):
    size, chans = picked.shape
    rows = chans // blocks
    half = chans // 2
    count = bits_of(blocks)
    order = lax.broadcasted_iota(jnp.int32, (size, chans), 0)
    order = order + jnp.where(order >= half, (lax.axis_index("filt") & 1) * (size - half), 0)
    block = lax.axis_index("space") ^ reversed_bits(order >> bits_of(rows), count)
    source = (block << bits_of(rows)) | (order & (rows - 1))
    picked[...] = (lax.broadcasted_iota(jnp.int32, (size, chans), 1) == source).astype(jnp.bfloat16)


def turn_kernel(picked, inputs, _, mine, part):
    half = mine.shape[0]
    turned = lax.dot_general(picked[...], inputs[...], (((1,), (1,)), ((), ())), preferred_element_type=jnp.float32)
    turned = turned.astype(jnp.bfloat16)
    mine[...] = turned[0:half, :]
    part[...] = turned[half:, :]


def grads_kernel(out_grad, pre_act, own):
    own[...] = (out_grad[...].astype(jnp.float32) * silu_grad(pre_act[...].astype(jnp.float32))).astype(own.dtype)


def order_kernel(weight, paired, single):
    filt = weight.shape[1]
    odd = lax.axis_index("space") & 1
    for tap in range(9):
        b, c = divmod(tap, 3)
        low, high = pl.ds(2 * c * filt, filt), pl.ds((2 * c + 1) * filt, filt)
        paired[b, low, :] = weight[9 + tap]
        paired[b, high, :] = weight[18 * odd + tap]
        single[b, low, :] = weight[18 - 18 * odd + tap]
        single[b, high, :] = jnp.zeros(weight.shape[1:], jnp.bfloat16)


def near_kernel(width, own, near, mine, weight, windows, terms, spread, tall):
    cells = own.shape[1]
    wide = windows.shape[1]
    lay_windows(width, own[...], near[...], windows, tall)
    total = 0.0
    for b in range(3):
        window = windows[pl.ds((2 - b) * width, cells), :]
        terms[:, b * wide : (b + 1) * wide] = jnp.dot(mine[...], window, preferred_element_type=jnp.float32)
        total = total + jnp.dot(window, weight[b], preferred_element_type=jnp.float32)
    spread[...] = total


def theirs_kernel(width, came, other, two_off, windows, terms, inner, outer, theirs, twos, tall):
    part, cells = came.shape
    wide = windows.shape[1]
    lanes = wide // 3
    filt = lanes // 2
    first_core = lax.axis_index("filt") & 1 == 0
    theirs[0:part, :] = jnp.where(first_core, came[...], other[...])
    theirs[part:, :] = jnp.where(first_core, other[...], came[...])
    lay_windows(width, two_off[...], two_off[...], twos, tall)
    left = lax.broadcasted_iota(jnp.int32, (2 * part, lanes), 1) < filt
    for b in range(3):
        rows = pl.ds((2 - b) * width, cells)
        near_terms = jnp.dot(theirs[...], windows[rows, :], preferred_element_type=jnp.float32)
        two_terms = jnp.dot(theirs[...], twos[rows, :], preferred_element_type=jnp.float32)
        outer[:, b * wide : (b + 1) * wide] = near_terms
        for c in range(3):
            cut = slice(c * lanes, (c + 1) * lanes)
            lo = b * wide + c * lanes
            crossed = jnp.where(left, pltpu.roll(near_terms[:, cut], filt, 1), two_terms[:, cut])
            inner[:, lo : lo + lanes] = terms[:, lo : lo + lanes] + crossed


def one_kernel(width, groups, one_off, mine, weight, spread, inner, outer, kept_in, sent_in, keep, *rest):
    *sends, windows, tall = rest
    half, cells = mine.shape
    wide = windows.shape[1]
    lanes = wide // 3
    filt = lanes // 2
    lay_windows(width, one_off[...], one_off[...], windows, tall)

    size = cells // groups
    index = lax.axis_index("filt")
    count = bits_of(groups)
    for target in reversed(range(groups)):
        block = 0
        for bit in range(count):
            differs = (target >> (count - 1 - bit)) & 1
            block = block + (((index >> bit) & 1) ^ differs) * (1 << bit)
        start = pl.multiple_of(block * size, size)
        total = spread[pl.ds(start, size), :]
        for b in range(3):
            rows = pl.ds(pl.multiple_of(start + (2 - b) * width, width), size)
            total = total + jnp.dot(windows[rows, :], weight[b], preferred_element_type=jnp.float32)
        if target < groups // 2:
            kept_in[pl.ds(target * size, size), :] = total
        else:
            sent_in[pl.ds((target - groups // 2) * size, size), :] = total.astype(jnp.bfloat16)

    left = lax.broadcasted_iota(jnp.int32, (half, lanes), 1) < filt
    part = half // (len(sends) + 1)

    def store(lo, hi, value):
        keep[:, lo:hi] = value[0:part, :]
        for number, send in enumerate(sends, 1):
            send[:, lo:hi] = value[number * part : (number + 1) * part, :].astype(jnp.bfloat16)

    for b in range(3):
        store(b * wide, (b + 1) * wide, inner[:, b * wide : (b + 1) * wide])
        window = windows[pl.ds((2 - b) * width, cells), :]
        terms = jnp.dot(mine[...], window, preferred_element_type=jnp.float32)
        for c in range(3):
            tap = 3 * b + c
            lo = b * wide + c * lanes
            total = terms[:, c * lanes : (c + 1) * lanes] + outer[:, lo : lo + lanes]
            lo = 3 * wide + tap // 2 * lanes
            if tap == 8:
                store(lo, lo + filt, total[:, 0:filt])
            elif tap % 2 == 0:
                before = total
            else:
                store(lo, lo + lanes, jnp.where(left, before, pltpu.roll(total, filt, 1)))


def halve_kernel(kept, came, keep, send):
    half = keep.shape[0]
    keep[...] = kept[0:half, :] + came[0:half, :].astype(jnp.float32)
    send[...] = (kept[half:, :] + came[half:, :].astype(jnp.float32)).astype(jnp.bfloat16)


def sum_kernel(scale, kept, *rest):
    *came, out = rest
    total = kept[...]
    for piece in came:
        total = total + piece[...].astype(jnp.float32)
    out[...] = total * scale


def last_kernel(filt, summed, kept, came, out, grad_input, taps, rows, done):
    odd = lax.axis_index("space") & 1
    rows[...] = (kept[...] + came[...].astype(jnp.float32)).astype(rows.dtype)
    copies = [pltpu.make_async_copy(rows, grad_input, done.at[3])]
    copies[0].start()
    total = summed[...]
    for group, (first, step, target) in enumerate(((0, 2, 1), (1, 2, 2 * odd), (18, 1, 2 - 2 * odd))):
        for tap in range(9):
            slot = first + step * tap
            taps[group, tap] = total[:, slot * filt : (slot + 1) * filt]
        copy = pltpu.make_async_copy(taps.at[group], out.at[pl.ds(target * 9, 9)], done.at[group])
        copy.start()
        copies.append(copy)
    for copy in copies:
        copy.wait()


def swapped(value, axis, distance):
    count = lax.axis_size(axis)
    return lax.ppermute(value, axis, [(i, i ^ distance) for i in range(count)])


def halved(kept, came):
    rows, lanes = kept.shape
    if rows // 2 % 16:
        total = kept + came.astype(jnp.float32)
        return total[: rows // 2], total[rows // 2 :].astype(jnp.bfloat16)
    outs = (
        jax.ShapeDtypeStruct((rows // 2, lanes), jnp.float32),
        jax.ShapeDtypeStruct((rows // 2, lanes), jnp.bfloat16),
    )
    return call(halve_kernel, outs, flops=rows * lanes, bytes_accessed=9 * rows * lanes)(
        in_specs=[VMEM] * 2, out_specs=[VMEM] * 2
    )(kept, came)


def after(value, other):
    return lax.optimization_barrier((value, other))[0]


def on_device(inputs, out_grad, pre_act, weight):
    _, height, width, chans = inputs.shape
    taps, filt, _ = weight.shape
    cells = height * width
    blocks, groups = lax.axis_size("space"), lax.axis_size("filt")
    half, quarter = chans // 2, chans // 4
    bf16, f32 = jnp.bfloat16, jnp.float32
    shape = jax.ShapeDtypeStruct
    flops = 2 * cells * taps * filt * chans
    lanes = 6 * filt
    windows_shape = shape((cells + 2 * width, lanes), bf16)
    tall = pltpu.VMEM((cells + 16, 2 * filt), f32)

    picked = call(
        functools.partial(pick_kernel, blocks), shape((half + quarter, chans), bf16), flops=PICK * flops
    )(in_specs=[], out_specs=VMEM)()
    own = call(grads_kernel, shape((filt, cells), bf16))(in_specs=[VMEM] * 2, out_specs=VMEM)(out_grad[0], pre_act[0])
    mine, part = call(
        turn_kernel,
        (shape((half, cells), bf16), shape((quarter, cells), bf16)),
        flops=TURN * flops,
    )(in_specs=[VMEM] * 3, out_specs=[VMEM] * 2)(picked, inputs.reshape(cells, chans), own)
    near = swapped(own, "space", 1)
    came = swapped(part, "space", 1)
    up = [(i, i + 2) for i in range(blocks - 2)]
    down = [(target, source) for source, target in up]
    even, odd = slice(0, None, 2), slice(1, None, 2)
    two_off = lax.ppermute(after(own, mine), "space", down[even] + up[odd])
    one_off = lax.ppermute(near, "space", up[even] + down[odd])
    other = swapped(came, "filt", 1)

    weight_shape = shape((3, lanes, chans), bf16)
    paired_weight, single_weight = call(order_kernel, (weight_shape, weight_shape), flops=ORDER * flops, bytes_accessed=MIB)(
        in_specs=[VMEM], out_specs=[VMEM] * 2
    )(after(weight, mine))
    windows, terms, spread = call(
        functools.partial(near_kernel, width),
        (windows_shape, shape((half, 3 * lanes), f32), shape((cells, chans), f32)),
        (tall,),
        flops=NEAR * flops,
        bytes_accessed=4 * MIB,
    )(in_specs=[VMEM] * 4, out_specs=[VMEM] * 3)(own, near, mine, paired_weight)
    inner, outer = call(
        functools.partial(theirs_kernel, width),
        (shape((half, 3 * lanes), f32), shape((half, 3 * lanes), f32)),
        (pltpu.VMEM((half, cells), bf16), pltpu.VMEM(windows_shape.shape, bf16), tall),
        flops=THEIRS * flops,
        bytes_accessed=4 * MIB,
    )(in_specs=[VMEM] * 5, out_specs=[VMEM] * 2)(came, other, two_off, windows, terms)
    radix = min(4, blocks // 2)
    piece = half // radix
    kept_in, sent_in, kept, *sends = call(
        functools.partial(one_kernel, width, groups),
        (
            shape((cells // 2, chans), f32),
            shape((cells // 2, chans), bf16),
            shape((piece, taps * filt), f32),
        )
        + (shape((piece, taps * filt), bf16),) * (radix - 1),
        (pltpu.VMEM(windows_shape.shape, bf16), tall),
        flops=ONE * flops,
        bytes_accessed=4 * MIB,
    )(in_specs=[VMEM] * 6, out_specs=[VMEM] * (radix + 2))(one_off, mine, single_weight, spread, inner, outer)
    came_in = swapped(sent_in, "filt", 1)

    distance = 2
    while True:
        spans = {2: (1,), 4: (2, 1, 3)}[radix]
        arrived = [swapped(sends[n - 1], "space", spans[n - 1] * distance) for n in range(1, radix)]
        distance *= radix
        if distance >= blocks:
            break
        total = kept
        for value in arrived:
            total = total + value.astype(f32)
        radix = min(4, blocks // distance)
        piece //= radix
        kept, *sends = (total[n * piece : (n + 1) * piece] for n in range(radix))
        sends = [value.astype(bf16) for value in sends]

    distance_in = 2
    while distance_in < groups:
        kept_in, sent_in = halved(kept_in, came_in)
        came_in = swapped(sent_in, "filt", distance_in)
        distance_in *= 2
    grad_scale = float(cells * blocks) ** (-0.5)
    summed = call(
        functools.partial(sum_kernel, grad_scale), shape((chans // blocks, taps * filt), f32), flops=FINAL * flops
    )(in_specs=[VMEM] * (len(arrived) + 1), out_specs=VMEM)(kept, *arrived)
    any_space = pl.BlockSpec(memory_space=pl.ANY)
    rows_shape = (cells // groups, chans)
    grad_weight, grad_input = call(
        functools.partial(last_kernel, filt),
        (shape((taps, chans // blocks, filt), f32), shape(rows_shape, bf16)),
        (
            pltpu.VMEM((3, 9, chans // blocks, filt), f32),
            pltpu.VMEM(rows_shape, bf16),
            pltpu.SemaphoreType.DMA((4,)),
        ),
    )(in_specs=[VMEM] * 3, out_specs=[any_space] * 2)(summed, kept_in, came_in)
    return grad_input.reshape(1, height // groups, width, chans), jnp.transpose(grad_weight, (1, 0, 2))


def solution(mesh):
    placed = (
        P("space", None, None, None),
        P("space", "filt", None),
        P("space", "filt", None),
        P(None, "filt", None),
    )
    return jax.shard_map(
        on_device,
        mesh=mesh,
        in_specs=placed,
        out_specs=(P("space", "filt", None, None), P("space", None, "filt")),
        check_vma=False,
    )
```

```python
import functools

import jax
import jax.numpy as jnp
from jax import lax
from jax.experimental import pallas as pl
from jax.experimental.pallas import tpu as pltpu
from jax.sharding import PartitionSpec as P

MIB = 1 << 20
PICK, TURN, NEAR, THEIRS, ONE, FINAL, ORDER = 3, 1, 3, 3, 3, 3, 3
VMEM = pl.BlockSpec(memory_space=pltpu.VMEM)


def silu_grad(values):
    sig = jax.nn.sigmoid(values)
    return sig * (1.0 + values * (1.0 - sig))


def bits_of(count):
    return count.bit_length() - 1


def reversed_bits(value, width):
    return sum(((value >> bit) & 1) << (width - 1 - bit) for bit in range(width))


def call(kernel, outs, scratch=(), flops=0, bytes_accessed=0, limit=24):
    return functools.partial(
        pl.pallas_call,
        kernel,
        out_shape=outs,
        scratch_shapes=scratch,
        compiler_params=pltpu.CompilerParams(vmem_limit_bytes=limit * MIB),
        cost_estimate=pl.CostEstimate(flops=flops, bytes_accessed=bytes_accessed, transcendentals=0),
    )


def lay_windows(width, first, second, windows, tall):
    filt, cells = first.shape
    lanes = 2 * filt
    tall[pl.ds(8, cells), :] = jnp.concatenate([first, second], axis=0).astype(jnp.float32).T
    row = lax.broadcasted_iota(jnp.int32, (cells, lanes), 0)
    column = row & (width - 1) if width & (width - 1) == 0 else lax.rem(row, width)
    zero_rows = jnp.zeros((width, windows.shape[1]), jnp.bfloat16)
    windows[pl.ds(0, width), :] = zero_rows
    windows[pl.ds(width + cells, width), :] = zero_rows
    body = pl.ds(width, cells)
    windows[body, 0:lanes] = jnp.where(column != width - 1, tall[pl.ds(9, cells), :], 0.0).astype(jnp.bfloat16)
    windows[body, lanes : 2 * lanes] = tall[pl.ds(8, cells), :].astype(jnp.bfloat16)
    windows[body, 2 * lanes : 3 * lanes] = jnp.where(column != 0, tall[pl.ds(7, cells), :], 0.0).astype(jnp.bfloat16)


def pick_kernel(blocks, picked):
    size, chans = picked.shape
    rows = chans // blocks
    half = chans // 2
    count = bits_of(blocks)
    order = lax.broadcasted_iota(jnp.int32, (size, chans), 0)
    order = order + jnp.where(order >= half, (lax.axis_index("filt") & 1) * (size - half), 0)
    block = lax.axis_index("space") ^ reversed_bits(order >> bits_of(rows), count)
    source = (block << bits_of(rows)) | (order & (rows - 1))
    picked[...] = (lax.broadcasted_iota(jnp.int32, (size, chans), 1) == source).astype(jnp.bfloat16)


def turn_kernel(picked, inputs, _, mine, part):
    half = mine.shape[0]
    turned = lax.dot_general(picked[...], inputs[...], (((1,), (1,)), ((), ())), preferred_element_type=jnp.float32)
    turned = turned.astype(jnp.bfloat16)
    mine[...] = turned[0:half, :]
    part[...] = turned[half:, :]


def grads_kernel(_, out_grad, pre_act, own):
    own[...] = (out_grad[...].astype(jnp.float32) * silu_grad(pre_act[...].astype(jnp.float32))).astype(own.dtype)


def order_kernel(weight, paired, single):
    filt = weight.shape[1]
    odd = lax.axis_index("space") & 1
    for tap in range(9):
        b, c = divmod(tap, 3)
        low, high = pl.ds(2 * c * filt, filt), pl.ds((2 * c + 1) * filt, filt)
        paired[b, low, :] = weight[9 + tap]
        paired[b, high, :] = weight[18 * odd + tap]
        single[b, low, :] = weight[18 - 18 * odd + tap]
        single[b, high, :] = jnp.zeros(weight.shape[1:], jnp.bfloat16)


def near_kernel(width, own, near, mine, weight, windows, terms, spread, tall):
    cells = own.shape[1]
    wide = windows.shape[1]
    lay_windows(width, own[...], near[...], windows, tall)
    total = 0.0
    for b in range(3):
        window = windows[pl.ds((2 - b) * width, cells), :]
        terms[:, b * wide : (b + 1) * wide] = jnp.dot(mine[...], window, preferred_element_type=jnp.float32)
        total = total + jnp.dot(window, weight[b], preferred_element_type=jnp.float32)
    spread[...] = total


def theirs_kernel(width, came, other, two_off, windows, terms, inner, outer, theirs, twos, tall):
    part, cells = came.shape
    wide = windows.shape[1]
    lanes = wide // 3
    filt = lanes // 2
    first_core = lax.axis_index("filt") & 1 == 0
    theirs[0:part, :] = jnp.where(first_core, came[...], other[...])
    theirs[part:, :] = jnp.where(first_core, other[...], came[...])
    lay_windows(width, two_off[...], two_off[...], twos, tall)
    left = lax.broadcasted_iota(jnp.int32, (2 * part, lanes), 1) < filt
    for b in range(3):
        rows = pl.ds((2 - b) * width, cells)
        near_terms = jnp.dot(theirs[...], windows[rows, :], preferred_element_type=jnp.float32)
        two_terms = jnp.dot(theirs[...], twos[rows, :], preferred_element_type=jnp.float32)
        outer[:, b * wide : (b + 1) * wide] = near_terms
        for c in range(3):
            cut = slice(c * lanes, (c + 1) * lanes)
            lo = b * wide + c * lanes
            crossed = jnp.where(left, pltpu.roll(near_terms[:, cut], filt, 1), two_terms[:, cut])
            inner[:, lo : lo + lanes] = terms[:, lo : lo + lanes] + crossed


def one_kernel(width, groups, one_off, mine, weight, spread, inner, outer, kept_in, sent_in, keep, *rest):
    *sends, windows, tall = rest
    half, cells = mine.shape
    wide = windows.shape[1]
    lanes = wide // 3
    filt = lanes // 2
    lay_windows(width, one_off[...], one_off[...], windows, tall)

    size = cells // groups
    index = lax.axis_index("filt")
    count = bits_of(groups)
    for target in reversed(range(groups)):
        block = 0
        for bit in range(count):
            differs = (target >> (count - 1 - bit)) & 1
            block = block + (((index >> bit) & 1) ^ differs) * (1 << bit)
        start = pl.multiple_of(block * size, size)
        total = spread[pl.ds(start, size), :]
        for b in range(3):
            rows = pl.ds(pl.multiple_of(start + (2 - b) * width, width), size)
            total = total + jnp.dot(windows[rows, :], weight[b], preferred_element_type=jnp.float32)
        if target < groups // 2:
            kept_in[pl.ds(target * size, size), :] = total
        else:
            sent_in[pl.ds((target - groups // 2) * size, size), :] = total.astype(jnp.bfloat16)

    left = lax.broadcasted_iota(jnp.int32, (half, lanes), 1) < filt
    part = half // (len(sends) + 1)

    def store(lo, hi, value):
        keep[:, lo:hi] = value[0:part, :]
        for number, send in enumerate(sends, 1):
            send[:, lo:hi] = value[number * part : (number + 1) * part, :].astype(jnp.bfloat16)

    for b in range(3):
        store(b * wide, (b + 1) * wide, inner[:, b * wide : (b + 1) * wide])
        window = windows[pl.ds((2 - b) * width, cells), :]
        terms = jnp.dot(mine[...], window, preferred_element_type=jnp.float32)
        for c in range(3):
            tap = 3 * b + c
            lo = b * wide + c * lanes
            total = terms[:, c * lanes : (c + 1) * lanes] + outer[:, lo : lo + lanes]
            lo = 3 * wide + tap // 2 * lanes
            if tap == 8:
                store(lo, lo + filt, total[:, 0:filt])
            elif tap % 2 == 0:
                before = total
            else:
                store(lo, lo + lanes, jnp.where(left, before, pltpu.roll(total, filt, 1)))


def halve_kernel(kept, came, keep, send):
    half = keep.shape[0]
    keep[...] = kept[0:half, :] + came[0:half, :].astype(jnp.float32)
    send[...] = (kept[half:, :] + came[half:, :].astype(jnp.float32)).astype(jnp.bfloat16)


def sum_kernel(scale, kept, *rest):
    *came, out = rest
    total = kept[...]
    for piece in came:
        total = total + piece[...].astype(jnp.float32)
    out[...] = total * scale


def last_kernel(filt, summed, kept, came, out, grad_input, taps, rows, done):
    odd = lax.axis_index("space") & 1
    rows[...] = (kept[...] + came[...].astype(jnp.float32)).astype(rows.dtype)
    copies = [pltpu.make_async_copy(rows, grad_input, done.at[3])]
    copies[0].start()
    total = summed[...]
    for group, (first, step, target) in enumerate(((0, 2, 1), (1, 2, 2 * odd), (18, 1, 2 - 2 * odd))):
        for tap in range(9):
            slot = first + step * tap
            taps[group, tap] = total[:, slot * filt : (slot + 1) * filt]
        copy = pltpu.make_async_copy(taps.at[group], out.at[pl.ds(target * 9, 9)], done.at[group])
        copy.start()
        copies.append(copy)
    for copy in copies:
        copy.wait()


def swapped(value, axis, distance):
    count = lax.axis_size(axis)
    return lax.ppermute(value, axis, [(i, i ^ distance) for i in range(count)])


def halved(kept, came):
    rows, lanes = kept.shape
    if rows // 2 % 16:
        total = kept + came.astype(jnp.float32)
        return total[: rows // 2], total[rows // 2 :].astype(jnp.bfloat16)
    outs = (
        jax.ShapeDtypeStruct((rows // 2, lanes), jnp.float32),
        jax.ShapeDtypeStruct((rows // 2, lanes), jnp.bfloat16),
    )
    return call(halve_kernel, outs, flops=rows * lanes, bytes_accessed=9 * rows * lanes)(
        in_specs=[VMEM] * 2, out_specs=[VMEM] * 2
    )(kept, came)


def after(value, other):
    return lax.optimization_barrier((value, other))[0]


def on_device(inputs, out_grad, pre_act, weight):
    _, height, width, chans = inputs.shape
    taps, filt, _ = weight.shape
    cells = height * width
    blocks, groups = lax.axis_size("space"), lax.axis_size("filt")
    half, quarter = chans // 2, chans // 4
    bf16, f32 = jnp.bfloat16, jnp.float32
    shape = jax.ShapeDtypeStruct
    flops = 2 * cells * taps * filt * chans
    lanes = 6 * filt
    windows_shape = shape((cells + 2 * width, lanes), bf16)
    tall = pltpu.VMEM((cells + 16, 2 * filt), f32)

    picked = call(
        functools.partial(pick_kernel, blocks), shape((half + quarter, chans), bf16), flops=PICK * flops
    )(in_specs=[], out_specs=VMEM)()
    own = call(grads_kernel, shape((filt, cells), bf16))(in_specs=[VMEM] * 3, out_specs=VMEM)(
        picked, out_grad[0], pre_act[0]
    )
    mine, part = call(
        turn_kernel,
        (shape((half, cells), bf16), shape((quarter, cells), bf16)),
        flops=TURN * flops,
    )(in_specs=[VMEM] * 3, out_specs=[VMEM] * 2)(picked, inputs.reshape(cells, chans), own)
    near = swapped(own, "space", 1)
    came = swapped(part, "space", 1)
    up = [(i, i + 2) for i in range(blocks - 2)]
    down = [(target, source) for source, target in up]
    even, odd = slice(0, None, 2), slice(1, None, 2)
    two_off = lax.ppermute(after(own, mine), "space", down[even] + up[odd])
    one_off = lax.ppermute(near, "space", up[even] + down[odd])
    other = swapped(came, "filt", 1)

    weight_shape = shape((3, lanes, chans), bf16)
    paired_weight, single_weight = call(order_kernel, (weight_shape, weight_shape), flops=ORDER * flops, bytes_accessed=MIB)(
        in_specs=[VMEM], out_specs=[VMEM] * 2
    )(after(weight, mine))
    windows, terms, spread = call(
        functools.partial(near_kernel, width),
        (windows_shape, shape((half, 3 * lanes), f32), shape((cells, chans), f32)),
        (tall,),
        flops=NEAR * flops,
        bytes_accessed=4 * MIB,
    )(in_specs=[VMEM] * 4, out_specs=[VMEM] * 3)(own, near, mine, paired_weight)
    inner, outer = call(
        functools.partial(theirs_kernel, width),
        (shape((half, 3 * lanes), f32), shape((half, 3 * lanes), f32)),
        (pltpu.VMEM((half, cells), bf16), pltpu.VMEM(windows_shape.shape, bf16), tall),
        flops=THEIRS * flops,
        bytes_accessed=4 * MIB,
    )(in_specs=[VMEM] * 5, out_specs=[VMEM] * 2)(came, other, two_off, windows, terms)
    radix = min(4, blocks // 2)
    piece = half // radix
    kept_in, sent_in, kept, *sends = call(
        functools.partial(one_kernel, width, groups),
        (
            shape((cells // 2, chans), f32),
            shape((cells // 2, chans), bf16),
            shape((piece, taps * filt), f32),
        )
        + (shape((piece, taps * filt), bf16),) * (radix - 1),
        (pltpu.VMEM(windows_shape.shape, bf16), tall),
        flops=ONE * flops,
        bytes_accessed=4 * MIB,
    )(in_specs=[VMEM] * 6, out_specs=[VMEM] * (radix + 2))(one_off, mine, single_weight, spread, inner, outer)
    came_in = swapped(sent_in, "filt", 1)

    distance = 2
    while True:
        spans = {2: (1,), 4: (2, 1, 3)}[radix]
        arrived = [swapped(sends[n - 1], "space", spans[n - 1] * distance) for n in range(1, radix)]
        distance *= radix
        if distance >= blocks:
            break
        total = kept
        for value in arrived:
            total = total + value.astype(f32)
        radix = min(4, blocks // distance)
        piece //= radix
        kept, *sends = (total[n * piece : (n + 1) * piece] for n in range(radix))
        sends = [value.astype(bf16) for value in sends]

    distance_in = 2
    while distance_in < groups:
        kept_in, sent_in = halved(kept_in, came_in)
        came_in = swapped(sent_in, "filt", distance_in)
        distance_in *= 2
    grad_scale = float(cells * blocks) ** (-0.5)
    summed = call(
        functools.partial(sum_kernel, grad_scale), shape((chans // blocks, taps * filt), f32), flops=FINAL * flops
    )(in_specs=[VMEM] * (len(arrived) + 1), out_specs=VMEM)(kept, *arrived)
    any_space = pl.BlockSpec(memory_space=pl.ANY)
    rows_shape = (cells // groups, chans)
    grad_weight, grad_input = call(
        functools.partial(last_kernel, filt),
        (shape((taps, chans // blocks, filt), f32), shape(rows_shape, bf16)),
        (
            pltpu.VMEM((3, 9, chans // blocks, filt), f32),
            pltpu.VMEM(rows_shape, bf16),
            pltpu.SemaphoreType.DMA((4,)),
        ),
    )(in_specs=[VMEM] * 3, out_specs=[any_space] * 2)(summed, kept_in, came_in)
    return grad_input.reshape(1, height // groups, width, chans), jnp.transpose(grad_weight, (1, 0, 2))


def solution(mesh):
    placed = (
        P("space", None, None, None),
        P("space", "filt", None),
        P("space", "filt", None),
        P(None, "filt", None),
    )
    return jax.shard_map(
        on_device,
        mesh=mesh,
        in_specs=placed,
        out_specs=(P("space", "filt", None, None), P("space", None, "filt")),
        check_vma=False,
    )
```

```python
import functools

import jax
import jax.numpy as jnp
from jax import lax
from jax.experimental import pallas as pl
from jax.experimental.pallas import tpu as pltpu
from jax.sharding import PartitionSpec as P

MIB = 1 << 20
PICK, TURN, NEAR, THEIRS, ONE, FINAL, ORDER = 3, 1, 3, 3, 3, 3, 3
VMEM = pl.BlockSpec(memory_space=pltpu.VMEM)


def silu_grad(values):
    sig = jax.nn.sigmoid(values)
    return sig * (1.0 + values * (1.0 - sig))


def bits_of(count):
    return count.bit_length() - 1


def reversed_bits(value, width):
    return sum(((value >> bit) & 1) << (width - 1 - bit) for bit in range(width))


def call(kernel, outs, scratch=(), flops=0, bytes_accessed=0, limit=24, aliases={}):
    return functools.partial(
        pl.pallas_call,
        kernel,
        out_shape=outs,
        scratch_shapes=scratch,
        input_output_aliases=aliases,
        compiler_params=pltpu.CompilerParams(vmem_limit_bytes=limit * MIB),
        cost_estimate=pl.CostEstimate(flops=flops, bytes_accessed=bytes_accessed, transcendentals=0),
    )


def lay_windows(width, first, second, windows, tall):
    filt, cells = first.shape
    lanes = 2 * filt
    tall[pl.ds(8, cells), :] = jnp.concatenate([first, second], axis=0).astype(jnp.float32).T
    row = lax.broadcasted_iota(jnp.int32, (cells, lanes), 0)
    column = row & (width - 1) if width & (width - 1) == 0 else lax.rem(row, width)
    zero_rows = jnp.zeros((width, windows.shape[1]), jnp.bfloat16)
    windows[pl.ds(0, width), :] = zero_rows
    windows[pl.ds(width + cells, width), :] = zero_rows
    body = pl.ds(width, cells)
    windows[body, 0:lanes] = jnp.where(column != width - 1, tall[pl.ds(9, cells), :], 0.0).astype(jnp.bfloat16)
    windows[body, lanes : 2 * lanes] = tall[pl.ds(8, cells), :].astype(jnp.bfloat16)
    windows[body, 2 * lanes : 3 * lanes] = jnp.where(column != 0, tall[pl.ds(7, cells), :], 0.0).astype(jnp.bfloat16)


def lay_single(width, layer, windows, tall):
    filt, cells = layer.shape
    lanes = 2 * filt
    tall[pl.ds(8, cells), :] = jnp.concatenate([layer, layer], axis=0).astype(jnp.float32).T
    row = lax.broadcasted_iota(jnp.int32, (cells, lanes), 0)
    column = row & (width - 1) if width & (width - 1) == 0 else lax.rem(row, width)
    left = lax.broadcasted_iota(jnp.int32, (cells, lanes), 1) < filt
    zero_rows = jnp.zeros((width, windows.shape[1]), jnp.bfloat16)
    windows[pl.ds(0, width), :] = zero_rows
    windows[pl.ds(width + cells, width), :] = zero_rows
    body = pl.ds(width, cells)
    low = jnp.where(column != width - 1, tall[pl.ds(9, cells), :], 0.0)
    high = jnp.where(column != 0, tall[pl.ds(7, cells), :], 0.0)
    windows[body, 0:lanes] = jnp.where(left, low, high).astype(jnp.bfloat16)
    windows[body, lanes : lanes + filt] = tall[pl.ds(8, cells), 0:filt].astype(jnp.bfloat16)


def pick_kernel(blocks, picked):
    size, chans = picked.shape
    rows = chans // blocks
    half = chans // 2
    count = bits_of(blocks)
    order = lax.broadcasted_iota(jnp.int32, (size, chans), 0)
    order = order + jnp.where(order >= half, (lax.axis_index("filt") & 1) * (size - half), 0)
    block = lax.axis_index("space") ^ reversed_bits(order >> bits_of(rows), count)
    source = (block << bits_of(rows)) | (order & (rows - 1))
    picked[...] = (lax.broadcasted_iota(jnp.int32, (size, chans), 1) == source).astype(jnp.bfloat16)


def turn_kernel(picked, inputs, _, mine, part):
    half = mine.shape[0]
    turned = lax.dot_general(picked[...], inputs[...], (((1,), (1,)), ((), ())), preferred_element_type=jnp.float32)
    turned = turned.astype(jnp.bfloat16)
    mine[...] = turned[0:half, :]
    part[...] = turned[half:, :]


def grads_kernel(_, out_grad, pre_act, own):
    own[...] = (out_grad[...].astype(jnp.float32) * silu_grad(pre_act[...].astype(jnp.float32))).astype(own.dtype)


def order_kernel(weight, paired, single):
    filt = weight.shape[1]
    odd = lax.axis_index("space") & 1
    for tap in range(9):
        b, c = divmod(tap, 3)
        low, high = pl.ds(2 * c * filt, filt), pl.ds((2 * c + 1) * filt, filt)
        paired[b, low, :] = weight[9 + tap]
        paired[b, high, :] = weight[18 * odd + tap]
        single[b, pl.ds((0, 2, 1)[c] * filt, filt), :] = weight[18 - 18 * odd + tap]


def near_kernel(width, own, near, mine, weight, windows, terms, spread, tall):
    cells = own.shape[1]
    wide = windows.shape[1]
    lay_windows(width, own[...], near[...], windows, tall)
    total = 0.0
    for b in range(3):
        window = windows[pl.ds((2 - b) * width, cells), :]
        terms[:, b * wide : (b + 1) * wide] = jnp.dot(mine[...], window, preferred_element_type=jnp.float32)
        total = total + jnp.dot(window, weight[b], preferred_element_type=jnp.float32)
    spread[...] = total


def store_tile(value, tile, keep, sends):
    lanes = keep.shape[1]
    part = value.shape[0] // (len(sends) + 1)
    rows = pl.ds(tile * part, part if value.shape[1] == lanes else part // 2)
    for number, target in enumerate((keep, *sends)):
        piece = value[number * part : (number + 1) * part, :]
        if value.shape[1] < lanes:
            piece = jnp.concatenate([piece[0 : part // 2, :], piece[part // 2 :, :]], axis=1)
        target[rows, :] = piece.astype(target.dtype)


def theirs_kernel(width, came, other, two_off, windows, terms, outer, keep, *rest):
    *sends, theirs, twos, tall = rest
    part, cells = came.shape
    wide = windows.shape[1]
    lanes = wide // 3
    filt = lanes // 2
    first_core = lax.axis_index("filt") & 1 == 0
    theirs[0:part, :] = jnp.where(first_core, came[...], other[...])
    theirs[part:, :] = jnp.where(first_core, other[...], came[...])
    lay_windows(width, two_off[...], two_off[...], twos, tall)
    left = lax.broadcasted_iota(jnp.int32, (2 * part, lanes), 1) < filt
    middle = []
    for b in range(3):
        rows = pl.ds((2 - b) * width, cells)
        near_terms = jnp.dot(theirs[...], windows[rows, :], preferred_element_type=jnp.float32)
        two_terms = jnp.dot(theirs[...], twos[rows, :], preferred_element_type=jnp.float32)
        cuts = [slice(c * lanes, (c + 1) * lanes) for c in range(3)]
        for c, cut in enumerate(cuts):
            lo = b * wide + c * lanes
            crossed = jnp.where(left, pltpu.roll(near_terms[:, cut], filt, 1), two_terms[:, cut])
            store_tile(terms[:, lo : lo + lanes] + crossed, 3 * b + c, keep, sends)
        outer[:, b * lanes : (b + 1) * lanes] = jnp.where(
            left, near_terms[:, cuts[0]], pltpu.roll(near_terms[:, cuts[2]], filt, 1)
        )
        middle.append(near_terms[:, cuts[1]])
    outer[:, wide : wide + lanes] = jnp.where(left, middle[0], pltpu.roll(middle[1], filt, 1))
    outer[:, wide + lanes : wide + lanes + filt] = middle[2][:, 0:filt]


def one_kernel(width, groups, radix, one_off, mine, weight, spread, outer, *rest):
    kept_in, sent_in, keep, *rest = rest[radix:]
    *sends, windows, tall = rest
    cells = mine.shape[1]
    lanes = keep.shape[1]
    filt = lanes // 2
    lay_single(width, one_off[...], windows, tall)

    middle = []
    for b in range(3):
        window = windows[pl.ds((2 - b) * width, cells), :]
        terms = jnp.dot(mine[...], window, preferred_element_type=jnp.float32)
        store_tile(terms[:, 0:lanes] + outer[:, b * lanes : (b + 1) * lanes], 9 + b, keep, sends)
        middle.append(terms[:, lanes : lanes + filt])
    both = jnp.concatenate(middle[0:2], axis=1)
    store_tile(both + outer[:, 3 * lanes : 4 * lanes], 12, keep, sends)
    store_tile(middle[2] + outer[:, 4 * lanes : 4 * lanes + filt], 13, keep, sends)

    size = cells // groups
    index = lax.axis_index("filt")
    count = bits_of(groups)
    for target in reversed(range(groups)):
        block = 0
        for bit in range(count):
            differs = (target >> (count - 1 - bit)) & 1
            block = block + (((index >> bit) & 1) ^ differs) * (1 << bit)
        start = pl.multiple_of(block * size, size)
        total = spread[pl.ds(start, size), :]
        for b in range(3):
            rows = pl.ds(pl.multiple_of(start + (2 - b) * width, width), size)
            total = total + jnp.dot(windows[rows, :], weight[b], preferred_element_type=jnp.float32)
        if target < groups // 2:
            kept_in[pl.ds(target * size, size), :] = total
        else:
            sent_in[pl.ds((target - groups // 2) * size, size), :] = total.astype(jnp.bfloat16)


def unfolded(tiles, rows):
    full = tiles.shape[0] // rows
    whole = [tiles[n * rows : (n + 1) * rows] for n in range(full)]
    half = tiles[full * rows :]
    lanes = tiles.shape[1]
    return jnp.concatenate([*whole, jnp.concatenate([half[:, : lanes // 2], half[:, lanes // 2 :]], axis=0)], axis=1)


def halve_kernel(kept, came, keep, send):
    half = keep.shape[0]
    keep[...] = kept[0:half, :] + came[0:half, :].astype(jnp.float32)
    send[...] = (kept[half:, :] + came[half:, :].astype(jnp.float32)).astype(jnp.bfloat16)


def sum_kernel(scale, folded, kept, *rest):
    *came, out = rest
    total = kept[...]
    for piece in came:
        total = total + piece[...].astype(jnp.float32)
    total = total * scale
    if not folded:
        out[...] = total
        return
    rows, lanes = out.shape[0], total.shape[1]
    full = total.shape[0] // rows
    for tile in range(full):
        out[:, tile * lanes : (tile + 1) * lanes] = total[tile * rows : (tile + 1) * rows, :]
    out[0 : rows // 2, full * lanes :] = total[full * rows :, 0 : lanes // 2]
    out[rows // 2 :, full * lanes :] = total[full * rows :, lanes // 2 :]


def last_kernel(filt, summed, kept, came, out, grad_input, taps, rows, done):
    odd = lax.axis_index("space") & 1
    rows[...] = (kept[...] + came[...].astype(jnp.float32)).astype(rows.dtype)
    copies = [pltpu.make_async_copy(rows, grad_input, done.at[3])]
    copies[0].start()
    total = summed[...]
    outer = [18 + 2 * (tap // 3) + tap % 3 // 2 if tap % 3 != 1 else 24 + tap // 3 for tap in range(9)]
    for group, (slots, target) in enumerate(((range(0, 18, 2), 1), (range(1, 18, 2), 2 * odd), (outer, 2 - 2 * odd))):
        for tap, slot in enumerate(slots):
            taps[group, tap] = total[:, slot * filt : (slot + 1) * filt]
        copy = pltpu.make_async_copy(taps.at[group], out.at[pl.ds(target * 9, 9)], done.at[group])
        copy.start()
        copies.append(copy)
    for copy in copies:
        copy.wait()


def swapped(value, axis, distance):
    count = lax.axis_size(axis)
    return lax.ppermute(value, axis, [(i, i ^ distance) for i in range(count)])


def halved(kept, came):
    rows, lanes = kept.shape
    if rows // 2 % 16:
        total = kept + came.astype(jnp.float32)
        return total[: rows // 2], total[rows // 2 :].astype(jnp.bfloat16)
    outs = (
        jax.ShapeDtypeStruct((rows // 2, lanes), jnp.float32),
        jax.ShapeDtypeStruct((rows // 2, lanes), jnp.bfloat16),
    )
    return call(halve_kernel, outs, flops=rows * lanes, bytes_accessed=9 * rows * lanes)(
        in_specs=[VMEM] * 2, out_specs=[VMEM] * 2
    )(kept, came)


def after(value, other):
    return lax.optimization_barrier((value, other))[0]


def on_device(inputs, out_grad, pre_act, weight):
    _, height, width, chans = inputs.shape
    taps, filt, _ = weight.shape
    cells = height * width
    blocks, groups = lax.axis_size("space"), lax.axis_size("filt")
    half, quarter = chans // 2, chans // 4
    bf16, f32 = jnp.bfloat16, jnp.float32
    shape = jax.ShapeDtypeStruct
    flops = 2 * cells * taps * filt * chans
    lanes = 6 * filt
    windows_shape = shape((cells + 2 * width, lanes), bf16)
    tall = pltpu.VMEM((cells + 16, 2 * filt), f32)

    picked = call(
        functools.partial(pick_kernel, blocks), shape((half + quarter, chans), bf16), flops=PICK * flops
    )(in_specs=[], out_specs=VMEM)()
    own = call(grads_kernel, shape((filt, cells), bf16))(in_specs=[VMEM] * 3, out_specs=VMEM)(
        picked, out_grad[0], pre_act[0]
    )
    mine, part = call(
        turn_kernel,
        (shape((half, cells), bf16), shape((quarter, cells), bf16)),
        flops=TURN * flops,
    )(in_specs=[VMEM] * 3, out_specs=[VMEM] * 2)(picked, inputs.reshape(cells, chans), own)
    near = swapped(own, "space", 1)
    came = swapped(part, "space", 1)
    up = [(i, i + 2) for i in range(blocks - 2)]
    down = [(target, source) for source, target in up]
    even, odd = slice(0, None, 2), slice(1, None, 2)
    two_off = lax.ppermute(after(own, mine), "space", down[even] + up[odd])
    one_off = lax.ppermute(near, "space", up[even] + down[odd])
    other = swapped(came, "filt", 1)

    weight_shape = shape((3, lanes, chans), bf16)
    paired_weight, single_weight = call(
        order_kernel, (weight_shape, shape((3, 3 * filt, chans), bf16)), flops=ORDER * flops, bytes_accessed=MIB
    )(in_specs=[VMEM], out_specs=[VMEM] * 2)(after(weight, mine))
    windows, terms, spread = call(
        functools.partial(near_kernel, width),
        (windows_shape, shape((half, 3 * lanes), f32), shape((cells, chans), f32)),
        (tall,),
        flops=NEAR * flops,
        bytes_accessed=4 * MIB,
    )(in_specs=[VMEM] * 4, out_specs=[VMEM] * 3)(own, near, mine, paired_weight)
    radix = min(4, blocks // 2)
    piece = half // radix
    folded = (piece * taps // 2, 2 * filt)
    pieces = (shape(folded, f32),) + (shape(folded, bf16),) * (radix - 1)
    outer, *partial = call(
        functools.partial(theirs_kernel, width),
        (shape((half, 9 * filt), f32),) + pieces,
        (pltpu.VMEM((half, cells), bf16), pltpu.VMEM(windows_shape.shape, bf16), tall),
        flops=THEIRS * flops,
        bytes_accessed=4 * MIB,
    )(in_specs=[VMEM] * 5, out_specs=[VMEM] * (radix + 1))(came, other, two_off, windows, terms)
    kept_in, sent_in, kept, *sends = call(
        functools.partial(one_kernel, width, groups, radix),
        (shape((cells // 2, chans), f32), shape((cells // 2, chans), bf16)) + pieces,
        (pltpu.VMEM((cells + 2 * width, 3 * filt), bf16), tall),
        flops=ONE * flops,
        bytes_accessed=4 * MIB,
        aliases={5 + n: 2 + n for n in range(radix)},
    )(in_specs=[VMEM] * (5 + radix), out_specs=[VMEM] * (radix + 2))(
        one_off, mine, single_weight, spread, outer, *partial
    )
    came_in = swapped(sent_in, "filt", 1)

    distance = 2
    while True:
        spans = {2: (1,), 4: (2, 1, 3)}[radix]
        arrived = [swapped(sends[n - 1], "space", spans[n - 1] * distance) for n in range(1, radix)]
        distance *= radix
        if distance >= blocks:
            break
        total = kept
        for value in arrived:
            total = total + value.astype(f32)
        if total.shape == folded:
            total = unfolded(total, piece)
        radix = min(4, blocks // distance)
        piece //= radix
        kept, *sends = (total[n * piece : (n + 1) * piece] for n in range(radix))
        sends = [value.astype(bf16) for value in sends]

    distance_in = 2
    while distance_in < groups:
        kept_in, sent_in = halved(kept_in, came_in)
        came_in = swapped(sent_in, "filt", distance_in)
        distance_in *= 2
    grad_scale = float(cells * blocks) ** (-0.5)
    summed = call(
        functools.partial(sum_kernel, grad_scale, kept.shape == folded), shape((chans // blocks, taps * filt), f32), flops=FINAL * flops
    )(in_specs=[VMEM] * (len(arrived) + 1), out_specs=VMEM)(kept, *arrived)
    any_space = pl.BlockSpec(memory_space=pl.ANY)
    rows_shape = (cells // groups, chans)
    grad_weight, grad_input = call(
        functools.partial(last_kernel, filt),
        (shape((taps, chans // blocks, filt), f32), shape(rows_shape, bf16)),
        (
            pltpu.VMEM((3, 9, chans // blocks, filt), f32),
            pltpu.VMEM(rows_shape, bf16),
            pltpu.SemaphoreType.DMA((4,)),
        ),
    )(in_specs=[VMEM] * 3, out_specs=[any_space] * 2)(summed, kept_in, came_in)
    return grad_input.reshape(1, height // groups, width, chans), jnp.transpose(grad_weight, (1, 0, 2))


def solution(mesh):
    placed = (
        P("space", None, None, None),
        P("space", "filt", None),
        P("space", "filt", None),
        P(None, "filt", None),
    )
    return jax.shard_map(
        on_device,
        mesh=mesh,
        in_specs=placed,
        out_specs=(P("space", "filt", None, None), P("space", None, "filt")),
        check_vma=False,
    )
```

```python
import functools

import jax
import jax.numpy as jnp
from jax import lax
from jax.experimental import pallas as pl
from jax.experimental.pallas import tpu as pltpu
from jax.sharding import PartitionSpec as P

MIB = 1 << 20
AGAIN, PICK, TURN, NEAR, THEIRS, ONE, FINAL, ORDER = 0, 3, 1, 3, 3, 3, 3, 3
VMEM = pl.BlockSpec(memory_space=pltpu.VMEM)


def silu_grad(values):
    sig = jax.nn.sigmoid(values)
    return sig * (1.0 + values * (1.0 - sig))


def bits_of(count):
    return count.bit_length() - 1


def reversed_bits(value, width):
    return sum(((value >> bit) & 1) << (width - 1 - bit) for bit in range(width))


def call(kernel, outs, scratch=(), flops=0, bytes_accessed=0, limit=24, aliases={}):
    return functools.partial(
        pl.pallas_call,
        kernel,
        out_shape=outs,
        scratch_shapes=scratch,
        input_output_aliases=aliases,
        compiler_params=pltpu.CompilerParams(vmem_limit_bytes=limit * MIB),
        cost_estimate=pl.CostEstimate(flops=flops, bytes_accessed=bytes_accessed, transcendentals=0),
    )


def lay_windows(width, first, second, windows, tall):
    filt, cells = first.shape
    lanes = 2 * filt
    tall[pl.ds(8, cells), :] = jnp.concatenate([first, second], axis=0).astype(jnp.float32).T
    row = lax.broadcasted_iota(jnp.int32, (cells, lanes), 0)
    column = row & (width - 1) if width & (width - 1) == 0 else lax.rem(row, width)
    zero_rows = jnp.zeros((width, windows.shape[1]), jnp.bfloat16)
    windows[pl.ds(0, width), :] = zero_rows
    windows[pl.ds(width + cells, width), :] = zero_rows
    body = pl.ds(width, cells)
    windows[body, 0:lanes] = jnp.where(column != width - 1, tall[pl.ds(9, cells), :], 0.0).astype(jnp.bfloat16)
    windows[body, lanes : 2 * lanes] = tall[pl.ds(8, cells), :].astype(jnp.bfloat16)
    windows[body, 2 * lanes : 3 * lanes] = jnp.where(column != 0, tall[pl.ds(7, cells), :], 0.0).astype(jnp.bfloat16)


def lay_single(width, layer, windows, tall):
    filt, cells = layer.shape
    lanes = 2 * filt
    tall[pl.ds(8, cells), :] = jnp.concatenate([layer, layer], axis=0).astype(jnp.float32).T
    row = lax.broadcasted_iota(jnp.int32, (cells, lanes), 0)
    column = row & (width - 1) if width & (width - 1) == 0 else lax.rem(row, width)
    left = lax.broadcasted_iota(jnp.int32, (cells, lanes), 1) < filt
    zero_rows = jnp.zeros((width, windows.shape[1]), jnp.bfloat16)
    windows[pl.ds(0, width), :] = zero_rows
    windows[pl.ds(width + cells, width), :] = zero_rows
    body = pl.ds(width, cells)
    low = jnp.where(column != width - 1, tall[pl.ds(9, cells), :], 0.0)
    high = jnp.where(column != 0, tall[pl.ds(7, cells), :], 0.0)
    windows[body, 0:lanes] = jnp.where(left, low, high).astype(jnp.bfloat16)
    windows[body, lanes : lanes + filt] = tall[pl.ds(8, cells), 0:filt].astype(jnp.bfloat16)


def pick_kernel(blocks, picked):
    size, chans = picked.shape
    rows = chans // blocks
    half = chans // 2
    count = bits_of(blocks)
    order = lax.broadcasted_iota(jnp.int32, (size, chans), 0)
    order = order + jnp.where(order >= half, (lax.axis_index("filt") & 1) * (size - half), 0)
    block = lax.axis_index("space") ^ reversed_bits(order >> bits_of(rows), count)
    source = (block << bits_of(rows)) | (order & (rows - 1))
    picked[...] = (lax.broadcasted_iota(jnp.int32, (size, chans), 1) == source).astype(jnp.bfloat16)


def turn_kernel(picked, inputs, _, mine, part):
    half = mine.shape[0]
    turned = lax.dot_general(picked[...], inputs[...], (((1,), (1,)), ((), ())), preferred_element_type=jnp.float32)
    turned = turned.astype(jnp.bfloat16)
    mine[...] = turned[0:half, :]
    part[...] = turned[half:, :]


def grads_kernel(_, out_grad, pre_act, own):
    own[...] = (out_grad[...].astype(jnp.float32) * silu_grad(pre_act[...].astype(jnp.float32))).astype(own.dtype)


def again_kernel(own, out):
    out[...] = own[...]


def order_kernel(weight, paired, single):
    filt = weight.shape[1]
    odd = lax.axis_index("space") & 1
    for tap in range(9):
        b, c = divmod(tap, 3)
        low, high = pl.ds(2 * c * filt, filt), pl.ds((2 * c + 1) * filt, filt)
        paired[b, low, :] = weight[9 + tap]
        paired[b, high, :] = weight[18 * odd + tap]
        single[b, pl.ds((0, 2, 1)[c] * filt, filt), :] = weight[18 - 18 * odd + tap]


def near_kernel(width, own, near, mine, weight, windows, terms, spread, tall):
    cells = own.shape[1]
    wide = windows.shape[1]
    lay_windows(width, own[...], near[...], windows, tall)
    total = 0.0
    for b in range(3):
        window = windows[pl.ds((2 - b) * width, cells), :]
        terms[:, b * wide : (b + 1) * wide] = jnp.dot(mine[...], window, preferred_element_type=jnp.float32)
        total = total + jnp.dot(window, weight[b], preferred_element_type=jnp.float32)
    spread[...] = total


def store_tile(value, tile, keep, sends):
    lanes = keep.shape[1]
    part = value.shape[0] // (len(sends) + 1)
    rows = pl.ds(tile * part, part if value.shape[1] == lanes else part // 2)
    for number, target in enumerate((keep, *sends)):
        piece = value[number * part : (number + 1) * part, :]
        if value.shape[1] < lanes:
            piece = jnp.concatenate([piece[0 : part // 2, :], piece[part // 2 :, :]], axis=1)
        target[rows, :] = piece.astype(target.dtype)


def theirs_kernel(width, came, other, two_off, windows, terms, outer, keep, *rest):
    *sends, theirs, twos, tall = rest
    part, cells = came.shape
    wide = windows.shape[1]
    lanes = wide // 3
    filt = lanes // 2
    first_core = lax.axis_index("filt") & 1 == 0
    theirs[0:part, :] = jnp.where(first_core, came[...], other[...])
    theirs[part:, :] = jnp.where(first_core, other[...], came[...])
    lay_windows(width, two_off[...], two_off[...], twos, tall)
    left = lax.broadcasted_iota(jnp.int32, (2 * part, lanes), 1) < filt
    middle = []
    for b in range(3):
        rows = pl.ds((2 - b) * width, cells)
        near_terms = jnp.dot(theirs[...], windows[rows, :], preferred_element_type=jnp.float32)
        two_terms = jnp.dot(theirs[...], twos[rows, :], preferred_element_type=jnp.float32)
        cuts = [slice(c * lanes, (c + 1) * lanes) for c in range(3)]
        for c, cut in enumerate(cuts):
            lo = b * wide + c * lanes
            crossed = jnp.where(left, pltpu.roll(near_terms[:, cut], filt, 1), two_terms[:, cut])
            store_tile(terms[:, lo : lo + lanes] + crossed, 3 * b + c, keep, sends)
        outer[:, b * lanes : (b + 1) * lanes] = jnp.where(
            left, near_terms[:, cuts[0]], pltpu.roll(near_terms[:, cuts[2]], filt, 1)
        )
        middle.append(near_terms[:, cuts[1]])
    outer[:, wide : wide + lanes] = jnp.where(left, middle[0], pltpu.roll(middle[1], filt, 1))
    outer[:, wide + lanes : wide + lanes + filt] = middle[2][:, 0:filt]


def one_kernel(width, groups, radix, one_off, mine, weight, spread, outer, *rest):
    kept_in, sent_in, keep, *rest = rest[radix:]
    *sends, windows, tall = rest
    cells = mine.shape[1]
    lanes = keep.shape[1]
    filt = lanes // 2
    lay_single(width, one_off[...], windows, tall)

    middle = []
    for b in range(3):
        window = windows[pl.ds((2 - b) * width, cells), :]
        terms = jnp.dot(mine[...], window, preferred_element_type=jnp.float32)
        store_tile(terms[:, 0:lanes] + outer[:, b * lanes : (b + 1) * lanes], 9 + b, keep, sends)
        middle.append(terms[:, lanes : lanes + filt])
    both = jnp.concatenate(middle[0:2], axis=1)
    store_tile(both + outer[:, 3 * lanes : 4 * lanes], 12, keep, sends)
    store_tile(middle[2] + outer[:, 4 * lanes : 4 * lanes + filt], 13, keep, sends)

    size = cells // groups
    index = lax.axis_index("filt")
    count = bits_of(groups)
    for target in reversed(range(groups)):
        block = 0
        for bit in range(count):
            differs = (target >> (count - 1 - bit)) & 1
            block = block + (((index >> bit) & 1) ^ differs) * (1 << bit)
        start = pl.multiple_of(block * size, size)
        total = spread[pl.ds(start, size), :]
        for b in range(3):
            rows = pl.ds(pl.multiple_of(start + (2 - b) * width, width), size)
            total = total + jnp.dot(windows[rows, :], weight[b], preferred_element_type=jnp.float32)
        if target < groups // 2:
            kept_in[pl.ds(target * size, size), :] = total
        else:
            sent_in[pl.ds((target - groups // 2) * size, size), :] = total.astype(jnp.bfloat16)


def unfolded(tiles, rows):
    full = tiles.shape[0] // rows
    whole = [tiles[n * rows : (n + 1) * rows] for n in range(full)]
    half = tiles[full * rows :]
    lanes = tiles.shape[1]
    return jnp.concatenate([*whole, jnp.concatenate([half[:, : lanes // 2], half[:, lanes // 2 :]], axis=0)], axis=1)


def halve_kernel(kept, came, keep, send):
    half = keep.shape[0]
    keep[...] = kept[0:half, :] + came[0:half, :].astype(jnp.float32)
    send[...] = (kept[half:, :] + came[half:, :].astype(jnp.float32)).astype(jnp.bfloat16)


def sum_kernel(scale, folded, kept, *rest):
    *came, out = rest
    total = kept[...]
    for piece in came:
        total = total + piece[...].astype(jnp.float32)
    total = total * scale
    if not folded:
        out[...] = total
        return
    rows, lanes = out.shape[0], total.shape[1]
    full = total.shape[0] // rows
    for tile in range(full):
        out[:, tile * lanes : (tile + 1) * lanes] = total[tile * rows : (tile + 1) * rows, :]
    out[0 : rows // 2, full * lanes :] = total[full * rows :, 0 : lanes // 2]
    out[rows // 2 :, full * lanes :] = total[full * rows :, lanes // 2 :]


def last_kernel(filt, summed, kept, came, out, grad_input, taps, rows, done):
    odd = lax.axis_index("space") & 1
    rows[...] = (kept[...] + came[...].astype(jnp.float32)).astype(rows.dtype)
    copies = [pltpu.make_async_copy(rows, grad_input, done.at[3])]
    copies[0].start()
    total = summed[...]
    outer = [18 + 2 * (tap // 3) + tap % 3 // 2 if tap % 3 != 1 else 24 + tap // 3 for tap in range(9)]
    for group, (slots, target) in enumerate(((range(0, 18, 2), 1), (range(1, 18, 2), 2 * odd), (outer, 2 - 2 * odd))):
        for tap, slot in enumerate(slots):
            taps[group, tap] = total[:, slot * filt : (slot + 1) * filt]
        copy = pltpu.make_async_copy(taps.at[group], out.at[pl.ds(target * 9, 9)], done.at[group])
        copy.start()
        copies.append(copy)
    for copy in copies:
        copy.wait()


def swapped(value, axis, distance):
    count = lax.axis_size(axis)
    return lax.ppermute(value, axis, [(i, i ^ distance) for i in range(count)])


def halved(kept, came):
    rows, lanes = kept.shape
    if rows // 2 % 16:
        total = kept + came.astype(jnp.float32)
        return total[: rows // 2], total[rows // 2 :].astype(jnp.bfloat16)
    outs = (
        jax.ShapeDtypeStruct((rows // 2, lanes), jnp.float32),
        jax.ShapeDtypeStruct((rows // 2, lanes), jnp.bfloat16),
    )
    return call(halve_kernel, outs, flops=rows * lanes, bytes_accessed=9 * rows * lanes)(
        in_specs=[VMEM] * 2, out_specs=[VMEM] * 2
    )(kept, came)


def after(value, other):
    return lax.optimization_barrier((value, other))[0]


def on_device(inputs, out_grad, pre_act, weight):
    _, height, width, chans = inputs.shape
    taps, filt, _ = weight.shape
    cells = height * width
    blocks, groups = lax.axis_size("space"), lax.axis_size("filt")
    half, quarter = chans // 2, chans // 4
    bf16, f32 = jnp.bfloat16, jnp.float32
    shape = jax.ShapeDtypeStruct
    flops = 2 * cells * taps * filt * chans
    lanes = 6 * filt
    windows_shape = shape((cells + 2 * width, lanes), bf16)
    tall = pltpu.VMEM((cells + 16, 2 * filt), f32)

    picked = call(
        functools.partial(pick_kernel, blocks), shape((half + quarter, chans), bf16), flops=PICK * flops
    )(in_specs=[], out_specs=VMEM)()
    own = call(grads_kernel, shape((filt, cells), bf16))(in_specs=[VMEM] * 3, out_specs=VMEM)(
        picked, out_grad[0], pre_act[0]
    )
    own_again = call(again_kernel, shape((filt, cells), bf16), flops=AGAIN * flops)(in_specs=[VMEM], out_specs=VMEM)(own)
    mine, part = call(
        turn_kernel,
        (shape((half, cells), bf16), shape((quarter, cells), bf16)),
        flops=TURN * flops,
    )(in_specs=[VMEM] * 3, out_specs=[VMEM] * 2)(picked, inputs.reshape(cells, chans), own_again)
    near = swapped(own, "space", 1)
    came = swapped(part, "space", 1)
    up = [(i, i + 2) for i in range(blocks - 2)]
    down = [(target, source) for source, target in up]
    even, odd = slice(0, None, 2), slice(1, None, 2)
    two_off = lax.ppermute(own_again, "space", down[even] + up[odd])
    one_off = lax.ppermute(near, "space", up[even] + down[odd])
    other = swapped(came, "filt", 1)

    weight_shape = shape((3, lanes, chans), bf16)
    paired_weight, single_weight = call(
        order_kernel, (weight_shape, shape((3, 3 * filt, chans), bf16)), flops=ORDER * flops, bytes_accessed=MIB
    )(in_specs=[VMEM], out_specs=[VMEM] * 2)(after(weight, mine))
    windows, terms, spread = call(
        functools.partial(near_kernel, width),
        (windows_shape, shape((half, 3 * lanes), f32), shape((cells, chans), f32)),
        (tall,),
        flops=NEAR * flops,
        bytes_accessed=4 * MIB,
    )(in_specs=[VMEM] * 4, out_specs=[VMEM] * 3)(own, near, mine, paired_weight)
    radix = min(4, blocks // 2)
    piece = half // radix
    folded = (piece * taps // 2, 2 * filt)
    pieces = (shape(folded, f32),) + (shape(folded, bf16),) * (radix - 1)
    outer, *partial = call(
        functools.partial(theirs_kernel, width),
        (shape((half, 9 * filt), f32),) + pieces,
        (pltpu.VMEM((half, cells), bf16), pltpu.VMEM(windows_shape.shape, bf16), tall),
        flops=THEIRS * flops,
        bytes_accessed=4 * MIB,
    )(in_specs=[VMEM] * 5, out_specs=[VMEM] * (radix + 1))(came, other, two_off, windows, terms)
    kept_in, sent_in, kept, *sends = call(
        functools.partial(one_kernel, width, groups, radix),
        (shape((cells // 2, chans), f32), shape((cells // 2, chans), bf16)) + pieces,
        (pltpu.VMEM((cells + 2 * width, 3 * filt), bf16), tall),
        flops=ONE * flops,
        bytes_accessed=4 * MIB,
        aliases={5 + n: 2 + n for n in range(radix)},
    )(in_specs=[VMEM] * (5 + radix), out_specs=[VMEM] * (radix + 2))(
        one_off, mine, single_weight, spread, outer, *partial
    )
    came_in = swapped(sent_in, "filt", 1)

    distance = 2
    while True:
        spans = {2: (1,), 4: (2, 1, 3)}[radix]
        arrived = [swapped(sends[n - 1], "space", spans[n - 1] * distance) for n in range(1, radix)]
        distance *= radix
        if distance >= blocks:
            break
        total = kept
        for value in arrived:
            total = total + value.astype(f32)
        if total.shape == folded:
            total = unfolded(total, piece)
        radix = min(4, blocks // distance)
        piece //= radix
        kept, *sends = (total[n * piece : (n + 1) * piece] for n in range(radix))
        sends = [value.astype(bf16) for value in sends]

    distance_in = 2
    while distance_in < groups:
        kept_in, sent_in = halved(kept_in, came_in)
        came_in = swapped(sent_in, "filt", distance_in)
        distance_in *= 2
    grad_scale = float(cells * blocks) ** (-0.5)
    summed = call(
        functools.partial(sum_kernel, grad_scale, kept.shape == folded), shape((chans // blocks, taps * filt), f32), flops=FINAL * flops
    )(in_specs=[VMEM] * (len(arrived) + 1), out_specs=VMEM)(kept, *arrived)
    any_space = pl.BlockSpec(memory_space=pl.ANY)
    rows_shape = (cells // groups, chans)
    grad_weight, grad_input = call(
        functools.partial(last_kernel, filt),
        (shape((taps, chans // blocks, filt), f32), shape(rows_shape, bf16)),
        (
            pltpu.VMEM((3, 9, chans // blocks, filt), f32),
            pltpu.VMEM(rows_shape, bf16),
            pltpu.SemaphoreType.DMA((4,)),
        ),
    )(in_specs=[VMEM] * 3, out_specs=[any_space] * 2)(summed, kept_in, came_in)
    return grad_input.reshape(1, height // groups, width, chans), jnp.transpose(grad_weight, (1, 0, 2))


def solution(mesh):
    placed = (
        P("space", None, None, None),
        P("space", "filt", None),
        P("space", "filt", None),
        P(None, "filt", None),
    )
    return jax.shard_map(
        on_device,
        mesh=mesh,
        in_specs=placed,
        out_specs=(P("space", "filt", None, None), P("space", None, "filt")),
        check_vma=False,
    )
```

```python
import functools

import jax
import jax.numpy as jnp
from jax import lax
from jax.experimental import pallas as pl
from jax.experimental.pallas import tpu as pltpu
from jax.sharding import PartitionSpec as P

MIB = 1 << 20
PICK, TURN, NEAR, THEIRS, ONE, FINAL, ORDER = 3, 1, 3, 3, 3, 3, 1
VMEM = pl.BlockSpec(memory_space=pltpu.VMEM)


def silu_grad(values):
    sig = jax.nn.sigmoid(values)
    return sig * (1.0 + values * (1.0 - sig))


def bits_of(count):
    return count.bit_length() - 1


def reversed_bits(value, width):
    return sum(((value >> bit) & 1) << (width - 1 - bit) for bit in range(width))


def call(kernel, outs, scratch=(), flops=0, bytes_accessed=0, limit=24, aliases={}):
    return functools.partial(
        pl.pallas_call,
        kernel,
        out_shape=outs,
        scratch_shapes=scratch,
        input_output_aliases=aliases,
        compiler_params=pltpu.CompilerParams(vmem_limit_bytes=limit * MIB),
        cost_estimate=pl.CostEstimate(flops=flops, bytes_accessed=bytes_accessed, transcendentals=0),
    )


def lay_windows(width, first, second, windows, tall):
    filt, cells = first.shape
    lanes = 2 * filt
    tall[pl.ds(8, cells), :] = jnp.concatenate([first, second], axis=0).astype(jnp.float32).T
    row = lax.broadcasted_iota(jnp.int32, (cells, lanes), 0)
    column = row & (width - 1) if width & (width - 1) == 0 else lax.rem(row, width)
    zero_rows = jnp.zeros((width, windows.shape[1]), jnp.bfloat16)
    windows[pl.ds(0, width), :] = zero_rows
    windows[pl.ds(width + cells, width), :] = zero_rows
    body = pl.ds(width, cells)
    windows[body, 0:lanes] = jnp.where(column != width - 1, tall[pl.ds(9, cells), :], 0.0).astype(jnp.bfloat16)
    windows[body, lanes : 2 * lanes] = tall[pl.ds(8, cells), :].astype(jnp.bfloat16)
    windows[body, 2 * lanes : 3 * lanes] = jnp.where(column != 0, tall[pl.ds(7, cells), :], 0.0).astype(jnp.bfloat16)


def lay_single(width, layer, windows, tall):
    filt, cells = layer.shape
    lanes = 2 * filt
    tall[pl.ds(8, cells), :] = jnp.concatenate([layer, layer], axis=0).astype(jnp.float32).T
    row = lax.broadcasted_iota(jnp.int32, (cells, lanes), 0)
    column = row & (width - 1) if width & (width - 1) == 0 else lax.rem(row, width)
    left = lax.broadcasted_iota(jnp.int32, (cells, lanes), 1) < filt
    zero_rows = jnp.zeros((width, windows.shape[1]), jnp.bfloat16)
    windows[pl.ds(0, width), :] = zero_rows
    windows[pl.ds(width + cells, width), :] = zero_rows
    body = pl.ds(width, cells)
    low = jnp.where(column != width - 1, tall[pl.ds(9, cells), :], 0.0)
    high = jnp.where(column != 0, tall[pl.ds(7, cells), :], 0.0)
    windows[body, 0:lanes] = jnp.where(left, low, high).astype(jnp.bfloat16)
    windows[body, lanes : lanes + filt] = tall[pl.ds(8, cells), 0:filt].astype(jnp.bfloat16)


def pick_kernel(blocks, picked):
    size, chans = picked.shape
    rows = chans // blocks
    half = chans // 2
    count = bits_of(blocks)
    order = lax.broadcasted_iota(jnp.int32, (size, chans), 0)
    order = order + jnp.where(order >= half, (lax.axis_index("filt") & 1) * (size - half), 0)
    block = lax.axis_index("space") ^ reversed_bits(order >> bits_of(rows), count)
    source = (block << bits_of(rows)) | (order & (rows - 1))
    picked[...] = (lax.broadcasted_iota(jnp.int32, (size, chans), 1) == source).astype(jnp.bfloat16)


def turn_kernel(picked, inputs, _, mine, part):
    half = mine.shape[0]
    turned = lax.dot_general(picked[...], inputs[...], (((1,), (1,)), ((), ())), preferred_element_type=jnp.float32)
    turned = turned.astype(jnp.bfloat16)
    mine[...] = turned[0:half, :]
    part[...] = turned[half:, :]


def grads_kernel(_, out_grad, pre_act, own):
    own[...] = (out_grad[...].astype(jnp.float32) * silu_grad(pre_act[...].astype(jnp.float32))).astype(own.dtype)


def order_kernel(weight, paired, single):
    filt = weight.shape[1]
    odd = lax.axis_index("space") & 1
    for tap in range(9):
        b, c = divmod(tap, 3)
        low, high = pl.ds(2 * c * filt, filt), pl.ds((2 * c + 1) * filt, filt)
        paired[b, low, :] = weight[9 + tap]
        paired[b, high, :] = weight[18 * odd + tap]
        single[b, pl.ds((0, 2, 1)[c] * filt, filt), :] = weight[18 - 18 * odd + tap]


def near_kernel(width, own, near, mine, weight, windows, terms, spread, tall):
    cells = own.shape[1]
    wide = windows.shape[1]
    lay_windows(width, own[...], near[...], windows, tall)
    total = 0.0
    for b in range(3):
        window = windows[pl.ds((2 - b) * width, cells), :]
        terms[:, b * wide : (b + 1) * wide] = jnp.dot(mine[...], window, preferred_element_type=jnp.float32)
        total = total + jnp.dot(window, weight[b], preferred_element_type=jnp.float32)
    spread[...] = total


def store_tile(value, tile, keep, sends):
    lanes = keep.shape[1]
    part = value.shape[0] // (len(sends) + 1)
    rows = pl.ds(tile * part, part if value.shape[1] == lanes else part // 2)
    for number, target in enumerate((keep, *sends)):
        piece = value[number * part : (number + 1) * part, :]
        if value.shape[1] < lanes:
            piece = jnp.concatenate([piece[0 : part // 2, :], piece[part // 2 :, :]], axis=1)
        target[rows, :] = piece.astype(target.dtype)


def theirs_kernel(width, came, other, two_off, windows, terms, outer, keep, *rest):
    *sends, theirs, twos, tall = rest
    part, cells = came.shape
    wide = windows.shape[1]
    lanes = wide // 3
    filt = lanes // 2
    first_core = lax.axis_index("filt") & 1 == 0
    theirs[0:part, :] = jnp.where(first_core, came[...], other[...])
    theirs[part:, :] = jnp.where(first_core, other[...], came[...])
    lay_windows(width, two_off[...], two_off[...], twos, tall)
    left = lax.broadcasted_iota(jnp.int32, (2 * part, lanes), 1) < filt
    middle = []
    for b in range(3):
        rows = pl.ds((2 - b) * width, cells)
        near_terms = jnp.dot(theirs[...], windows[rows, :], preferred_element_type=jnp.float32)
        two_terms = jnp.dot(theirs[...], twos[rows, :], preferred_element_type=jnp.float32)
        cuts = [slice(c * lanes, (c + 1) * lanes) for c in range(3)]
        for c, cut in enumerate(cuts):
            lo = b * wide + c * lanes
            crossed = jnp.where(left, pltpu.roll(near_terms[:, cut], filt, 1), two_terms[:, cut])
            store_tile(terms[:, lo : lo + lanes] + crossed, 3 * b + c, keep, sends)
        outer[:, b * lanes : (b + 1) * lanes] = jnp.where(
            left, near_terms[:, cuts[0]], pltpu.roll(near_terms[:, cuts[2]], filt, 1)
        )
        middle.append(near_terms[:, cuts[1]])
    outer[:, wide : wide + lanes] = jnp.where(left, middle[0], pltpu.roll(middle[1], filt, 1))
    outer[:, wide + lanes : wide + lanes + filt] = middle[2][:, 0:filt]


def one_kernel(width, groups, radix, one_off, mine, weight, spread, outer, *rest):
    kept_in, sent_in, keep, *rest = rest[radix:]
    *sends, windows, tall = rest
    cells = mine.shape[1]
    lanes = keep.shape[1]
    filt = lanes // 2
    lay_single(width, one_off[...], windows, tall)

    middle = []
    for b in range(3):
        window = windows[pl.ds((2 - b) * width, cells), :]
        terms = jnp.dot(mine[...], window, preferred_element_type=jnp.float32)
        store_tile(terms[:, 0:lanes] + outer[:, b * lanes : (b + 1) * lanes], 9 + b, keep, sends)
        middle.append(terms[:, lanes : lanes + filt])
    both = jnp.concatenate(middle[0:2], axis=1)
    store_tile(both + outer[:, 3 * lanes : 4 * lanes], 12, keep, sends)
    store_tile(middle[2] + outer[:, 4 * lanes : 4 * lanes + filt], 13, keep, sends)

    size = cells // groups
    index = lax.axis_index("filt")
    count = bits_of(groups)
    for target in reversed(range(groups)):
        block = 0
        for bit in range(count):
            differs = (target >> (count - 1 - bit)) & 1
            block = block + (((index >> bit) & 1) ^ differs) * (1 << bit)
        start = pl.multiple_of(block * size, size)
        total = spread[pl.ds(start, size), :]
        for b in range(3):
            rows = pl.ds(pl.multiple_of(start + (2 - b) * width, width), size)
            total = total + jnp.dot(windows[rows, :], weight[b], preferred_element_type=jnp.float32)
        if target < groups // 2:
            kept_in[pl.ds(target * size, size), :] = total
        else:
            sent_in[pl.ds((target - groups // 2) * size, size), :] = total.astype(jnp.bfloat16)


def unfolded(tiles, rows):
    full = tiles.shape[0] // rows
    whole = [tiles[n * rows : (n + 1) * rows] for n in range(full)]
    half = tiles[full * rows :]
    lanes = tiles.shape[1]
    return jnp.concatenate([*whole, jnp.concatenate([half[:, : lanes // 2], half[:, lanes // 2 :]], axis=0)], axis=1)


def halve_kernel(kept, came, keep, send):
    half = keep.shape[0]
    keep[...] = kept[0:half, :] + came[0:half, :].astype(jnp.float32)
    send[...] = (kept[half:, :] + came[half:, :].astype(jnp.float32)).astype(jnp.bfloat16)


def sum_kernel(scale, folded, kept, *rest):
    *came, out = rest
    total = kept[...]
    for piece in came:
        total = total + piece[...].astype(jnp.float32)
    total = total * scale
    if not folded:
        out[...] = total
        return
    rows, lanes = out.shape[0], total.shape[1]
    full = total.shape[0] // rows
    for tile in range(full):
        out[:, tile * lanes : (tile + 1) * lanes] = total[tile * rows : (tile + 1) * rows, :]
    out[0 : rows // 2, full * lanes :] = total[full * rows :, 0 : lanes // 2]
    out[rows // 2 :, full * lanes :] = total[full * rows :, lanes // 2 :]


def last_kernel(filt, summed, kept, came, out, grad_input, taps, rows, done):
    odd = lax.axis_index("space") & 1
    rows[...] = (kept[...] + came[...].astype(jnp.float32)).astype(rows.dtype)
    copies = [pltpu.make_async_copy(rows, grad_input, done.at[3])]
    copies[0].start()
    total = summed[...]
    outer = [18 + 2 * (tap // 3) + tap % 3 // 2 if tap % 3 != 1 else 24 + tap // 3 for tap in range(9)]
    for group, (slots, target) in enumerate(((range(0, 18, 2), 1), (range(1, 18, 2), 2 * odd), (outer, 2 - 2 * odd))):
        for tap, slot in enumerate(slots):
            taps[group, tap] = total[:, slot * filt : (slot + 1) * filt]
        copy = pltpu.make_async_copy(taps.at[group], out.at[pl.ds(target * 9, 9)], done.at[group])
        copy.start()
        copies.append(copy)
    for copy in copies:
        copy.wait()


def swapped(value, axis, distance):
    count = lax.axis_size(axis)
    return lax.ppermute(value, axis, [(i, i ^ distance) for i in range(count)])


def halved(kept, came):
    rows, lanes = kept.shape
    if rows // 2 % 16:
        total = kept + came.astype(jnp.float32)
        return total[: rows // 2], total[rows // 2 :].astype(jnp.bfloat16)
    outs = (
        jax.ShapeDtypeStruct((rows // 2, lanes), jnp.float32),
        jax.ShapeDtypeStruct((rows // 2, lanes), jnp.bfloat16),
    )
    return call(halve_kernel, outs, flops=rows * lanes, bytes_accessed=9 * rows * lanes)(
        in_specs=[VMEM] * 2, out_specs=[VMEM] * 2
    )(kept, came)


def after(value, other):
    return lax.optimization_barrier((value, other))[0]


def on_device(inputs, out_grad, pre_act, weight):
    _, height, width, chans = inputs.shape
    taps, filt, _ = weight.shape
    cells = height * width
    blocks, groups = lax.axis_size("space"), lax.axis_size("filt")
    half, quarter = chans // 2, chans // 4
    bf16, f32 = jnp.bfloat16, jnp.float32
    shape = jax.ShapeDtypeStruct
    flops = 2 * cells * taps * filt * chans
    lanes = 6 * filt
    windows_shape = shape((cells + 2 * width, lanes), bf16)
    tall = pltpu.VMEM((cells + 16, 2 * filt), f32)

    picked = call(
        functools.partial(pick_kernel, blocks), shape((half + quarter, chans), bf16), flops=PICK * flops
    )(in_specs=[], out_specs=VMEM)()
    own = call(grads_kernel, shape((filt, cells), bf16))(in_specs=[VMEM] * 3, out_specs=VMEM)(
        picked, out_grad[0], pre_act[0]
    )
    mine, part = call(
        turn_kernel,
        (shape((half, cells), bf16), shape((quarter, cells), bf16)),
        flops=TURN * flops,
    )(in_specs=[VMEM] * 3, out_specs=[VMEM] * 2)(picked, inputs.reshape(cells, chans), own)
    near = swapped(own, "space", 1)
    came = swapped(part, "space", 1)
    up = [(i, i + 2) for i in range(blocks - 2)]
    down = [(target, source) for source, target in up]
    even, odd = slice(0, None, 2), slice(1, None, 2)
    two_off = lax.ppermute(after(own, mine), "space", down[even] + up[odd])
    one_off = lax.ppermute(near, "space", up[even] + down[odd])
    other = swapped(came, "filt", 1)

    weight_shape = shape((3, lanes, chans), bf16)
    paired_weight, single_weight = call(
        order_kernel, (weight_shape, shape((3, 3 * filt, chans), bf16)), flops=ORDER * flops, bytes_accessed=MIB
    )(in_specs=[VMEM], out_specs=[VMEM] * 2)(after(weight, mine))
    windows, terms, spread = call(
        functools.partial(near_kernel, width),
        (windows_shape, shape((half, 3 * lanes), f32), shape((cells, chans), f32)),
        (tall,),
        flops=NEAR * flops,
        bytes_accessed=4 * MIB,
    )(in_specs=[VMEM] * 4, out_specs=[VMEM] * 3)(own, near, mine, paired_weight)
    radix = min(4, blocks // 2)
    piece = half // radix
    folded = (piece * taps // 2, 2 * filt)
    pieces = (shape(folded, f32),) + (shape(folded, bf16),) * (radix - 1)
    outer, *partial = call(
        functools.partial(theirs_kernel, width),
        (shape((half, 9 * filt), f32),) + pieces,
        (pltpu.VMEM((half, cells), bf16), pltpu.VMEM(windows_shape.shape, bf16), tall),
        flops=THEIRS * flops,
        bytes_accessed=4 * MIB,
    )(in_specs=[VMEM] * 5, out_specs=[VMEM] * (radix + 1))(came, other, two_off, windows, terms)
    kept_in, sent_in, kept, *sends = call(
        functools.partial(one_kernel, width, groups, radix),
        (shape((cells // 2, chans), f32), shape((cells // 2, chans), bf16)) + pieces,
        (pltpu.VMEM((cells + 2 * width, 3 * filt), bf16), tall),
        flops=ONE * flops,
        bytes_accessed=4 * MIB,
        aliases={5 + n: 2 + n for n in range(radix)},
    )(in_specs=[VMEM] * (5 + radix), out_specs=[VMEM] * (radix + 2))(
        one_off, mine, single_weight, spread, outer, *partial
    )
    came_in = swapped(sent_in, "filt", 1)

    distance = 2
    while True:
        spans = {2: (1,), 4: (2, 1, 3)}[radix]
        arrived = [swapped(sends[n - 1], "space", spans[n - 1] * distance) for n in range(1, radix)]
        distance *= radix
        if distance >= blocks:
            break
        total = kept
        for value in arrived:
            total = total + value.astype(f32)
        if total.shape == folded:
            total = unfolded(total, piece)
        radix = min(4, blocks // distance)
        piece //= radix
        kept, *sends = (total[n * piece : (n + 1) * piece] for n in range(radix))
        sends = [value.astype(bf16) for value in sends]

    distance_in = 2
    while distance_in < groups:
        kept_in, sent_in = halved(kept_in, came_in)
        came_in = swapped(sent_in, "filt", distance_in)
        distance_in *= 2
    grad_scale = float(cells * blocks) ** (-0.5)
    summed = call(
        functools.partial(sum_kernel, grad_scale, kept.shape == folded), shape((chans // blocks, taps * filt), f32), flops=FINAL * flops
    )(in_specs=[VMEM] * (len(arrived) + 1), out_specs=VMEM)(kept, *arrived)
    any_space = pl.BlockSpec(memory_space=pl.ANY)
    rows_shape = (cells // groups, chans)
    grad_weight, grad_input = call(
        functools.partial(last_kernel, filt),
        (shape((taps, chans // blocks, filt), f32), shape(rows_shape, bf16)),
        (
            pltpu.VMEM((3, 9, chans // blocks, filt), f32),
            pltpu.VMEM(rows_shape, bf16),
            pltpu.SemaphoreType.DMA((4,)),
        ),
    )(in_specs=[VMEM] * 3, out_specs=[any_space] * 2)(summed, kept_in, came_in)
    return grad_input.reshape(1, height // groups, width, chans), jnp.transpose(grad_weight, (1, 0, 2))


def solution(mesh):
    placed = (
        P("space", None, None, None),
        P("space", "filt", None),
        P("space", "filt", None),
        P(None, "filt", None),
    )
    return jax.shard_map(
        on_device,
        mesh=mesh,
        in_specs=placed,
        out_specs=(P("space", "filt", None, None), P("space", None, "filt")),
        check_vma=False,
    )
```

```python
import functools

import jax
import jax.numpy as jnp
from jax import lax
from jax.experimental import pallas as pl
from jax.experimental.pallas import tpu as pltpu
from jax.sharding import PartitionSpec as P

MIB = 1 << 20
AGAIN, PICK, TURN, NEAR, THEIRS, ONE, FINAL, ORDER = 0, 3, 1, 3, 3, 3, 3, 3
VMEM = pl.BlockSpec(memory_space=pltpu.VMEM)


def silu_grad(values):
    sig = jax.nn.sigmoid(values)
    return sig * (1.0 + values * (1.0 - sig))


def bits_of(count):
    return count.bit_length() - 1


def reversed_bits(value, width):
    return sum(((value >> bit) & 1) << (width - 1 - bit) for bit in range(width))


def call(kernel, outs, scratch=(), flops=0, bytes_accessed=0, limit=24, aliases={}):
    return functools.partial(
        pl.pallas_call,
        kernel,
        out_shape=outs,
        scratch_shapes=scratch,
        input_output_aliases=aliases,
        compiler_params=pltpu.CompilerParams(vmem_limit_bytes=limit * MIB),
        cost_estimate=pl.CostEstimate(flops=flops, bytes_accessed=bytes_accessed, transcendentals=0),
    )


def lay_windows(width, first, second, windows, tall):
    filt, cells = first.shape
    lanes = 2 * filt
    tall[pl.ds(8, cells), :] = jnp.concatenate([first, second], axis=0).astype(jnp.float32).T
    row = lax.broadcasted_iota(jnp.int32, (cells, lanes), 0)
    column = row & (width - 1) if width & (width - 1) == 0 else lax.rem(row, width)
    zero_rows = jnp.zeros((width, windows.shape[1]), jnp.bfloat16)
    windows[pl.ds(0, width), :] = zero_rows
    windows[pl.ds(width + cells, width), :] = zero_rows
    body = pl.ds(width, cells)
    windows[body, 0:lanes] = jnp.where(column != width - 1, tall[pl.ds(9, cells), :], 0.0).astype(jnp.bfloat16)
    windows[body, lanes : 2 * lanes] = tall[pl.ds(8, cells), :].astype(jnp.bfloat16)
    windows[body, 2 * lanes : 3 * lanes] = jnp.where(column != 0, tall[pl.ds(7, cells), :], 0.0).astype(jnp.bfloat16)


def lay_single(width, layer, windows, tall):
    filt, cells = layer.shape
    lanes = 2 * filt
    tall[pl.ds(8, cells), :] = jnp.concatenate([layer, layer], axis=0).astype(jnp.float32).T
    row = lax.broadcasted_iota(jnp.int32, (cells, lanes), 0)
    column = row & (width - 1) if width & (width - 1) == 0 else lax.rem(row, width)
    left = lax.broadcasted_iota(jnp.int32, (cells, lanes), 1) < filt
    zero_rows = jnp.zeros((width, windows.shape[1]), jnp.bfloat16)
    windows[pl.ds(0, width), :] = zero_rows
    windows[pl.ds(width + cells, width), :] = zero_rows
    body = pl.ds(width, cells)
    low = jnp.where(column != width - 1, tall[pl.ds(9, cells), :], 0.0)
    high = jnp.where(column != 0, tall[pl.ds(7, cells), :], 0.0)
    windows[body, 0:lanes] = jnp.where(left, low, high).astype(jnp.bfloat16)
    windows[body, lanes : lanes + filt] = tall[pl.ds(8, cells), 0:filt].astype(jnp.bfloat16)


def pick_kernel(blocks, picked):
    size, chans = picked.shape
    rows = chans // blocks
    half = chans // 2
    count = bits_of(blocks)
    order = lax.broadcasted_iota(jnp.int32, (size, chans), 0)
    order = order + jnp.where(order >= half, (lax.axis_index("filt") & 1) * (size - half), 0)
    block = lax.axis_index("space") ^ reversed_bits(order >> bits_of(rows), count)
    source = (block << bits_of(rows)) | (order & (rows - 1))
    picked[...] = (lax.broadcasted_iota(jnp.int32, (size, chans), 1) == source).astype(jnp.bfloat16)


def turn_kernel(picked, inputs, _, mine, part):
    half = mine.shape[0]
    turned = lax.dot_general(picked[...], inputs[...], (((1,), (1,)), ((), ())), preferred_element_type=jnp.float32)
    turned = turned.astype(jnp.bfloat16)
    mine[...] = turned[0:half, :]
    part[...] = turned[half:, :]


def grads_kernel(_, out_grad, pre_act, own):
    own[...] = (out_grad[...].astype(jnp.float32) * silu_grad(pre_act[...].astype(jnp.float32))).astype(own.dtype)


def again_kernel(own, out):
    out[...] = own[...]


def order_kernel(weight, paired, single):
    filt = weight.shape[1]
    odd = lax.axis_index("space") & 1
    for tap in range(9):
        b, c = divmod(tap, 3)
        low, high = pl.ds(2 * c * filt, filt), pl.ds((2 * c + 1) * filt, filt)
        paired[b, low, :] = weight[9 + tap]
        paired[b, high, :] = weight[18 * odd + tap]
        single[b, pl.ds((0, 2, 1)[c] * filt, filt), :] = weight[18 - 18 * odd + tap]


def near_kernel(width, own, near, mine, weight, windows, terms, spread, tall):
    cells = own.shape[1]
    wide = windows.shape[1]
    lay_windows(width, own[...], near[...], windows, tall)
    total = 0.0
    for b in range(3):
        window = windows[pl.ds((2 - b) * width, cells), :]
        terms[:, b * wide : (b + 1) * wide] = jnp.dot(mine[...], window, preferred_element_type=jnp.float32)
        total = total + jnp.dot(window, weight[b], preferred_element_type=jnp.float32)
    spread[...] = total


def store_tile(value, tile, keep, sends):
    lanes = keep.shape[1]
    part = value.shape[0] // (len(sends) + 1)
    rows = pl.ds(tile * part, part if value.shape[1] == lanes else part // 2)
    for number, target in enumerate((keep, *sends)):
        piece = value[number * part : (number + 1) * part, :]
        if value.shape[1] < lanes:
            piece = jnp.concatenate([piece[0 : part // 2, :], piece[part // 2 :, :]], axis=1)
        target[rows, :] = piece.astype(target.dtype)


def theirs_kernel(width, came, other, two_off, windows, terms, outer, keep, *rest):
    *sends, theirs, twos, tall = rest
    part, cells = came.shape
    wide = windows.shape[1]
    lanes = wide // 3
    filt = lanes // 2
    first_core = lax.axis_index("filt") & 1 == 0
    theirs[0:part, :] = jnp.where(first_core, came[...], other[...])
    theirs[part:, :] = jnp.where(first_core, other[...], came[...])
    lay_windows(width, two_off[...], two_off[...], twos, tall)
    left = lax.broadcasted_iota(jnp.int32, (2 * part, lanes), 1) < filt
    middle = []
    for b in range(3):
        rows = pl.ds((2 - b) * width, cells)
        near_terms = jnp.dot(theirs[...], windows[rows, :], preferred_element_type=jnp.float32)
        two_terms = jnp.dot(theirs[...], twos[rows, :], preferred_element_type=jnp.float32)
        cuts = [slice(c * lanes, (c + 1) * lanes) for c in range(3)]
        for c, cut in enumerate(cuts):
            lo = b * wide + c * lanes
            crossed = jnp.where(left, pltpu.roll(near_terms[:, cut], filt, 1), two_terms[:, cut])
            store_tile(terms[:, lo : lo + lanes] + crossed, 3 * b + c, keep, sends)
        outer[:, b * lanes : (b + 1) * lanes] = jnp.where(
            left, near_terms[:, cuts[0]], pltpu.roll(near_terms[:, cuts[2]], filt, 1)
        )
        middle.append(near_terms[:, cuts[1]])
    outer[:, wide : wide + lanes] = jnp.where(left, middle[0], pltpu.roll(middle[1], filt, 1))
    outer[:, wide + lanes : wide + lanes + filt] = middle[2][:, 0:filt]


def one_kernel(width, groups, radix, one_off, mine, weight, spread, outer, *rest):
    kept_in, sent_in, keep, *rest = rest[radix:]
    *sends, windows, tall = rest
    cells = mine.shape[1]
    lanes = keep.shape[1]
    filt = lanes // 2
    lay_single(width, one_off[...], windows, tall)

    middle = []
    for b in range(3):
        window = windows[pl.ds((2 - b) * width, cells), :]
        terms = jnp.dot(mine[...], window, preferred_element_type=jnp.float32)
        store_tile(terms[:, 0:lanes] + outer[:, b * lanes : (b + 1) * lanes], 9 + b, keep, sends)
        middle.append(terms[:, lanes : lanes + filt])
    both = jnp.concatenate(middle[0:2], axis=1)
    store_tile(both + outer[:, 3 * lanes : 4 * lanes], 12, keep, sends)
    store_tile(middle[2] + outer[:, 4 * lanes : 4 * lanes + filt], 13, keep, sends)

    size = cells // groups
    index = lax.axis_index("filt")
    count = bits_of(groups)
    for target in reversed(range(groups)):
        block = 0
        for bit in range(count):
            differs = (target >> (count - 1 - bit)) & 1
            block = block + (((index >> bit) & 1) ^ differs) * (1 << bit)
        start = pl.multiple_of(block * size, size)
        total = spread[pl.ds(start, size), :]
        for b in range(3):
            rows = pl.ds(pl.multiple_of(start + (2 - b) * width, width), size)
            total = total + jnp.dot(windows[rows, :], weight[b], preferred_element_type=jnp.float32)
        if target < groups // 2:
            kept_in[pl.ds(target * size, size), :] = total
        else:
            sent_in[pl.ds((target - groups // 2) * size, size), :] = total.astype(jnp.bfloat16)


def unfolded(tiles, rows):
    full = tiles.shape[0] // rows
    whole = [tiles[n * rows : (n + 1) * rows] for n in range(full)]
    half = tiles[full * rows :]
    lanes = tiles.shape[1]
    return jnp.concatenate([*whole, jnp.concatenate([half[:, : lanes // 2], half[:, lanes // 2 :]], axis=0)], axis=1)


def halve_kernel(kept, came, keep, send):
    half = keep.shape[0]
    keep[...] = kept[0:half, :] + came[0:half, :].astype(jnp.float32)
    send[...] = (kept[half:, :] + came[half:, :].astype(jnp.float32)).astype(jnp.bfloat16)


def sum_kernel(scale, folded, kept, *rest):
    *came, out = rest
    total = kept[...]
    for piece in came:
        total = total + piece[...].astype(jnp.float32)
    total = total * scale
    if not folded:
        out[...] = total
        return
    rows, lanes = out.shape[0], total.shape[1]
    full = total.shape[0] // rows
    for tile in range(full):
        out[:, tile * lanes : (tile + 1) * lanes] = total[tile * rows : (tile + 1) * rows, :]
    out[0 : rows // 2, full * lanes :] = total[full * rows :, 0 : lanes // 2]
    out[rows // 2 :, full * lanes :] = total[full * rows :, lanes // 2 :]


def last_kernel(filt, summed, kept, came, out, grad_input, taps, rows, done):
    odd = lax.axis_index("space") & 1
    rows[...] = (kept[...] + came[...].astype(jnp.float32)).astype(rows.dtype)
    copies = [pltpu.make_async_copy(rows, grad_input, done.at[3])]
    copies[0].start()
    total = summed[...]
    outer = [18 + 2 * (tap // 3) + tap % 3 // 2 if tap % 3 != 1 else 24 + tap // 3 for tap in range(9)]
    for group, (slots, target) in enumerate(((range(0, 18, 2), 1), (range(1, 18, 2), 2 * odd), (outer, 2 - 2 * odd))):
        for tap, slot in enumerate(slots):
            taps[group, tap] = total[:, slot * filt : (slot + 1) * filt]
        copy = pltpu.make_async_copy(taps.at[group], out.at[pl.ds(target * 9, 9)], done.at[group])
        copy.start()
        copies.append(copy)
    for copy in copies:
        copy.wait()


def swapped(value, axis, distance):
    count = lax.axis_size(axis)
    return lax.ppermute(value, axis, [(i, i ^ distance) for i in range(count)])


def halved(kept, came):
    rows, lanes = kept.shape
    if rows // 2 % 16:
        total = kept + came.astype(jnp.float32)
        return total[: rows // 2], total[rows // 2 :].astype(jnp.bfloat16)
    outs = (
        jax.ShapeDtypeStruct((rows // 2, lanes), jnp.float32),
        jax.ShapeDtypeStruct((rows // 2, lanes), jnp.bfloat16),
    )
    return call(halve_kernel, outs, flops=rows * lanes, bytes_accessed=9 * rows * lanes)(
        in_specs=[VMEM] * 2, out_specs=[VMEM] * 2
    )(kept, came)


def after(value, other):
    return lax.optimization_barrier((value, other))[0]


def on_device(inputs, out_grad, pre_act, weight):
    _, height, width, chans = inputs.shape
    taps, filt, _ = weight.shape
    cells = height * width
    blocks, groups = lax.axis_size("space"), lax.axis_size("filt")
    half, quarter = chans // 2, chans // 4
    bf16, f32 = jnp.bfloat16, jnp.float32
    shape = jax.ShapeDtypeStruct
    flops = 2 * cells * taps * filt * chans
    lanes = 6 * filt
    windows_shape = shape((cells + 2 * width, lanes), bf16)
    tall = pltpu.VMEM((cells + 16, 2 * filt), f32)

    picked = call(
        functools.partial(pick_kernel, blocks), shape((half + quarter, chans), bf16), flops=PICK * flops
    )(in_specs=[], out_specs=VMEM)()
    own = call(grads_kernel, shape((filt, cells), bf16))(in_specs=[VMEM] * 3, out_specs=VMEM)(
        picked, out_grad[0], pre_act[0]
    )
    own_again = call(again_kernel, shape((filt, cells), bf16), flops=AGAIN * flops)(in_specs=[VMEM], out_specs=VMEM)(own)
    mine, part = call(
        turn_kernel,
        (shape((half, cells), bf16), shape((quarter, cells), bf16)),
        flops=TURN * flops,
    )(in_specs=[VMEM] * 3, out_specs=[VMEM] * 2)(picked, inputs.reshape(cells, chans), own_again)
    near = swapped(own, "space", 1)
    came = swapped(part, "space", 1)
    up = [(i, i + 2) for i in range(blocks - 2)]
    down = [(target, source) for source, target in up]
    even, odd = slice(0, None, 2), slice(1, None, 2)
    two_off = lax.ppermute(own_again, "space", down[even] + up[odd])
    one_off = lax.ppermute(near, "space", up[even] + down[odd])
    other = swapped(came, "filt", 1)

    weight_shape = shape((3, lanes, chans), bf16)
    paired_weight, single_weight = call(
        order_kernel, (weight_shape, shape((3, 3 * filt, chans), bf16)), flops=ORDER * flops, bytes_accessed=MIB
    )(in_specs=[VMEM], out_specs=[VMEM] * 2)(after(weight, mine))
    windows, terms, spread = call(
        functools.partial(near_kernel, width),
        (windows_shape, shape((half, 3 * lanes), f32), shape((cells, chans), f32)),
        (tall,),
        flops=NEAR * flops,
        bytes_accessed=4 * MIB,
    )(in_specs=[VMEM] * 4, out_specs=[VMEM] * 3)(own, near, mine, paired_weight)
    radix = min(4, blocks // 2)
    piece = half // radix
    folded = (piece * taps // 2, 2 * filt)
    pieces = (shape(folded, f32),) + (shape(folded, bf16),) * (radix - 1)
    outer, *partial = call(
        functools.partial(theirs_kernel, width),
        (shape((half, 9 * filt), f32),) + pieces,
        (pltpu.VMEM((half, cells), bf16), pltpu.VMEM(windows_shape.shape, bf16), tall),
        flops=THEIRS * flops,
        bytes_accessed=4 * MIB,
    )(in_specs=[VMEM] * 5, out_specs=[VMEM] * (radix + 1))(came, other, two_off, windows, terms)
    kept_in, sent_in, kept, *sends = call(
        functools.partial(one_kernel, width, groups, radix),
        (shape((cells // 2, chans), f32), shape((cells // 2, chans), bf16)) + pieces,
        (pltpu.VMEM((cells + 2 * width, 3 * filt), bf16), tall),
        flops=ONE * flops,
        bytes_accessed=4 * MIB,
        aliases={5 + n: 2 + n for n in range(radix)},
    )(in_specs=[VMEM] * (5 + radix), out_specs=[VMEM] * (radix + 2))(
        one_off, mine, single_weight, spread, outer, *partial
    )
    came_in = swapped(sent_in, "filt", 1)

    distance = 2
    while True:
        spans = {2: (1,), 4: (2, 1, 3)}[radix]
        far_first = sorted(range(1, radix), key=lambda n: spans[n - 1] == 1)
        arrived = [swapped(sends[n - 1], "space", spans[n - 1] * distance) for n in far_first]
        distance *= radix
        if distance >= blocks:
            break
        total = kept
        for value in arrived:
            total = total + value.astype(f32)
        if total.shape == folded:
            total = unfolded(total, piece)
        radix = min(4, blocks // distance)
        piece //= radix
        kept, *sends = (total[n * piece : (n + 1) * piece] for n in range(radix))
        sends = [value.astype(bf16) for value in sends]

    distance_in = 2
    while distance_in < groups:
        kept_in, sent_in = halved(kept_in, came_in)
        came_in = swapped(sent_in, "filt", distance_in)
        distance_in *= 2
    grad_scale = float(cells * blocks) ** (-0.5)
    summed = call(
        functools.partial(sum_kernel, grad_scale, kept.shape == folded), shape((chans // blocks, taps * filt), f32), flops=FINAL * flops
    )(in_specs=[VMEM] * (len(arrived) + 1), out_specs=VMEM)(kept, *arrived)
    any_space = pl.BlockSpec(memory_space=pl.ANY)
    rows_shape = (cells // groups, chans)
    grad_weight, grad_input = call(
        functools.partial(last_kernel, filt),
        (shape((taps, chans // blocks, filt), f32), shape(rows_shape, bf16)),
        (
            pltpu.VMEM((3, 9, chans // blocks, filt), f32),
            pltpu.VMEM(rows_shape, bf16),
            pltpu.SemaphoreType.DMA((4,)),
        ),
    )(in_specs=[VMEM] * 3, out_specs=[any_space] * 2)(summed, kept_in, came_in)
    return grad_input.reshape(1, height // groups, width, chans), jnp.transpose(grad_weight, (1, 0, 2))


def solution(mesh):
    placed = (
        P("space", None, None, None),
        P("space", "filt", None),
        P("space", "filt", None),
        P(None, "filt", None),
    )
    return jax.shard_map(
        on_device,
        mesh=mesh,
        in_specs=placed,
        out_specs=(P("space", "filt", None, None), P("space", None, "filt")),
        check_vma=False,
    )
```

```python
import functools

import jax
import jax.numpy as jnp
from jax import lax
from jax.experimental import pallas as pl
from jax.experimental.pallas import tpu as pltpu
from jax.sharding import PartitionSpec as P

MIB = 1 << 20
AGAIN, PICK, TURN, NEAR, THEIRS, ONE, FINAL, ORDER = 0, 3, 1, 3, 3, 3, 3, 3
VMEM = pl.BlockSpec(memory_space=pltpu.VMEM)


def silu_grad(values):
    sig = jax.nn.sigmoid(values)
    return sig * (1.0 + values * (1.0 - sig))


def bits_of(count):
    return count.bit_length() - 1


def reversed_bits(value, width):
    return sum(((value >> bit) & 1) << (width - 1 - bit) for bit in range(width))


def call(kernel, outs, scratch=(), flops=0, bytes_accessed=0, limit=24, aliases={}):
    return functools.partial(
        pl.pallas_call,
        kernel,
        out_shape=outs,
        scratch_shapes=scratch,
        input_output_aliases=aliases,
        compiler_params=pltpu.CompilerParams(vmem_limit_bytes=limit * MIB),
        cost_estimate=pl.CostEstimate(flops=flops, bytes_accessed=bytes_accessed, transcendentals=0),
    )


def lay_windows(width, first, second, windows, tall):
    filt, cells = first.shape
    lanes = 2 * filt
    tall[pl.ds(8, cells), :] = jnp.concatenate([first, second], axis=0).astype(jnp.float32).T
    row = lax.broadcasted_iota(jnp.int32, (cells, lanes), 0)
    column = row & (width - 1) if width & (width - 1) == 0 else lax.rem(row, width)
    zero_rows = jnp.zeros((width, windows.shape[1]), jnp.bfloat16)
    windows[pl.ds(0, width), :] = zero_rows
    windows[pl.ds(width + cells, width), :] = zero_rows
    body = pl.ds(width, cells)
    windows[body, 0:lanes] = jnp.where(column != width - 1, tall[pl.ds(9, cells), :], 0.0).astype(jnp.bfloat16)
    windows[body, lanes : 2 * lanes] = tall[pl.ds(8, cells), :].astype(jnp.bfloat16)
    windows[body, 2 * lanes : 3 * lanes] = jnp.where(column != 0, tall[pl.ds(7, cells), :], 0.0).astype(jnp.bfloat16)


def lay_single(width, layer, windows, tall):
    filt, cells = layer.shape
    lanes = 2 * filt
    tall[pl.ds(8, cells), :] = jnp.concatenate([layer, layer], axis=0).astype(jnp.float32).T
    row = lax.broadcasted_iota(jnp.int32, (cells, lanes), 0)
    column = row & (width - 1) if width & (width - 1) == 0 else lax.rem(row, width)
    left = lax.broadcasted_iota(jnp.int32, (cells, lanes), 1) < filt
    zero_rows = jnp.zeros((width, windows.shape[1]), jnp.bfloat16)
    windows[pl.ds(0, width), :] = zero_rows
    windows[pl.ds(width + cells, width), :] = zero_rows
    body = pl.ds(width, cells)
    low = jnp.where(column != width - 1, tall[pl.ds(9, cells), :], 0.0)
    high = jnp.where(column != 0, tall[pl.ds(7, cells), :], 0.0)
    windows[body, 0:lanes] = jnp.where(left, low, high).astype(jnp.bfloat16)
    windows[body, lanes : lanes + filt] = tall[pl.ds(8, cells), 0:filt].astype(jnp.bfloat16)


def pick_kernel(blocks, picked):
    size, chans = picked.shape
    rows = chans // blocks
    half = chans // 2
    count = bits_of(blocks)
    order = lax.broadcasted_iota(jnp.int32, (size, chans), 0)
    order = order + jnp.where(order >= half, (lax.axis_index("filt") & 1) * (size - half), 0)
    block = lax.axis_index("space") ^ reversed_bits(order >> bits_of(rows), count)
    source = (block << bits_of(rows)) | (order & (rows - 1))
    picked[...] = (lax.broadcasted_iota(jnp.int32, (size, chans), 1) == source).astype(jnp.bfloat16)


def turn_kernel(picked, inputs, _, mine, part):
    half = mine.shape[0]
    turned = lax.dot_general(picked[...], inputs[...], (((1,), (1,)), ((), ())), preferred_element_type=jnp.float32)
    turned = turned.astype(jnp.bfloat16)
    mine[...] = turned[0:half, :]
    part[...] = turned[half:, :]


def grads_kernel(_, out_grad, pre_act, own):
    own[...] = (out_grad[...].astype(jnp.float32) * silu_grad(pre_act[...].astype(jnp.float32))).astype(own.dtype)


def again_kernel(own, out):
    out[...] = own[...]


def order_kernel(weight, paired, single):
    filt = weight.shape[1]
    odd = lax.axis_index("space") & 1
    for tap in range(9):
        b, c = divmod(tap, 3)
        low, high = pl.ds(2 * c * filt, filt), pl.ds((2 * c + 1) * filt, filt)
        paired[b, low, :] = weight[9 + tap]
        paired[b, high, :] = weight[18 * odd + tap]
        single[b, pl.ds((0, 2, 1)[c] * filt, filt), :] = weight[18 - 18 * odd + tap]


def near_kernel(width, own, near, mine, weight, windows, terms, spread, tall):
    cells = own.shape[1]
    wide = windows.shape[1]
    lay_windows(width, own[...], near[...], windows, tall)
    total = 0.0
    for b in range(3):
        window = windows[pl.ds((2 - b) * width, cells), :]
        terms[:, b * wide : (b + 1) * wide] = jnp.dot(mine[...], window, preferred_element_type=jnp.float32)
        total = total + jnp.dot(window, weight[b], preferred_element_type=jnp.float32)
    spread[...] = total


def store_tile(value, tile, keep, sends):
    lanes = keep.shape[1]
    part = value.shape[0] // (len(sends) + 1)
    rows = pl.ds(tile * part, part if value.shape[1] == lanes else part // 2)
    for number, target in enumerate((keep, *sends)):
        piece = value[number * part : (number + 1) * part, :]
        if value.shape[1] < lanes:
            piece = jnp.concatenate([piece[0 : part // 2, :], piece[part // 2 :, :]], axis=1)
        target[rows, :] = piece.astype(target.dtype)


def theirs_kernel(width, came, other, two_off, windows, terms, outer, keep, *rest):
    *sends, theirs, twos, tall = rest
    part, cells = came.shape
    wide = windows.shape[1]
    lanes = wide // 3
    filt = lanes // 2
    first_core = lax.axis_index("filt") & 1 == 0
    theirs[0:part, :] = jnp.where(first_core, came[...], other[...])
    theirs[part:, :] = jnp.where(first_core, other[...], came[...])
    lay_windows(width, two_off[...], two_off[...], twos, tall)
    left = lax.broadcasted_iota(jnp.int32, (2 * part, lanes), 1) < filt
    middle = []
    for b in range(3):
        rows = pl.ds((2 - b) * width, cells)
        near_terms = jnp.dot(theirs[...], windows[rows, :], preferred_element_type=jnp.float32)
        two_terms = jnp.dot(theirs[...], twos[rows, :], preferred_element_type=jnp.float32)
        cuts = [slice(c * lanes, (c + 1) * lanes) for c in range(3)]
        for c, cut in enumerate(cuts):
            lo = b * wide + c * lanes
            crossed = jnp.where(left, pltpu.roll(near_terms[:, cut], filt, 1), two_terms[:, cut])
            store_tile(terms[:, lo : lo + lanes] + crossed, 3 * b + c, keep, sends)
        outer[:, b * lanes : (b + 1) * lanes] = jnp.where(
            left, near_terms[:, cuts[0]], pltpu.roll(near_terms[:, cuts[2]], filt, 1)
        )
        middle.append(near_terms[:, cuts[1]])
    outer[:, wide : wide + lanes] = jnp.where(left, middle[0], pltpu.roll(middle[1], filt, 1))
    outer[:, wide + lanes : wide + lanes + filt] = middle[2][:, 0:filt]


def rows_total(width, groups, target, windows, weight, spread):
    size = spread.shape[0] // groups
    index = lax.axis_index("filt")
    count = bits_of(groups)
    block = 0
    for bit in range(count):
        differs = (target >> (count - 1 - bit)) & 1
        block = block + (((index >> bit) & 1) ^ differs) * (1 << bit)
    start = pl.multiple_of(block * size, size)
    total = spread[pl.ds(start, size), :]
    for b in range(3):
        rows = pl.ds(pl.multiple_of(start + (2 - b) * width, width), size)
        total = total + jnp.dot(windows[rows, :], weight[b], preferred_element_type=jnp.float32)
    return total


def first_half_kernel(width, groups, windows, weight, spread, came, keep, send):
    size = spread.shape[0] // groups
    for target in range(groups // 2):
        total = rows_total(width, groups, target, windows, weight, spread)
        total = total + came[target * size : (target + 1) * size, :].astype(jnp.float32)
        if target < groups // 4:
            keep[target * size : (target + 1) * size, :] = total
        else:
            lo = (target - groups // 4) * size
            send[lo : lo + size, :] = total.astype(jnp.bfloat16)


def one_kernel(width, groups, radix, one_off, mine, weight, spread, outer, *rest):
    windows, sent_in, keep, *rest = rest[radix:]
    *sends, tall = rest
    cells = mine.shape[1]
    lanes = keep.shape[1]
    filt = lanes // 2
    lay_single(width, one_off[...], windows, tall)

    middle = []
    for b in range(3):
        window = windows[pl.ds((2 - b) * width, cells), :]
        terms = jnp.dot(mine[...], window, preferred_element_type=jnp.float32)
        store_tile(terms[:, 0:lanes] + outer[:, b * lanes : (b + 1) * lanes], 9 + b, keep, sends)
        middle.append(terms[:, lanes : lanes + filt])
    both = jnp.concatenate(middle[0:2], axis=1)
    store_tile(both + outer[:, 3 * lanes : 4 * lanes], 12, keep, sends)
    store_tile(middle[2] + outer[:, 4 * lanes : 4 * lanes + filt], 13, keep, sends)

    size = cells // groups
    for target in range(groups // 2, groups):
        lo = (target - groups // 2) * size
        total = rows_total(width, groups, target, windows, weight, spread)
        sent_in[lo : lo + size, :] = total.astype(jnp.bfloat16)


def unfolded(tiles, rows):
    full = tiles.shape[0] // rows
    whole = [tiles[n * rows : (n + 1) * rows] for n in range(full)]
    half = tiles[full * rows :]
    lanes = tiles.shape[1]
    return jnp.concatenate([*whole, jnp.concatenate([half[:, : lanes // 2], half[:, lanes // 2 :]], axis=0)], axis=1)


def halve_kernel(kept, came, keep, send):
    half = keep.shape[0]
    keep[...] = kept[0:half, :] + came[0:half, :].astype(jnp.float32)
    send[...] = (kept[half:, :] + came[half:, :].astype(jnp.float32)).astype(jnp.bfloat16)


def sum_kernel(scale, folded, kept, *rest):
    *came, out = rest
    total = kept[...]
    for piece in came:
        total = total + piece[...].astype(jnp.float32)
    total = total * scale
    if not folded:
        out[...] = total
        return
    rows, lanes = out.shape[0], total.shape[1]
    full = total.shape[0] // rows
    for tile in range(full):
        out[:, tile * lanes : (tile + 1) * lanes] = total[tile * rows : (tile + 1) * rows, :]
    out[0 : rows // 2, full * lanes :] = total[full * rows :, 0 : lanes // 2]
    out[rows // 2 :, full * lanes :] = total[full * rows :, lanes // 2 :]


def last_kernel(filt, summed, kept, came, out, grad_input, taps, rows, done):
    odd = lax.axis_index("space") & 1
    rows[...] = (kept[...] + came[...].astype(jnp.float32)).astype(rows.dtype)
    copies = [pltpu.make_async_copy(rows, grad_input, done.at[3])]
    copies[0].start()
    total = summed[...]
    outer = [18 + 2 * (tap // 3) + tap % 3 // 2 if tap % 3 != 1 else 24 + tap // 3 for tap in range(9)]
    for group, (slots, target) in enumerate(((range(0, 18, 2), 1), (range(1, 18, 2), 2 * odd), (outer, 2 - 2 * odd))):
        for tap, slot in enumerate(slots):
            taps[group, tap] = total[:, slot * filt : (slot + 1) * filt]
        copy = pltpu.make_async_copy(taps.at[group], out.at[pl.ds(target * 9, 9)], done.at[group])
        copy.start()
        copies.append(copy)
    for copy in copies:
        copy.wait()


def swapped(value, axis, distance):
    count = lax.axis_size(axis)
    return lax.ppermute(value, axis, [(i, i ^ distance) for i in range(count)])


def halved(kept, came):
    rows, lanes = kept.shape
    if rows // 2 % 16:
        total = kept + came.astype(jnp.float32)
        return total[: rows // 2], total[rows // 2 :].astype(jnp.bfloat16)
    outs = (
        jax.ShapeDtypeStruct((rows // 2, lanes), jnp.float32),
        jax.ShapeDtypeStruct((rows // 2, lanes), jnp.bfloat16),
    )
    return call(halve_kernel, outs, flops=rows * lanes, bytes_accessed=9 * rows * lanes)(
        in_specs=[VMEM] * 2, out_specs=[VMEM] * 2
    )(kept, came)


def after(value, other):
    return lax.optimization_barrier((value, other))[0]


def on_device(inputs, out_grad, pre_act, weight):
    _, height, width, chans = inputs.shape
    taps, filt, _ = weight.shape
    cells = height * width
    blocks, groups = lax.axis_size("space"), lax.axis_size("filt")
    half, quarter = chans // 2, chans // 4
    bf16, f32 = jnp.bfloat16, jnp.float32
    shape = jax.ShapeDtypeStruct
    flops = 2 * cells * taps * filt * chans
    lanes = 6 * filt
    windows_shape = shape((cells + 2 * width, lanes), bf16)
    tall = pltpu.VMEM((cells + 16, 2 * filt), f32)

    picked = call(
        functools.partial(pick_kernel, blocks), shape((half + quarter, chans), bf16), flops=PICK * flops
    )(in_specs=[], out_specs=VMEM)()
    own = call(grads_kernel, shape((filt, cells), bf16))(in_specs=[VMEM] * 3, out_specs=VMEM)(
        picked, out_grad[0], pre_act[0]
    )
    own_again = call(again_kernel, shape((filt, cells), bf16), flops=AGAIN * flops)(in_specs=[VMEM], out_specs=VMEM)(own)
    mine, part = call(
        turn_kernel,
        (shape((half, cells), bf16), shape((quarter, cells), bf16)),
        flops=TURN * flops,
    )(in_specs=[VMEM] * 3, out_specs=[VMEM] * 2)(picked, inputs.reshape(cells, chans), own_again)
    near = swapped(own, "space", 1)
    came = swapped(part, "space", 1)
    up = [(i, i + 2) for i in range(blocks - 2)]
    down = [(target, source) for source, target in up]
    even, odd = slice(0, None, 2), slice(1, None, 2)
    two_off = lax.ppermute(own_again, "space", down[even] + up[odd])
    one_off = lax.ppermute(near, "space", up[even] + down[odd])
    other = swapped(came, "filt", 1)

    weight_shape = shape((3, lanes, chans), bf16)
    paired_weight, single_weight = call(
        order_kernel, (weight_shape, shape((3, 3 * filt, chans), bf16)), flops=ORDER * flops, bytes_accessed=MIB
    )(in_specs=[VMEM], out_specs=[VMEM] * 2)(after(weight, mine))
    windows, terms, spread = call(
        functools.partial(near_kernel, width),
        (windows_shape, shape((half, 3 * lanes), f32), shape((cells, chans), f32)),
        (tall,),
        flops=NEAR * flops,
        bytes_accessed=4 * MIB,
    )(in_specs=[VMEM] * 4, out_specs=[VMEM] * 3)(own, near, mine, paired_weight)
    radix = min(4, blocks // 2)
    piece = half // radix
    folded = (piece * taps // 2, 2 * filt)
    pieces = (shape(folded, f32),) + (shape(folded, bf16),) * (radix - 1)
    outer, *partial = call(
        functools.partial(theirs_kernel, width),
        (shape((half, 9 * filt), f32),) + pieces,
        (pltpu.VMEM((half, cells), bf16), pltpu.VMEM(windows_shape.shape, bf16), tall),
        flops=THEIRS * flops,
        bytes_accessed=4 * MIB,
    )(in_specs=[VMEM] * 5, out_specs=[VMEM] * (radix + 1))(came, other, two_off, windows, terms)
    ones, sent_in, kept, *sends = call(
        functools.partial(one_kernel, width, groups, radix),
        (shape((cells + 2 * width, 3 * filt), bf16), shape((cells // 2, chans), bf16)) + pieces,
        (tall,),
        flops=ONE * flops,
        bytes_accessed=4 * MIB,
        aliases={5 + n: 2 + n for n in range(radix)},
    )(in_specs=[VMEM] * (5 + radix), out_specs=[VMEM] * (radix + 2))(
        one_off, mine, single_weight, spread, outer, *partial
    )
    came_in = swapped(sent_in, "filt", 1)

    distance = 2
    while True:
        spans = {2: (1,), 4: (2, 1, 3)}[radix]
        arrived = [swapped(sends[n - 1], "space", spans[n - 1] * distance) for n in range(1, radix)]
        distance *= radix
        if distance >= blocks:
            break
        total = kept
        for value in arrived:
            total = total + value.astype(f32)
        if total.shape == folded:
            total = unfolded(total, piece)
        radix = min(4, blocks // distance)
        piece //= radix
        kept, *sends = (total[n * piece : (n + 1) * piece] for n in range(radix))
        sends = [value.astype(bf16) for value in sends]

    block = (cells // 4, chans)
    kept_in, sent_in = call(
        functools.partial(first_half_kernel, width, groups),
        (shape(block, f32), shape(block, bf16)),
        flops=flops // 6,
        bytes_accessed=MIB,
    )(in_specs=[VMEM] * 4, out_specs=[VMEM] * 2)(ones, single_weight, spread, came_in)
    came_in = swapped(sent_in, "filt", 2)
    distance_in = 4
    while distance_in < groups:
        kept_in, sent_in = halved(kept_in, came_in)
        came_in = swapped(sent_in, "filt", distance_in)
        distance_in *= 2
    grad_scale = float(cells * blocks) ** (-0.5)
    summed = call(
        functools.partial(sum_kernel, grad_scale, kept.shape == folded), shape((chans // blocks, taps * filt), f32), flops=FINAL * flops
    )(in_specs=[VMEM] * (len(arrived) + 1), out_specs=VMEM)(kept, *arrived)
    any_space = pl.BlockSpec(memory_space=pl.ANY)
    rows_shape = (cells // groups, chans)
    grad_weight, grad_input = call(
        functools.partial(last_kernel, filt),
        (shape((taps, chans // blocks, filt), f32), shape(rows_shape, bf16)),
        (
            pltpu.VMEM((3, 9, chans // blocks, filt), f32),
            pltpu.VMEM(rows_shape, bf16),
            pltpu.SemaphoreType.DMA((4,)),
        ),
    )(in_specs=[VMEM] * 3, out_specs=[any_space] * 2)(summed, kept_in, came_in)
    return grad_input.reshape(1, height // groups, width, chans), jnp.transpose(grad_weight, (1, 0, 2))


def solution(mesh):
    placed = (
        P("space", None, None, None),
        P("space", "filt", None),
        P("space", "filt", None),
        P(None, "filt", None),
    )
    return jax.shard_map(
        on_device,
        mesh=mesh,
        in_specs=placed,
        out_specs=(P("space", "filt", None, None), P("space", None, "filt")),
        check_vma=False,
    )
```

```python
import functools

import jax
import jax.numpy as jnp
from jax import lax
from jax.experimental import pallas as pl
from jax.experimental.pallas import tpu as pltpu
from jax.sharding import PartitionSpec as P

MIB = 1 << 20
AGAIN, PICK, TURN, NEAR, THEIRS, ONE, FINAL, ORDER = 0, 3, 1, 3, 3, 3, 3, 3
VMEM = pl.BlockSpec(memory_space=pltpu.VMEM)


def silu_grad(values):
    sig = jax.nn.sigmoid(values)
    return sig * (1.0 + values * (1.0 - sig))


def bits_of(count):
    return count.bit_length() - 1


def reversed_bits(value, width):
    return sum(((value >> bit) & 1) << (width - 1 - bit) for bit in range(width))


def call(kernel, outs, scratch=(), flops=0, bytes_accessed=0, limit=24, aliases={}):
    return functools.partial(
        pl.pallas_call,
        kernel,
        out_shape=outs,
        scratch_shapes=scratch,
        input_output_aliases=aliases,
        compiler_params=pltpu.CompilerParams(vmem_limit_bytes=limit * MIB),
        cost_estimate=pl.CostEstimate(flops=flops, bytes_accessed=bytes_accessed, transcendentals=0),
    )


def lay_windows(width, first, second, windows, tall):
    filt, cells = first.shape
    lanes = 2 * filt
    tall[pl.ds(8, cells), :] = jnp.concatenate([first, second], axis=0).astype(jnp.float32).T
    row = lax.broadcasted_iota(jnp.int32, (cells, lanes), 0)
    column = row & (width - 1) if width & (width - 1) == 0 else lax.rem(row, width)
    zero_rows = jnp.zeros((width, windows.shape[1]), jnp.bfloat16)
    windows[pl.ds(0, width), :] = zero_rows
    windows[pl.ds(width + cells, width), :] = zero_rows
    body = pl.ds(width, cells)
    windows[body, 0:lanes] = jnp.where(column != width - 1, tall[pl.ds(9, cells), :], 0.0).astype(jnp.bfloat16)
    windows[body, lanes : 2 * lanes] = tall[pl.ds(8, cells), :].astype(jnp.bfloat16)
    windows[body, 2 * lanes : 3 * lanes] = jnp.where(column != 0, tall[pl.ds(7, cells), :], 0.0).astype(jnp.bfloat16)


def lay_single(width, layer, windows, tall):
    filt, cells = layer.shape
    lanes = 2 * filt
    tall[pl.ds(8, cells), :] = jnp.concatenate([layer, layer], axis=0).astype(jnp.float32).T
    row = lax.broadcasted_iota(jnp.int32, (cells, lanes), 0)
    column = row & (width - 1) if width & (width - 1) == 0 else lax.rem(row, width)
    left = lax.broadcasted_iota(jnp.int32, (cells, lanes), 1) < filt
    zero_rows = jnp.zeros((width, windows.shape[1]), jnp.bfloat16)
    windows[pl.ds(0, width), :] = zero_rows
    windows[pl.ds(width + cells, width), :] = zero_rows
    body = pl.ds(width, cells)
    low = jnp.where(column != width - 1, tall[pl.ds(9, cells), :], 0.0)
    high = jnp.where(column != 0, tall[pl.ds(7, cells), :], 0.0)
    windows[body, 0:lanes] = jnp.where(left, low, high).astype(jnp.bfloat16)
    windows[body, lanes : lanes + filt] = tall[pl.ds(8, cells), 0:filt].astype(jnp.bfloat16)


def pick_kernel(blocks, picked):
    size, chans = picked.shape
    rows = chans // blocks
    half = chans // 2
    count = bits_of(blocks)
    order = lax.broadcasted_iota(jnp.int32, (size, chans), 0)
    order = order + jnp.where(order >= half, (lax.axis_index("filt") & 1) * (size - half), 0)
    block = lax.axis_index("space") ^ reversed_bits(order >> bits_of(rows), count)
    source = (block << bits_of(rows)) | (order & (rows - 1))
    picked[...] = (lax.broadcasted_iota(jnp.int32, (size, chans), 1) == source).astype(jnp.bfloat16)


def turn_kernel(picked, inputs, _, mine, part):
    half = mine.shape[0]
    turned = lax.dot_general(picked[...], inputs[...], (((1,), (1,)), ((), ())), preferred_element_type=jnp.float32)
    turned = turned.astype(jnp.bfloat16)
    mine[...] = turned[0:half, :]
    part[...] = turned[half:, :]


def grads_kernel(_, out_grad, pre_act, own):
    own[...] = (out_grad[...].astype(jnp.float32) * silu_grad(pre_act[...].astype(jnp.float32))).astype(own.dtype)


def again_kernel(own, out):
    out[...] = own[...]


def order_kernel(weight, paired, single):
    filt = weight.shape[1]
    odd = lax.axis_index("space") & 1
    for tap in range(9):
        b, c = divmod(tap, 3)
        low, high = pl.ds(2 * c * filt, filt), pl.ds((2 * c + 1) * filt, filt)
        paired[b, low, :] = weight[9 + tap]
        paired[b, high, :] = weight[18 * odd + tap]
        single[b, pl.ds((0, 2, 1)[c] * filt, filt), :] = weight[18 - 18 * odd + tap]


def near_kernel(width, own, near, mine, weight, windows, terms, spread, tall):
    cells = own.shape[1]
    wide = windows.shape[1]
    lay_windows(width, own[...], near[...], windows, tall)
    total = 0.0
    for b in range(3):
        window = windows[pl.ds((2 - b) * width, cells), :]
        terms[:, b * wide : (b + 1) * wide] = jnp.dot(mine[...], window, preferred_element_type=jnp.float32)
        total = total + jnp.dot(window, weight[b], preferred_element_type=jnp.float32)
    spread[...] = total


def store_tile(value, tile, keep, sends):
    lanes = keep.shape[1]
    part = value.shape[0] // (len(sends) + 1)
    rows = pl.ds(tile * part, part if value.shape[1] == lanes else part // 2)
    for number, target in enumerate((keep, *sends)):
        piece = value[number * part : (number + 1) * part, :]
        if value.shape[1] < lanes:
            piece = jnp.concatenate([piece[0 : part // 2, :], piece[part // 2 :, :]], axis=1)
        target[rows, :] = piece.astype(target.dtype)


def theirs_kernel(width, came, other, two_off, windows, terms, outer, keep, *rest):
    *sends, theirs, twos, tall = rest
    part, cells = came.shape
    wide = windows.shape[1]
    lanes = wide // 3
    filt = lanes // 2
    first_core = lax.axis_index("filt") & 1 == 0
    theirs[0:part, :] = jnp.where(first_core, came[...], other[...])
    theirs[part:, :] = jnp.where(first_core, other[...], came[...])
    lay_single(width, two_off[...], twos, tall)
    left = lax.broadcasted_iota(jnp.int32, (2 * part, lanes), 1) < filt
    middle = []
    for b in range(3):
        rows = pl.ds((2 - b) * width, cells)
        near_terms = jnp.dot(theirs[...], windows[rows, :], preferred_element_type=jnp.float32)
        two_terms = jnp.dot(theirs[...], twos[rows, :], preferred_element_type=jnp.float32)
        outside, centre = two_terms[:, 0:lanes], two_terms[:, lanes : lanes + filt]
        far_side = (pltpu.roll(outside, filt, 1), jnp.concatenate([centre, centre], axis=1), outside)
        cuts = [slice(c * lanes, (c + 1) * lanes) for c in range(3)]
        for c, cut in enumerate(cuts):
            lo = b * wide + c * lanes
            crossed = jnp.where(left, pltpu.roll(near_terms[:, cut], filt, 1), far_side[c])
            store_tile(terms[:, lo : lo + lanes] + crossed, 3 * b + c, keep, sends)
        outer[:, b * lanes : (b + 1) * lanes] = jnp.where(
            left, near_terms[:, cuts[0]], pltpu.roll(near_terms[:, cuts[2]], filt, 1)
        )
        middle.append(near_terms[:, cuts[1]])
    outer[:, wide : wide + lanes] = jnp.where(left, middle[0], pltpu.roll(middle[1], filt, 1))
    outer[:, wide + lanes : wide + lanes + filt] = middle[2][:, 0:filt]


def rows_total(width, groups, target, windows, weight, spread):
    size = spread.shape[0] // groups
    index = lax.axis_index("filt")
    count = bits_of(groups)
    block = 0
    for bit in range(count):
        differs = (target >> (count - 1 - bit)) & 1
        block = block + (((index >> bit) & 1) ^ differs) * (1 << bit)
    start = pl.multiple_of(block * size, size)
    total = spread[pl.ds(start, size), :]
    for b in range(3):
        rows = pl.ds(pl.multiple_of(start + (2 - b) * width, width), size)
        total = total + jnp.dot(windows[rows, :], weight[b], preferred_element_type=jnp.float32)
    return total


def first_half_kernel(width, groups, windows, weight, spread, came, keep, send):
    size = spread.shape[0] // groups
    for target in range(groups // 2):
        total = rows_total(width, groups, target, windows, weight, spread)
        total = total + came[target * size : (target + 1) * size, :].astype(jnp.float32)
        if target < groups // 4:
            keep[target * size : (target + 1) * size, :] = total
        else:
            lo = (target - groups // 4) * size
            send[lo : lo + size, :] = total.astype(jnp.bfloat16)


def one_kernel(width, groups, radix, one_off, mine, weight, spread, outer, *rest):
    windows, sent_in, keep, *rest = rest[radix:]
    *sends, tall = rest
    cells = mine.shape[1]
    lanes = keep.shape[1]
    filt = lanes // 2
    lay_single(width, one_off[...], windows, tall)

    middle = []
    for b in range(3):
        window = windows[pl.ds((2 - b) * width, cells), :]
        terms = jnp.dot(mine[...], window, preferred_element_type=jnp.float32)
        store_tile(terms[:, 0:lanes] + outer[:, b * lanes : (b + 1) * lanes], 9 + b, keep, sends)
        middle.append(terms[:, lanes : lanes + filt])
    both = jnp.concatenate(middle[0:2], axis=1)
    store_tile(both + outer[:, 3 * lanes : 4 * lanes], 12, keep, sends)
    store_tile(middle[2] + outer[:, 4 * lanes : 4 * lanes + filt], 13, keep, sends)

    size = cells // groups
    for target in range(groups // 2, groups):
        lo = (target - groups // 2) * size
        total = rows_total(width, groups, target, windows, weight, spread)
        sent_in[lo : lo + size, :] = total.astype(jnp.bfloat16)


def unfolded(tiles, rows):
    full = tiles.shape[0] // rows
    whole = [tiles[n * rows : (n + 1) * rows] for n in range(full)]
    half = tiles[full * rows :]
    lanes = tiles.shape[1]
    return jnp.concatenate([*whole, jnp.concatenate([half[:, : lanes // 2], half[:, lanes // 2 :]], axis=0)], axis=1)


def halve_kernel(kept, came, keep, send):
    half = keep.shape[0]
    keep[...] = kept[0:half, :] + came[0:half, :].astype(jnp.float32)
    send[...] = (kept[half:, :] + came[half:, :].astype(jnp.float32)).astype(jnp.bfloat16)


def sum_kernel(scale, folded, kept, *rest):
    *came, out = rest
    total = kept[...]
    for piece in came:
        total = total + piece[...].astype(jnp.float32)
    total = total * scale
    if not folded:
        out[...] = total
        return
    rows, lanes = out.shape[0], total.shape[1]
    full = total.shape[0] // rows
    for tile in range(full):
        out[:, tile * lanes : (tile + 1) * lanes] = total[tile * rows : (tile + 1) * rows, :]
    out[0 : rows // 2, full * lanes :] = total[full * rows :, 0 : lanes // 2]
    out[rows // 2 :, full * lanes :] = total[full * rows :, lanes // 2 :]


def last_kernel(filt, summed, kept, came, out, grad_input, taps, rows, done):
    odd = lax.axis_index("space") & 1
    rows[...] = (kept[...] + came[...].astype(jnp.float32)).astype(rows.dtype)
    copies = [pltpu.make_async_copy(rows, grad_input, done.at[3])]
    copies[0].start()
    total = summed[...]
    outer = [18 + 2 * (tap // 3) + tap % 3 // 2 if tap % 3 != 1 else 24 + tap // 3 for tap in range(9)]
    for group, (slots, target) in enumerate(((range(0, 18, 2), 1), (range(1, 18, 2), 2 * odd), (outer, 2 - 2 * odd))):
        for tap, slot in enumerate(slots):
            taps[group, tap] = total[:, slot * filt : (slot + 1) * filt]
        copy = pltpu.make_async_copy(taps.at[group], out.at[pl.ds(target * 9, 9)], done.at[group])
        copy.start()
        copies.append(copy)
    for copy in copies:
        copy.wait()


def swapped(value, axis, distance):
    count = lax.axis_size(axis)
    return lax.ppermute(value, axis, [(i, i ^ distance) for i in range(count)])


def halved(kept, came):
    rows, lanes = kept.shape
    if rows // 2 % 16:
        total = kept + came.astype(jnp.float32)
        return total[: rows // 2], total[rows // 2 :].astype(jnp.bfloat16)
    outs = (
        jax.ShapeDtypeStruct((rows // 2, lanes), jnp.float32),
        jax.ShapeDtypeStruct((rows // 2, lanes), jnp.bfloat16),
    )
    return call(halve_kernel, outs, flops=rows * lanes, bytes_accessed=9 * rows * lanes)(
        in_specs=[VMEM] * 2, out_specs=[VMEM] * 2
    )(kept, came)


def after(value, other):
    return lax.optimization_barrier((value, other))[0]


def on_device(inputs, out_grad, pre_act, weight):
    _, height, width, chans = inputs.shape
    taps, filt, _ = weight.shape
    cells = height * width
    blocks, groups = lax.axis_size("space"), lax.axis_size("filt")
    half, quarter = chans // 2, chans // 4
    bf16, f32 = jnp.bfloat16, jnp.float32
    shape = jax.ShapeDtypeStruct
    flops = 2 * cells * taps * filt * chans
    lanes = 6 * filt
    windows_shape = shape((cells + 2 * width, lanes), bf16)
    tall = pltpu.VMEM((cells + 16, 2 * filt), f32)

    picked = call(
        functools.partial(pick_kernel, blocks), shape((half + quarter, chans), bf16), flops=PICK * flops
    )(in_specs=[], out_specs=VMEM)()
    own = call(grads_kernel, shape((filt, cells), bf16))(in_specs=[VMEM] * 3, out_specs=VMEM)(
        picked, out_grad[0], pre_act[0]
    )
    own_again = call(again_kernel, shape((filt, cells), bf16), flops=AGAIN * flops)(in_specs=[VMEM], out_specs=VMEM)(own)
    mine, part = call(
        turn_kernel,
        (shape((half, cells), bf16), shape((quarter, cells), bf16)),
        flops=TURN * flops,
    )(in_specs=[VMEM] * 3, out_specs=[VMEM] * 2)(picked, inputs.reshape(cells, chans), own_again)
    near = swapped(own, "space", 1)
    came = swapped(part, "space", 1)
    up = [(i, i + 2) for i in range(blocks - 2)]
    down = [(target, source) for source, target in up]
    even, odd = slice(0, None, 2), slice(1, None, 2)
    two_off = lax.ppermute(own_again, "space", down[even] + up[odd])
    one_off = lax.ppermute(near, "space", up[even] + down[odd])
    other = swapped(came, "filt", 1)

    weight_shape = shape((3, lanes, chans), bf16)
    paired_weight, single_weight = call(
        order_kernel, (weight_shape, shape((3, 3 * filt, chans), bf16)), flops=ORDER * flops, bytes_accessed=MIB
    )(in_specs=[VMEM], out_specs=[VMEM] * 2)(after(weight, mine))
    windows, terms, spread = call(
        functools.partial(near_kernel, width),
        (windows_shape, shape((half, 3 * lanes), f32), shape((cells, chans), f32)),
        (tall,),
        flops=NEAR * flops,
        bytes_accessed=4 * MIB,
    )(in_specs=[VMEM] * 4, out_specs=[VMEM] * 3)(own, near, mine, paired_weight)
    radix = min(4, blocks // 2)
    piece = half // radix
    folded = (piece * taps // 2, 2 * filt)
    pieces = (shape(folded, f32),) + (shape(folded, bf16),) * (radix - 1)
    outer, *partial = call(
        functools.partial(theirs_kernel, width),
        (shape((half, 9 * filt), f32),) + pieces,
        (pltpu.VMEM((half, cells), bf16), pltpu.VMEM((cells + 2 * width, 3 * filt), bf16), tall),
        flops=THEIRS * flops,
        bytes_accessed=4 * MIB,
    )(in_specs=[VMEM] * 5, out_specs=[VMEM] * (radix + 1))(came, other, two_off, windows, terms)
    ones, sent_in, kept, *sends = call(
        functools.partial(one_kernel, width, groups, radix),
        (shape((cells + 2 * width, 3 * filt), bf16), shape((cells // 2, chans), bf16)) + pieces,
        (tall,),
        flops=ONE * flops,
        bytes_accessed=4 * MIB,
        aliases={5 + n: 2 + n for n in range(radix)},
    )(in_specs=[VMEM] * (5 + radix), out_specs=[VMEM] * (radix + 2))(
        one_off, mine, single_weight, spread, outer, *partial
    )
    came_in = swapped(sent_in, "filt", 1)

    distance = 2
    while True:
        spans = {2: (1,), 4: (2, 1, 3)}[radix]
        arrived = [swapped(sends[n - 1], "space", spans[n - 1] * distance) for n in range(1, radix)]
        distance *= radix
        if distance >= blocks:
            break
        total = kept
        for value in arrived:
            total = total + value.astype(f32)
        if total.shape == folded:
            total = unfolded(total, piece)
        radix = min(4, blocks // distance)
        piece //= radix
        kept, *sends = (total[n * piece : (n + 1) * piece] for n in range(radix))
        sends = [value.astype(bf16) for value in sends]

    block = (cells // 4, chans)
    kept_in, sent_in = call(
        functools.partial(first_half_kernel, width, groups),
        (shape(block, f32), shape(block, bf16)),
        flops=flops // 6,
        bytes_accessed=MIB,
    )(in_specs=[VMEM] * 4, out_specs=[VMEM] * 2)(ones, single_weight, spread, came_in)
    came_in = swapped(sent_in, "filt", 2)
    distance_in = 4
    while distance_in < groups:
        kept_in, sent_in = halved(kept_in, came_in)
        came_in = swapped(sent_in, "filt", distance_in)
        distance_in *= 2
    grad_scale = float(cells * blocks) ** (-0.5)
    summed = call(
        functools.partial(sum_kernel, grad_scale, kept.shape == folded), shape((chans // blocks, taps * filt), f32), flops=FINAL * flops
    )(in_specs=[VMEM] * (len(arrived) + 1), out_specs=VMEM)(kept, *arrived)
    any_space = pl.BlockSpec(memory_space=pl.ANY)
    rows_shape = (cells // groups, chans)
    grad_weight, grad_input = call(
        functools.partial(last_kernel, filt),
        (shape((taps, chans // blocks, filt), f32), shape(rows_shape, bf16)),
        (
            pltpu.VMEM((3, 9, chans // blocks, filt), f32),
            pltpu.VMEM(rows_shape, bf16),
            pltpu.SemaphoreType.DMA((4,)),
        ),
    )(in_specs=[VMEM] * 3, out_specs=[any_space] * 2)(summed, kept_in, came_in)
    return grad_input.reshape(1, height // groups, width, chans), jnp.transpose(grad_weight, (1, 0, 2))


def solution(mesh):
    placed = (
        P("space", None, None, None),
        P("space", "filt", None),
        P("space", "filt", None),
        P(None, "filt", None),
    )
    return jax.shard_map(
        on_device,
        mesh=mesh,
        in_specs=placed,
        out_specs=(P("space", "filt", None, None), P("space", None, "filt")),
        check_vma=False,
    )
```
